256 devices in a mesh: cls: 8 (over x, core), ptcl: 32 (over y, z).
Axes of the slice: x: 4, y: 4, z: 8, core: 2. Of those that a mesh axis runs over, the one named last changes fastest.
Arguments:
- images: bfloat16 [49152, 4096], P('ptcl'), may hold values from -8000 to 8000
- target: int32 [49152], P('ptcl'), may hold values from -1 to 24575, as said below
- ctf_group: int32 [49152], P('ptcl'), may hold values from 0 to 15
- ctf_table: float32 [16, 4096], replicated, may hold values from -1 to 1
- noise_weight: float32 [4096], replicated, may hold values from 0.01 to 0.1
- references: bfloat16 [3744, 4096], P('cls', 'ptcl'), may hold values from -6 to 6
Outputs:
- class_sums: float32 [4096, 3744], P('ptcl', 'cls')
- class_weights: float32 [16, 3744], P(None, 'cls')
- log_evidence: float32 [24576], P('ptcl')
The draws below stay inside these ranges and needn't reach their ends.
Inputs may be any that keep to these rules, and one draw needn't show every extreme that they name: `target`: every position of 0 to 24575 names exactly one slot; the others hold -1. Of one device's 1536 slots at most 48 name positions of one destination shard (positions d * 768 to (d + 1) * 768 - 1); in every draw some device sends 48 to every shard and has all 1536 slots live.
All inputs are finite; a program needn't handle non-finite values.
Results may differ from the reference program's by a relative error of at most 0.0058.
Values may be sent and summed in bfloat16 or wider, within the bound.
No kernel may reach another device: no remote copies, remote signals or barrier semaphores. Data moves between devices by JAX's collectives and lax.ppermute only.
A program may use at most 128 MiB of HBM per device.

```python
import math
import jax
import jax.numpy as jnp
from jax import lax

COEFS = 4096
GROUPS = 16
PTCL_DEV = 768
HOLD = 1536
PANELS = 3744
N_PTCL = 32


def panel_values(key):
    key = jax.random.fold_in(key, 101)
    return jnp.clip(jax.random.normal(key, (PANELS, COEFS), jnp.float32), -6.0, 6.0)


def ctf_values(key):
    key = jax.random.fold_in(key, 102)
    return jax.random.uniform(key, (GROUPS, COEFS), jnp.float32, -1.0, 1.0)


def group_values(key):
    key = jax.random.fold_in(key, 103)
    return jax.random.randint(key, (N_PTCL * HOLD,), 0, GROUPS).astype(jnp.int32)


def draw_target(key, part):
    key = jax.random.fold_in(key, 104)
    subkeys = jax.random.split(key, 4)
    shard_count = N_PTCL
    share_size = PTCL_DEV // N_PTCL
    leaning = jax.random.randint(subkeys[0], (shard_count,), 0, 4) * 16
    favoured = jax.random.randint(subkeys[1], (), 0, shard_count)
    leaning = jnp.where(jnp.arange(shard_count) == favoured, 100000, leaning)
    jitter = jax.random.randint(subkeys[2], (shard_count, shard_count), 0, 16)
    ranking_score = (jitter + leaning[None, :]) * shard_count + jnp.arange(shard_count)[None, :]
    ranking = jnp.argsort(-ranking_score, axis=1)
    position = jnp.argsort(ranking, axis=1)
    amount = jnp.where(position < shard_count // 4, 2 * share_size, jnp.where(position < 3 * shard_count // 4, share_size, 0)).T
    run_ends = jnp.cumsum(amount, axis=1)
    run_starts = run_ends - amount
    earlier = jnp.cumsum(amount, axis=0) - amount
    live_total = run_ends[:, -1]
    slot_index = jnp.arange(HOLD, dtype=jnp.int32)
    dest_shard = jnp.sum((slot_index[None, :, None] >= run_ends[:, None, :]).astype(jnp.int32), axis=2)
    dest_shard = jnp.minimum(dest_shard, shard_count - 1)
    offset = slot_index[None, :] - jnp.take_along_axis(run_starts, dest_shard, axis=1) + jnp.take_along_axis(earlier, dest_shard, axis=1)
    placed = jnp.where(slot_index[None, :] < live_total[:, None], dest_shard * PTCL_DEV + offset, -1)
    shuffle = jax.random.randint(subkeys[3], (shard_count, HOLD), 0, 1 << 20) * HOLD + slot_index[None, :]
    reorder = jnp.argsort(shuffle, axis=1)
    return jnp.take_along_axis(placed, reorder, axis=1).reshape(-1).astype(jnp.int32)


def draw_ctf_group(key, part):
    return group_values(key)


def draw_ctf_table(key, part):
    return ctf_values(key)


def draw_references(key, part):
    return panel_values(key).astype(jnp.bfloat16)


def drawn_rows(keys, groups, ctf_rows, panel_rows, levels):
    slot_count = groups.shape[0]
    first_panel = jax.random.randint(keys[0], (slot_count,), 0, PANELS)
    second_panel = (first_panel + 1 + jax.random.randint(keys[1], (slot_count,), 0, PANELS - 1)) % PANELS
    level = levels[jax.random.randint(keys[2], (slot_count,), 0, 3)]
    strength = 0.5 + level * (25000.0 / COEFS)
    mixed = panel_rows[first_panel] + panel_rows[second_panel]
    return strength[:, None] * ctf_rows[groups] * mixed


def draw_images(key, part):
    groups = group_values(key)
    ctf_rows = ctf_values(key)
    panel_rows = panel_values(key)
    key = jax.random.fold_in(key, 105)
    subkeys = jax.random.split(key, 6)
    slot_count = N_PTCL * HOLD
    chosen = jax.random.randint(subkeys[2], (slot_count,), 0, 8) == 0
    baseline = jnp.clip(jax.random.normal(subkeys[0], (slot_count, COEFS), jnp.float32), -6.0, 6.0)
    aligned = drawn_rows(subkeys[3:6], groups, ctf_rows, panel_rows, jnp.array([0.5, 1.0, 2.0], jnp.float32))
    drawn = jnp.where(chosen[:, None], aligned, baseline)
    return drawn.astype(jnp.bfloat16)


def setup_inputs(seed: int = 0) -> dict:
    key_of = jax.random.split(jax.random.key(seed), 7)
    return {
        "images": draw_images(jax.random.fold_in(key_of[6], 71), 0),
        "target": draw_target(jax.random.fold_in(key_of[6], 71), 0),
        "ctf_group": draw_ctf_group(jax.random.fold_in(key_of[6], 71), 0),
        "ctf_table": draw_ctf_table(jax.random.fold_in(key_of[6], 71), 0),
        "noise_weight": jnp.clip(jnp.exp(jax.random.uniform(key_of[4], (COEFS,), jnp.float32, math.log(0.01), math.log(0.1))), 0.01, 0.1),
        "references": draw_references(jax.random.fold_in(key_of[6], 71), 0),
    }


def reference(images, target, ctf_group, ctf_table, noise_weight, references):
    total_count = PTCL_DEV * N_PTCL
    landing = jnp.where(target >= 0, target, total_count).astype(jnp.int32)
    relaid = jnp.zeros((total_count, COEFS), jnp.bfloat16).at[landing].set(images, mode="drop")
    groups = jnp.zeros((total_count,), jnp.int32).at[landing].set(ctf_group, mode="drop")
    sq_weight = ctf_table * ctf_table * noise_weight[None, :]
    widened = references.astype(jnp.float32)
    energy = jnp.dot(sq_weight, (widened * widened).T, precision=lax.Precision.HIGHEST)
    block_count = total_count // PTCL_DEV

    def advance(running, block_index):
        sums_now, weights_now = running
        begin_row = (block_index * PTCL_DEV).astype(jnp.int32)
        particles = lax.dynamic_slice_in_dim(relaid, begin_row, PTCL_DEV, 0)
        block_groups = lax.dynamic_slice_in_dim(groups, begin_row, PTCL_DEV, 0)
        weighted = (particles.astype(jnp.float32) * ctf_table[block_groups] * noise_weight[None, :]).astype(jnp.bfloat16)
        scores = jnp.dot(weighted, references.T, preferred_element_type=jnp.float32) - 0.5 * energy[block_groups]
        highest = jnp.max(scores, axis=1, keepdims=True)
        log_total = highest[:, 0] + jnp.log(jnp.sum(jnp.exp(scores - highest), axis=1))
        posterior = jnp.exp(scores - log_total[:, None]).astype(jnp.bfloat16)
        sums_now = sums_now + jnp.dot(weighted.T, posterior, preferred_element_type=jnp.float32)
        onehot = (block_groups[:, None] == jnp.arange(GROUPS, dtype=jnp.int32)[None, :]).astype(jnp.float32)
        weights_now = weights_now + jnp.dot(onehot.T, posterior.astype(jnp.float32), precision=lax.Precision.HIGHEST)
        return (sums_now, weights_now), log_total

    initial = (jnp.zeros((COEFS, PANELS), jnp.float32), jnp.zeros((GROUPS, PANELS), jnp.float32))
    (class_sums, class_weights), evidence = lax.scan(advance, initial, jnp.arange(block_count, dtype=jnp.int32))
    return class_sums, class_weights, evidence.reshape(total_count)
```

```python
import functools

import jax
import jax.numpy as jnp
from jax import lax
from jax.experimental import pallas as pl
from jax.experimental.pallas import tpu as pltpu
from jax.sharding import PartitionSpec as P

NY, NZ = 4, 8
LANES = 128
TILE = 16
F32, BF16, I16, I32 = jnp.float32, jnp.bfloat16, jnp.int16, jnp.int32
NT = (((1,), (1,)), ((), ()))
TN = (((0,), (0,)), ((), ()))
VMEM_LIMIT = 40 * 1024 * 1024
LOW_EXPONENT = -100.0


def dot(a, b, dims=(((1,), (0,)), ((), ()))):
    return lax.dot_general(a, b, dims, preferred_element_type=F32)


def split3(x):
    hi = x.astype(BF16)
    rest = x - hi.astype(F32)
    mid = rest.astype(BF16)
    low = (rest - mid.astype(F32)).astype(BF16)
    return jnp.concatenate([hi.astype(F32), mid.astype(F32), low.astype(F32)], axis=0).astype(BF16)


def onehot3(groups, count):
    row = lax.broadcasted_iota(I32, (3 * count, groups.shape[1]), 0)
    row = jnp.where(row >= 2 * count, row - 2 * count, jnp.where(row >= count, row - count, row))
    return (row == groups).astype(F32).astype(BF16)


def params(**kw):
    return pltpu.CompilerParams(vmem_limit_bytes=VMEM_LIMIT, **kw)


def cost(flops, byte_count):
    return pl.CostEstimate(flops=int(flops), bytes_accessed=int(byte_count), transcendentals=0)


def weight_kernel(order, groups, *refs):
    images, tables, noises = refs[:NY], refs[NY : 2 * NY], refs[2 * NY : 3 * NY]
    weighted, square = refs[3 * NY :]
    count = tables[0].shape[0]
    slots = images[0].shape[0]
    table = jnp.concatenate([t[...] for t in tables], axis=1)
    noise = jnp.concatenate([n[...] for n in noises], axis=1)
    square[0] = split3(table * table * noise)
    pieces = split3(table)
    member = onehot3(groups[...], count)
    step = 256
    for begin in range(0, slots, step):
        rows = dot(member[:, begin : begin + step], pieces, TN)
        picture = jnp.concatenate([i[begin : begin + step, :] for i in images], axis=1)
        weighted[0, begin : begin + step, :] = (picture.astype(F32) * rows * noise).astype(BF16)


def weigh(order, groups, images, table, noise):
    slots, count = images.shape[0], table.shape[0]
    wide = NY * LANES

    def block(j):
        return lambda i, o: (0, o[i * NY + j])

    specs = [pl.BlockSpec((1, slots), lambda i, o: (0, 0))]
    for rows in (slots, count, 1):
        specs += [pl.BlockSpec((rows, LANES), block(j)) for j in range(NY)]
    return pl.pallas_call(
        weight_kernel,
        grid_spec=pltpu.PrefetchScalarGridSpec(
            num_scalar_prefetch=1,
            grid=(NZ,),
            in_specs=specs,
            out_specs=[
                pl.BlockSpec((1, slots, wide), lambda i, o: (i, 0, 0)),
                pl.BlockSpec((1, 3 * count, wide), lambda i, o: (i, 0, 0)),
            ],
        ),
        out_shape=[
            jax.ShapeDtypeStruct((NZ, slots, wide), BF16),
            jax.ShapeDtypeStruct((NZ, 3 * count, wide), BF16),
        ],
        compiler_params=params(),
        cost_estimate=cost(6e9, 4 * images.size),
        name="weigh",
    )(order, groups, *[images] * NY, *[table] * NY, *[noise] * NY)


def score_kernel(parts, first, last, panels, offsets, *refs):
    refs = list(refs)
    chunks = [[refs.pop(0) for _ in part] for part in parts]
    weighted, square, groups = refs[:3]
    refs = refs[3:]
    if not first:
        total_in, energy_in = refs[:2]
        refs = refs[2:]
    if last:
        mass, peak, evidence, total, energy = refs
    else:
        total, energy = refs
    step = pl.program_id(0)

    @pl.when(step == 0)
    def _():
        if first:
            total[...] = jnp.zeros_like(total)
            energy[...] = jnp.zeros_like(energy)
        else:
            total[...] = total_in[...]
            energy[...] = energy_in[...]

    for number, chunk in enumerate(chunks):

        @pl.when(step == number)
        def _(chunk=chunk):
            blocks = [c[j] for c in chunk for j in range(c.shape[0])]
            panel = jnp.concatenate(blocks, axis=1)
            total[...] += dot(panel, weighted[0], NT)
            wide = panel.astype(F32)
            wide = wide * wide
            hi = wide.astype(BF16)
            low = (wide - hi.astype(F32)).astype(BF16)
            energy[...] += dot(hi, square[0], NT) + dot(low, square[0], NT)

    if last:

        @pl.when(step == len(chunks) - 1)
        def _():
            count = energy.shape[1] // 3
            member = onehot3(groups[...], count)
            each = energy[...]
            hi = each.astype(BF16)
            rest = each - hi.astype(F32)
            mid = rest.astype(BF16)
            low = (rest - mid.astype(F32)).astype(BF16)
            offset = dot(hi, member) + dot(mid, member) + dot(low, member)
            scores = total[...] - 0.5 * offset
            row = lax.broadcasted_iota(I32, scores.shape, 0)
            scores = jnp.where(row < panels, scores, -jnp.inf)
            top = jnp.max(scores, axis=0, keepdims=True)
            shifted = jnp.exp(scores - top)
            mass[...] = shifted
            peak[...] = top
            evidence[...] = top + jnp.log(jnp.sum(shifted, axis=0, keepdims=True))


def score(offsets, parts, weighted, square, groups, carry, last, panels):
    rows = parts[0][0].shape[1]
    slots = groups.shape[1]
    wide = NY * LANES
    count3 = square.shape[1]
    offsets = jnp.array(offsets, I32)

    def whole(shape):
        return pl.BlockSpec(shape, lambda i, o: (0,) * len(shape))

    specs = [whole(a.shape) for part in parts for a in part]
    specs += [
        pl.BlockSpec((1, slots, wide), lambda i, o: (o[i], 0, 0)),
        pl.BlockSpec((1, count3, wide), lambda i, o: (o[i], 0, 0)),
        whole((1, slots)),
    ]
    state = [jax.ShapeDtypeStruct((rows, slots), F32), jax.ShapeDtypeStruct((rows, count3), F32)]
    if carry is not None:
        specs += [whole(s.shape) for s in state]
    if last:
        outs = [state[0]] + [jax.ShapeDtypeStruct((1, slots), F32)] * 2
        scratch = [pltpu.VMEM(s.shape, s.dtype) for s in state]
    else:
        outs, scratch = state, []
    return pl.pallas_call(
        functools.partial(
            score_kernel, [[None] * len(p) for p in parts], carry is None, last, panels
        ),
        grid_spec=pltpu.PrefetchScalarGridSpec(
            num_scalar_prefetch=1,
            grid=(len(parts),),
            in_specs=specs,
            out_specs=[whole(o.shape) for o in outs],
            scratch_shapes=scratch,
        ),
        out_shape=outs,
        compiler_params=params(),
        cost_estimate=cost(2.5 * rows * slots * wide * len(parts), 4e6 * len(parts)),
        name="score",
    )(
        offsets,
        *[a for part in parts for a in part],
        weighted,
        square,
        groups,
        *([] if carry is None else carry),
    )


def posterior_kernel(mass, peak, evidence, place, groups, post, weights, relay):
    live = place[...] >= 0
    scale = jnp.where(live, jnp.exp(peak[...] - evidence[...]), 0.0)
    value = (mass[...] * scale).astype(BF16)
    post[...] = value
    count = weights.shape[0]
    slots = groups.shape[1]
    member = (lax.broadcasted_iota(I32, (count, slots), 0) == groups[...]).astype(F32).astype(BF16)
    weights[...] = dot(member, value, NT)
    spot = place[...]
    high = (lax.broadcasted_iota(I32, (relay.shape[0], slots), 0) == lax.shift_right_arithmetic(spot, 7)).astype(F32)
    lane = lax.broadcasted_iota(I32, (LANES, slots), 0) == (spot & 127)
    found = split3(jnp.where(live, evidence[...], 0.0))
    out = jnp.zeros(relay.shape, F32)
    for k in (2, 1, 0):
        out += dot(high.astype(BF16), jnp.where(lane, found[k : k + 1].astype(F32), 0.0).astype(BF16), NT)
    relay[...] = out


def posterior(mass, peak, evidence, place, groups, count):
    rows, slots = mass.shape
    return pl.pallas_call(
        posterior_kernel,
        out_shape=[
            jax.ShapeDtypeStruct((rows, slots), BF16),
            jax.ShapeDtypeStruct((count, rows), F32),
            jax.ShapeDtypeStruct((NZ * NY * 8, LANES), F32),
        ],
        compiler_params=params(),
        cost_estimate=cost(1e9, 5e6),
        name="posterior",
    )(mass, peak, evidence, place, groups)


def exponent(x):
    top = jnp.max(jnp.abs(x), axis=0, keepdims=True)
    return jnp.maximum(jnp.ceil(jnp.log2(jnp.maximum(top, 2.0**LOW_EXPONENT))), LOW_EXPONENT)


def to_int(x):
    return jnp.round(x).astype(I32)


def encode(sums, relay):
    e = exponent(sums)
    main = to_int(sums * jnp.exp2(14.0 - e)).astype(I16)
    f = exponent(relay)
    up, down = jnp.exp2(14.0 - f), jnp.exp2(f - 14.0)
    high = jnp.round(relay * up)
    low = to_int((relay - high * down) * up * 2.0**14)
    row = lax.broadcasted_iota(I32, relay.shape, 0)
    high = jnp.where(row == 0, e, jnp.where(row == 1, f, high)).astype(I32)
    low = jnp.where(row < 2, 0, low)
    return main, jnp.concatenate([high, low], axis=0).astype(I16)


def decode(block):
    rows = block.shape[0] - TILE
    tail = block[rows:, :].astype(I32).astype(F32)
    high, low = tail[:8], tail[8:]
    sums = block[:rows, :].astype(I32).astype(F32) * jnp.exp2(high[0:1] - 14.0)
    down = jnp.exp2(high[1:2] - 14.0)
    row = lax.broadcasted_iota(I32, high.shape, 0)
    return sums, jnp.where(row < 2, 0.0, (high + low * 2.0**-14) * down)


def put(out, j, sums, relay):
    rows = out.shape[1] - TILE
    main, tail = encode(sums, relay)
    out[j, :rows, :] = main
    out[j, rows:, :] = tail


def sums_kernel(ways, halves, post, *refs):
    refs = list(refs)
    inputs = [(refs.pop(0), refs.pop(0)) for _ in range(ways)]
    came = [refs.pop(0) for _ in range(2)] if halves is not None else []
    outs = refs
    for way, (weighted, relay) in enumerate(inputs):
        product = dot(post[...], weighted[0])
        for j in range(product.shape[1] // LANES):
            sums = product[:, j * LANES : (j + 1) * LANES]
            extra = relay[0, j]
            if halves == "half":
                s, r = decode(came[way][j])
                mine = pl.program_id(0) == way
                sums = sums + jnp.where(mine, s, 0.0)
                extra = extra + jnp.where(mine, r, 0.0)
            elif halves == "full":
                for c in came if ways == 1 else [came[way]]:
                    s, r = decode(c[j])
                    sums, extra = sums + s, extra + r
            put(outs[way], j, sums, extra)


def sums_step(offsets, halves, post, weighted, relay, came):
    rows, slots = post.shape
    pair = 2
    whole = pl.BlockSpec((rows, slots), lambda i: (0, 0))
    specs, args = [whole], [post]
    for o in offsets:
        specs += [
            pl.BlockSpec((1, slots, pair * LANES), lambda i, o=o: (o, 0, i)),
            pl.BlockSpec((1, pair, 8, LANES), lambda i, o=o: (o, i, 0, 0)),
        ]
        args += [weighted, relay]
    tall = rows + TILE
    if halves == "half":
        specs += [pl.BlockSpec((pair, tall, LANES), lambda i: (0, 0, 0))] * 2
        args += came
    elif halves == "full":
        specs += [pl.BlockSpec((pair, tall, LANES), lambda i: (i, 0, 0))] * 2
        args += came
    out = jax.ShapeDtypeStruct((NY, tall, LANES), I16)
    return pl.pallas_call(
        functools.partial(sums_kernel, len(offsets), halves),
        grid=(NY // pair,),
        in_specs=specs,
        out_specs=[pl.BlockSpec((pair, tall, LANES), lambda i: (i, 0, 0))] * len(offsets),
        out_shape=[out] * len(offsets),
        compiler_params=params(),
        cost_estimate=cost(2 * rows * slots * NY * LANES * len(offsets), 4e6),
        name="sums",
    )(*args)


def start_kernel(post, weighted, relay, out):
    product = dot(post[...], weighted[0])
    for j in range(product.shape[1] // LANES):
        put(out, j, product[:, j * LANES : (j + 1) * LANES], relay[0, j])


def sums_start(offset, half, post, weighted, relay):
    rows, slots = post.shape
    pair = 2
    tall = rows + TILE
    return pl.pallas_call(
        start_kernel,
        grid=(1,),
        in_specs=[
            pl.BlockSpec((rows, slots), lambda i: (0, 0)),
            pl.BlockSpec((1, slots, pair * LANES), lambda i: (offset, 0, half)),
            pl.BlockSpec((1, pair, 8, LANES), lambda i: (offset, half, 0, 0)),
        ],
        out_specs=pl.BlockSpec((pair, tall, LANES), lambda i: (0, 0, 0)),
        out_shape=jax.ShapeDtypeStruct((pair, tall, LANES), I16),
        compiler_params=params(),
        cost_estimate=cost(2 * rows * slots * pair * LANES, 3e6),
        name="sums0",
    )(post, weighted, relay)


def finish_kernel(panels, own, a, b, c, sums, evidence):
    total, relay = decode(own[0])
    for other in (a, b, c):
        s, r = decode(other[...])
        total, relay = total + s, relay + r
    sums[...] = total.T[:, :panels]
    evidence[...] = relay


def finish(panels, own, others):
    tall = own.shape[1]
    whole = pl.BlockSpec((tall, LANES), lambda i: (0, 0))
    return pl.pallas_call(
        functools.partial(finish_kernel, panels),
        grid=(1,),
        in_specs=[pl.BlockSpec((1, tall, LANES), lambda i: (0, 0, 0))] + [whole] * 3,
        out_specs=[
            pl.BlockSpec((LANES, panels), lambda i: (0, 0)),
            pl.BlockSpec((8, LANES), lambda i: (0, 0)),
        ],
        out_shape=[
            jax.ShapeDtypeStruct((LANES, panels), F32),
            jax.ShapeDtypeStruct((8, LANES), F32),
        ],
        compiler_params=params(),
        name="finish",
    )(own, *others)


def along_z(x, shift):
    pairs = [(y * NZ + z, y * NZ + (z + shift) % NZ) for y in range(NY) for z in range(NZ)]
    return lax.ppermute(x, "ptcl", pairs)


def along_y(x, shift):
    pairs = [(y * NZ + z, (y + shift) % NY * NZ + z) for y in range(NY) for z in range(NZ)]
    return lax.ppermute(x, "ptcl", pairs)


def across(x, mask, size):
    return lax.ppermute(x, "cls", [(i, i ^ mask) for i in range(size)])


def shards(images, target, ctf_group, ctf_table, noise_weight, references):
    panels = references.shape[0]
    count = ctf_table.shape[0]
    me = lax.axis_index("ptcl")
    y, z = me // NZ, me % NZ
    rel_z, rel_y = jnp.arange(NZ * NY, dtype=I32) // NY, jnp.arange(NZ * NY, dtype=I32) % NY
    order = (y + rel_y) % NY * NZ + (z + rel_z) % NZ
    slots = images.shape[0]
    groups = ctf_group.reshape(1, slots)
    weighted, square = weigh(order, groups, images, ctf_table, noise_weight.reshape(1, -1))

    rows = -(-panels // 32) * 32
    mine = jnp.pad(references, ((0, rows - panels), (0, 0)))
    column = jnp.stack([mine] + [along_y(mine, NY - j) for j in range(1, NY)])
    up, down = [column], [column]
    for _ in range(NZ // 2 - 1):
        up.append(along_z(up[-1], 1))
        down.append(along_z(down[-1], -1))
    half = NY // 2
    far = [along_z(up[-1][:half], 1), along_z(down[-1][half:], -1)]
    carry = score(
        [0, 7, 1, 6, 2],
        [[column], [up[1]], [down[1]], [up[2]], [down[2]]],
        weighted, square, groups, None, False, panels,
    )
    mass, peak, evidence = score(
        [5, 3, 4], [[up[3]], [down[3]], far], weighted, square, groups, carry, True, panels
    )

    size = lax.axis_size("cls")
    mask = 1
    while mask < size:
        other = across(evidence, mask, size)
        top = jnp.maximum(evidence, other)
        evidence = top + jnp.log(jnp.exp(evidence - top) + jnp.exp(other - top))
        mask *= 2

    share = 24 * NZ * NY
    shard = target // share
    shard_y, shard_z = shard // NZ, shard % NZ
    block = (shard_z - z + NZ) % NZ * NY + (shard_y - y + NY) % NY
    place = jnp.where(target >= 0, (block * 8 + 2) * LANES + target % share, -1)
    post, weights, relay = posterior(mass, peak, evidence, place.reshape(1, slots), groups, count)
    relay = relay.reshape(NZ, NY, 8, LANES)

    class_weights = jnp.sum(lax.all_gather(weights, "ptcl", axis=0), axis=0)[:, :panels]

    far = NZ // 2
    came = [
        along_z(sums_start(far, 0, post, weighted, relay), 1),
        along_z(sums_start(far, 1, post, weighted, relay), -1),
    ]
    for step in range(far - 1, 0, -1):
        kind = "half" if step == far - 1 else "full"
        to_up, to_down = sums_step([step, NZ - step], kind, post, weighted, relay, came)
        came = [along_z(to_up, 1), along_z(to_down, -1)]
    (own,) = sums_step([0], "full", post, weighted, relay, came)
    others = [along_y(own[j], j) for j in range(1, NY)]
    class_sums, found = finish(panels, own, others)
    log_evidence = found[2:].reshape(-1)
    return class_sums, class_weights, log_evidence


def solution(mesh):
    placed = (P("ptcl", None), P("ptcl"), P("ptcl"), P(), P(), P("cls", "ptcl"))
    return jax.shard_map(
        shards,
        mesh=mesh,
        in_specs=placed,
        out_specs=(P("ptcl", "cls"), P(None, "cls"), P("ptcl")),
        check_vma=False,
    )
```

```python
import functools

import jax
import jax.numpy as jnp
from jax import lax
from jax.experimental import pallas as pl
from jax.experimental.pallas import tpu as pltpu
from jax.sharding import PartitionSpec as P

NY, NZ = 4, 8
LANES = 128
TILE = 16
F32, BF16, I16, I32 = jnp.float32, jnp.bfloat16, jnp.int16, jnp.int32
NT = (((1,), (1,)), ((), ()))
TN = (((0,), (0,)), ((), ()))
VMEM_LIMIT = 63 * 1024 * 1024
WEIGHT = 100
LOW_EXPONENT = -100.0


def dot(a, b, dims=(((1,), (0,)), ((), ()))):
    return lax.dot_general(a, b, dims, preferred_element_type=F32)


def split3(x):
    hi = x.astype(BF16)
    rest = x - hi.astype(F32)
    mid = rest.astype(BF16)
    low = (rest - mid.astype(F32)).astype(BF16)
    return jnp.concatenate([hi.astype(F32), mid.astype(F32), low.astype(F32)], axis=0).astype(BF16)


def onehot3(groups, count):
    row = lax.broadcasted_iota(I32, (3 * count, groups.shape[1]), 0)
    row = jnp.where(row >= 2 * count, row - 2 * count, jnp.where(row >= count, row - count, row))
    return (row == groups).astype(F32).astype(BF16)


def params(**kw):
    return pltpu.CompilerParams(vmem_limit_bytes=VMEM_LIMIT, **kw)


def cost(flops, byte_count):
    return pl.CostEstimate(flops=int(flops), bytes_accessed=int(byte_count), transcendentals=0)


def weight_kernel(order, groups, *refs):
    images, tables, noises = refs[:NY], refs[NY : 2 * NY], refs[2 * NY : 3 * NY]
    weighted, square = refs[3 * NY :]
    count = tables[0].shape[0]
    slots = images[0].shape[0]
    table = jnp.concatenate([t[...] for t in tables], axis=1)
    noise = jnp.concatenate([n[...] for n in noises], axis=1)
    square[0] = split3(table * table * noise)
    pieces = split3(table)
    member = onehot3(groups[...], count)
    step = 256
    for begin in range(0, slots, step):
        rows = dot(member[:, begin : begin + step], pieces, TN)
        picture = jnp.concatenate([i[begin : begin + step, :] for i in images], axis=1)
        weighted[0, begin : begin + step, :] = (picture.astype(F32) * rows * noise).astype(BF16)


def weigh(order, groups, images, table, noise):
    slots, count = images.shape[0], table.shape[0]
    wide = NY * LANES

    def block(j):
        return lambda i, o: (0, o[i * NY + j])

    specs = [pl.BlockSpec((1, slots), lambda i, o: (0, 0))]
    for rows in (slots, count, 1):
        specs += [pl.BlockSpec((rows, LANES), block(j)) for j in range(NY)]
    return pl.pallas_call(
        weight_kernel,
        grid_spec=pltpu.PrefetchScalarGridSpec(
            num_scalar_prefetch=1,
            grid=(NZ // 2,),
            in_specs=specs,
            out_specs=[
                pl.BlockSpec((1, slots, wide), lambda i, o: (i, 0, 0)),
                pl.BlockSpec((1, 3 * count, wide), lambda i, o: (i, 0, 0)),
            ],
        ),
        out_shape=[
            jax.ShapeDtypeStruct((NZ // 2, slots, wide), BF16),
            jax.ShapeDtypeStruct((NZ // 2, 3 * count, wide), BF16),
        ],
        compiler_params=params(),
        cost_estimate=cost(3e9 * WEIGHT, 2 * images.size),
        name="weigh",
    )(order, groups, *[images] * NY, *[table] * NY, *[noise] * NY)


def score_kernel(jobs, first, last, panels, passes, table, *refs):
    refs = list(refs)
    chunks = [[refs.pop(0) for _ in range(n)] for _, n in jobs]
    wa, wb, sa, sb, groups = refs[:5]
    refs = refs[5:]
    if not first:
        before = refs[:2]
        refs = refs[2:]
    refs = refs[passes:]
    state = refs[-2:] if last else refs[:2]
    step = pl.program_id(0)

    @pl.when(step == 0)
    def _():
        for k, ref in enumerate(state):
            ref[...] = jnp.zeros_like(ref) if first else before[k][...]

    for number, (place, _) in enumerate(jobs):

        @pl.when(step == number)
        def _(place=place, chunk=chunks[number]):
            panel = jnp.concatenate([c[j] for c in chunk for j in range(c.shape[0])], axis=1)
            right = (wa if place < NZ // 2 else wb)[0]
            square = (sa if place < NZ // 2 else sb)[0]
            state[0][...] += dot(panel, right, NT)
            wide = panel.astype(F32)
            wide = wide * wide
            hi = wide.astype(BF16)
            low = (wide - hi.astype(F32)).astype(BF16)
            state[1][...] += dot(hi, square, NT) + dot(low, square, NT)

    if last:
        mass, peak, evidence = refs[:3]

        @pl.when(step == len(jobs) - 1)
        def _():
            member = onehot3(groups[...], state[1].shape[1] // 3)
            each = state[1][...]
            hi = each.astype(BF16)
            rest = each - hi.astype(F32)
            mid = rest.astype(BF16)
            low = (rest - mid.astype(F32)).astype(BF16)
            offset = dot(hi, member) + dot(mid, member) + dot(low, member)
            value = state[0][...] - 0.5 * offset
            row = lax.broadcasted_iota(I32, value.shape, 0)
            value = jnp.where(row < panels, value, -jnp.inf)
            top = jnp.max(value, axis=0, keepdims=True)
            value = jnp.exp(value - top)
            mass[...] = value
            peak[...] = top
            evidence[...] = top + jnp.log(jnp.sum(value, axis=0, keepdims=True))


def score(jobs, weighted, square, groups, carry, last, panels, passed=None):
    rows = jobs[0][1][0].shape[1]
    slots = groups.shape[1]
    count3 = square[0].shape[1]
    wide = NY * LANES
    table = [[], []]
    for place, _ in jobs:
        for k in range(2):
            table[k].append(place % (NZ // 2) if k == place // (NZ // 2) else None)
    for row in table:
        known = [v for v in row if v is not None] or [0]
        previous = known[0]
        for i, v in enumerate(row):
            previous = row[i] = previous if v is None else v

    if all(place < NZ // 2 for place, _ in jobs):
        weighted, square = weighted[:1] * 2, square[:1] * 2

    def whole(shape):
        return pl.BlockSpec(shape, lambda i, t: (0,) * len(shape))

    specs = [whole(a.shape) for job in jobs for a in job[1]]
    for depth in (slots, count3):
        specs += [pl.BlockSpec((1, depth, wide), lambda i, t, k=k: (t[k, i], 0, 0)) for k in (0, 1)]
    specs.append(whole((1, slots)))
    state = [jax.ShapeDtypeStruct((rows, slots), F32), jax.ShapeDtypeStruct((rows, count3), F32)]
    if carry is not None:
        specs += [whole(s.shape) for s in state]
    if last:
        outs = [state[0]] + [jax.ShapeDtypeStruct((1, slots), F32)] * 2
        scratch = [pltpu.VMEM(s.shape, s.dtype) for s in state]
    else:
        outs, scratch = list(state), []
    out_specs = [whole(o.shape) for o in outs]
    args = [jnp.array(table, I32), *[a for job in jobs for a in job[1]], *weighted, *square, groups]
    args += [] if carry is None else list(carry)
    aliases = {}
    if passed is not None:
        aliases = {len(args): len(outs)}
        args.append(passed)
        specs.append(pl.BlockSpec(memory_space=pl.ANY))
        out_specs.append(pl.BlockSpec(memory_space=pl.ANY))
        outs.append(jax.ShapeDtypeStruct(passed.shape, passed.dtype))
    work = 2.5 * rows * slots * wide * len(jobs)
    found = pl.pallas_call(
        functools.partial(
            score_kernel,
            [(j[0], len(j[1])) for j in jobs],
            carry is None,
            last,
            panels,
            int(passed is not None),
        ),
        grid_spec=pltpu.PrefetchScalarGridSpec(
            num_scalar_prefetch=1,
            grid=(len(jobs),),
            in_specs=specs,
            out_specs=out_specs,
            scratch_shapes=scratch,
        ),
        out_shape=outs,
        input_output_aliases=aliases,
        compiler_params=params(),
        cost_estimate=cost(work * WEIGHT, 4e6 * len(jobs)),
        name="score",
    )(*args)
    return found if passed is None else (found[:-1], found[-1])


def posterior_kernel(mass, peak, evidence, place, groups, post, weights, relay):
    live = place[...] >= 0
    scale = jnp.where(live, jnp.exp(peak[...] - evidence[...]), 0.0)
    value = (mass[...] * scale).astype(BF16)
    post[...] = value
    count = weights.shape[1]
    slots = groups.shape[1]
    member = (lax.broadcasted_iota(I32, (count, slots), 0) == groups[...]).astype(F32).astype(BF16)
    for j in range(NY):
        begin = min(j * LANES, value.shape[0] - LANES)
        weights[j] = dot(member, value[begin : begin + LANES], NT)
    spot = place[...]
    line = lax.shift_right_arithmetic(spot, 7)
    high = (lax.broadcasted_iota(I32, (relay.shape[0], slots), 0) == line).astype(F32).astype(BF16)
    lane = lax.broadcasted_iota(I32, (LANES, slots), 0) == (spot & 127)
    found = split3(jnp.where(live, evidence[...], 0.0))
    out = jnp.zeros(relay.shape, F32)
    for k in (2, 1, 0):
        out += dot(high, jnp.where(lane, found[k : k + 1].astype(F32), 0.0).astype(BF16), NT)
    relay[...] = out


def posterior(mass, peak, evidence, place, groups, count):
    rows, slots = mass.shape
    return pl.pallas_call(
        posterior_kernel,
        out_shape=[
            jax.ShapeDtypeStruct((rows, slots), BF16),
            jax.ShapeDtypeStruct((NY, count, LANES), F32),
            jax.ShapeDtypeStruct((NZ * NY * 8, LANES), F32),
        ],
        compiler_params=params(),
        cost_estimate=cost(1e9, 5e6),
        name="posterior",
    )(mass, peak, evidence, place, groups)


def exponent(x):
    top = jnp.max(jnp.abs(x), axis=0, keepdims=True)
    return jnp.maximum(jnp.ceil(jnp.log2(jnp.maximum(top, 2.0**LOW_EXPONENT))), LOW_EXPONENT)


def to_int(x):
    return jnp.round(x).astype(I32)


def put(out, j, sums, relay, weights):
    rows = sums.shape[0]
    e = exponent(sums)
    out[j, :rows, :] = to_int(sums * jnp.exp2(14.0 - e)).astype(I16)
    row = lax.broadcasted_iota(I32, (8, LANES), 0)
    high = jnp.where(row == 0, e, 0.0).astype(I32)
    low = jnp.zeros_like(high)
    if relay is not None:
        f, g = exponent(relay), exponent(weights)
        up, down = jnp.exp2(14.0 - f), jnp.exp2(f - 14.0)
        part = jnp.round(relay * up)
        rest = to_int((relay - part * down) * up * 2.0**14)
        high = jnp.where(row < 2, jnp.where(row == 0, e, f), part).astype(I32)
        low = jnp.where(row < 2, jnp.where(row == 0, g, 0.0).astype(I32), rest)
        out[j, rows + TILE :, :] = to_int(weights * jnp.exp2(14.0 - g)).astype(I16)
    out[j, rows : rows + TILE, :] = jnp.concatenate([high, low], axis=0).astype(I16)


def number(x):
    return x.astype(I32).astype(F32)


def decode(block, rows):
    tail = number(block[rows : rows + TILE, :])
    high, low = tail[:8], tail[8:]
    sums = number(block[:rows, :]) * jnp.exp2(high[0:1] - 14.0)
    if block.shape[0] == rows + TILE:
        return sums, None, None
    down = jnp.exp2(high[1:2] - 14.0)
    row = lax.broadcasted_iota(I32, high.shape, 0)
    relay = jnp.where(row < 2, 0.0, (high + low * 2.0**-14) * down)
    return sums, relay, number(block[rows + TILE :, :]) * jnp.exp2(low[0:1] - 14.0)


def plus(a, b, keep=None):
    if keep is not None:
        b = [None if x is None else jnp.where(keep, x, 0.0) for x in b]
    return [None if x is None else x + w for x, w in zip(a, b)]


def terms(product, j, relay, weights):
    return [
        product[:, j * LANES : (j + 1) * LANES],
        None if relay is None else relay[0, j],
        None if weights is None else weights[j],
    ]


def ring_kernel(extra, keep, post, weighted, *refs):
    refs = list(refs)
    relay, weights = [refs.pop(0) for _ in range(2)] if extra else (None, None)
    came = refs.pop(0) if keep is not None else None
    out = refs.pop(0)
    rows = post.shape[0]
    product = dot(post[...], weighted[0])
    for j in range(2):
        mine = terms(product, j, relay, weights)
        if came is not None:
            mask = None if keep < 0 else pl.program_id(0) == keep
            mine = plus(mine, decode(came[j], rows), mask)
        put(out, j, *mine)


def ring_step(place, way, post, weighted, relay, weights, came):
    rows, slots = post.shape
    pair = 2
    tall = rows + TILE + weights.shape[1]
    far, near = place // (NZ // 2), place % (NZ // 2)
    begin = came is None
    halves = not begin and came.shape[0] < NY
    shift = way if begin else 0
    specs = [
        pl.BlockSpec((rows, slots), lambda i: (0, 0)),
        pl.BlockSpec((1, slots, pair * LANES), lambda i: (near, 0, i + shift)),
        pl.BlockSpec((1, pair, 8, LANES), lambda i: (place, i + shift, 0, 0)),
        pl.BlockSpec((pair, weights.shape[1], LANES), lambda i: (i + shift, 0, 0)),
    ]
    args = [post, weighted[far], relay, weights]
    if not begin:
        specs.append(pl.BlockSpec((pair, tall, LANES), lambda i: (0 if halves else i, 0, 0)))
        args.append(came)
    size = pair if begin else NY
    return pl.pallas_call(
        functools.partial(ring_kernel, True, None if begin else way if halves else -1),
        grid=(size // pair,),
        in_specs=specs,
        out_specs=pl.BlockSpec((pair, tall, LANES), lambda i: (i, 0, 0)),
        out_shape=jax.ShapeDtypeStruct((size, tall, LANES), I16),
        compiler_params=params(),
        cost_estimate=cost(2 * rows * slots * size * LANES, 4e6),
        name="ring",
    )(*args)


def last_kernel(post, weighted, relay, weights, up, down, out):
    rows = post.shape[0]
    step = pl.program_id(0)
    mass = []
    for j in range(NY):
        mass.append(weights[j] + decode(up[j], rows)[2] + decode(down[j], rows)[2])
    mass = jnp.concatenate(mass, axis=0)
    product = dot(post[...], weighted[0])
    for j in range(2):
        mine = terms(product, j, relay, None)
        for c in (up, down):
            mine = plus(mine, [*decode(c[2 * step + j], rows)[:2], None])
        put(out, j, mine[0], mine[1], mass)


def ring_last(post, weighted, relay, weights, came):
    rows, slots = post.shape
    pair = 2
    tall = rows + TILE + NY * weights.shape[1]

    def whole(a):
        return pl.BlockSpec(a.shape, lambda i: (0,) * len(a.shape))

    return pl.pallas_call(
        last_kernel,
        grid=(NY // pair,),
        in_specs=[
            whole(post),
            pl.BlockSpec((1, slots, pair * LANES), lambda i: (0, 0, i)),
            pl.BlockSpec((1, pair, 8, LANES), lambda i: (0, i, 0, 0)),
            whole(weights),
        ]
        + [whole(c) for c in came],
        out_specs=pl.BlockSpec((pair, tall, LANES), lambda i: (i, 0, 0)),
        out_shape=jax.ShapeDtypeStruct((NY, tall, LANES), I16),
        compiler_params=params(),
        cost_estimate=cost(2 * rows * slots * NY * LANES, 4e6),
        name="last",
    )(post, weighted[0], relay, weights, *came)


def finish_kernel(panels, rows, own, a, b, c, sums, evidence, weights):
    total = decode(own[0], rows)
    for other in (a, b, c):
        total = plus(total, decode(other[...], rows))
    sums[...] = total[0].T[:, :panels]
    evidence[...] = total[1]
    weights[...] = total[2]


def finish(panels, rows, own, others):
    tall = own.shape[1]
    whole = pl.BlockSpec((tall, LANES), lambda i: (0, 0))
    shapes = [(LANES, panels), (8, LANES), (tall - rows - TILE, LANES)]
    return pl.pallas_call(
        functools.partial(finish_kernel, panels, rows),
        grid=(1,),
        in_specs=[pl.BlockSpec((1, tall, LANES), lambda i: (0, 0, 0))] + [whole] * 3,
        out_specs=[pl.BlockSpec(s, lambda i: (0, 0)) for s in shapes],
        out_shape=[jax.ShapeDtypeStruct(s, F32) for s in shapes],
        compiler_params=params(),
        name="finish",
    )(own, *others)


def along_z(x, shift):
    pairs = [(y * NZ + z, y * NZ + (z + shift) % NZ) for y in range(NY) for z in range(NZ)]
    return lax.ppermute(x, "ptcl", pairs)


def along_y(x, shift):
    pairs = [(y * NZ + z, (y + shift) % NY * NZ + z) for y in range(NY) for z in range(NZ)]
    return lax.ppermute(x, "ptcl", pairs)


def across(x, mask, size):
    return lax.ppermute(x, "cls", [(i, i ^ mask) for i in range(size)])


def shards(images, target, ctf_group, ctf_table, noise_weight, references):
    panels = references.shape[0]
    count = ctf_table.shape[0]
    me = lax.axis_index("ptcl")
    y, z = me // NZ, me % NZ
    slots = images.shape[0]
    groups = ctf_group.reshape(1, slots)
    noise = noise_weight.reshape(1, -1)
    rel = jnp.arange(NZ * NY, dtype=I32)
    order = (y + rel % NY) % NY * NZ + (z + rel // NY) % NZ
    middle = NZ * NY // 2
    weighted, square = zip(
        *[weigh(o, groups, images, ctf_table, noise) for o in (order[:middle], order[middle:])]
    )

    rows = -(-panels // 32) * 32
    mine = jnp.pad(references, ((0, rows - panels), (0, 0)))
    column = jnp.stack([mine] + [along_y(mine, NY - j) for j in range(1, NY)])
    common = (weighted, square, groups)
    up, down = along_z(column, 1), None
    carry = score([(0, [column])], *common, None, False, panels)
    down = along_z(column, -1)
    for step in range(1, NZ // 2):
        jobs = [(NZ - step, [up]), (step, [down])]
        half = NY // 2
        ahead = along_z(up if step < half + 1 else up[:half], 1)
        carry = score(jobs, *common, carry, False, panels)
        down = along_z(down if step < half + 1 else down[half:], -1)
        up = ahead
    mass, peak, evidence = score([(NZ // 2, [up, down])], *common, carry, True, panels)

    size = lax.axis_size("cls")
    mask = 1
    while mask < size:
        other = across(evidence, mask, size)
        top = jnp.maximum(evidence, other)
        evidence = top + jnp.log(jnp.exp(evidence - top) + jnp.exp(other - top))
        mask *= 2

    share = 24 * NZ * NY
    shard = target // share
    shard_y, shard_z = shard // NZ, shard % NZ
    block = (shard_z - z + NZ) % NZ * NY + (shard_y - y + NY) % NY
    place = jnp.where(target >= 0, (block * 8 + 2) * LANES + target % share, -1)
    post, weights, relay = posterior(mass, peak, evidence, place.reshape(1, slots), groups, count)
    relay = relay.reshape(NZ, NY, 8, LANES)

    fixed = (post, weighted, relay, weights)
    middle = NZ // 2
    up = down = None
    for step in range(middle, 0, -1):
        up = along_z(ring_step(step, 0, *fixed, up), 1)
        down = along_z(ring_step(NZ - step, 1, *fixed, down), -1)
    own = ring_last(*fixed, (up, down))
    others = [along_y(own[j], j) for j in range(1, NY)]
    class_sums, found, quarters = finish(panels, rows, own, others)
    log_evidence = found[2:].reshape(-1)
    quarters = quarters.reshape(NY, count, LANES)
    skip = NY * LANES - rows
    class_weights = jnp.concatenate(
        [quarters[j] for j in range(NY - 1)] + [quarters[NY - 1][:, skip:]], axis=1
    )[:, :panels]
    return class_sums, class_weights, log_evidence


def solution(mesh):
    placed = (P("ptcl", None), P("ptcl"), P("ptcl"), P(), P(), P("cls", "ptcl"))
    return jax.shard_map(
        shards,
        mesh=mesh,
        in_specs=placed,
        out_specs=(P("ptcl", "cls"), P(None, "cls"), P("ptcl")),
        check_vma=False,
    )
```

```python
import functools

import jax
import jax.numpy as jnp
from jax import lax
from jax.experimental import pallas as pl
from jax.experimental.pallas import tpu as pltpu
from jax.sharding import PartitionSpec as P

NY, NZ = 4, 8
LANES = 128
TILE = 16
F32, BF16, I16, I32 = jnp.float32, jnp.bfloat16, jnp.int16, jnp.int32
NT = (((1,), (1,)), ((), ()))
TN = (((0,), (0,)), ((), ()))
WEIGH_VMEM, SCORE_VMEM, POST_VMEM, RING_VMEM = 20, 34, 24, 16
WEIGHT = 100
LOW_EXPONENT = -100.0


def dot(a, b, dims=(((1,), (0,)), ((), ()))):
    return lax.dot_general(a, b, dims, preferred_element_type=F32)


def split3(x):
    hi = x.astype(BF16)
    rest = x - hi.astype(F32)
    mid = rest.astype(BF16)
    low = (rest - mid.astype(F32)).astype(BF16)
    return jnp.concatenate([hi.astype(F32), mid.astype(F32), low.astype(F32)], axis=0).astype(BF16)


def onehot3(groups, count):
    row = lax.broadcasted_iota(I32, (3 * count, groups.shape[1]), 0)
    row = jnp.where(row >= 2 * count, row - 2 * count, jnp.where(row >= count, row - count, row))
    return (row == groups).astype(F32).astype(BF16)


def params(size):
    return pltpu.CompilerParams(vmem_limit_bytes=size * 1024 * 1024)


def cost(flops, byte_count):
    return pl.CostEstimate(flops=int(flops), bytes_accessed=int(byte_count), transcendentals=0)


def weight_kernel(order, groups, *refs):
    images, tables, noises = refs[:NY], refs[NY : 2 * NY], refs[2 * NY : 3 * NY]
    weighted, square = refs[3 * NY :]
    count = tables[0].shape[0]
    slots = images[0].shape[0]
    table = jnp.concatenate([t[...] for t in tables], axis=1)
    noise = jnp.concatenate([n[...] for n in noises], axis=1)
    square[0] = split3(table * table * noise)
    pieces = split3(table)
    member = onehot3(groups[...], count)
    step = 256
    for begin in range(0, slots, step):
        rows = dot(member[:, begin : begin + step], pieces, TN)
        picture = jnp.concatenate([i[begin : begin + step, :] for i in images], axis=1)
        weighted[0, begin : begin + step, :] = (picture.astype(F32) * rows * noise).astype(BF16)


def weigh(order, groups, images, table, noise):
    slots, count = images.shape[0], table.shape[0]
    wide = NY * LANES

    def block(j):
        return lambda i, o: (0, o[i * NY + j])

    specs = [pl.BlockSpec((1, slots), lambda i, o: (0, 0))]
    for rows in (slots, count, 1):
        specs += [pl.BlockSpec((rows, LANES), block(j)) for j in range(NY)]
    return pl.pallas_call(
        weight_kernel,
        grid_spec=pltpu.PrefetchScalarGridSpec(
            num_scalar_prefetch=1,
            grid=(NZ // 2,),
            in_specs=specs,
            out_specs=[
                pl.BlockSpec((1, slots, wide), lambda i, o: (i, 0, 0)),
                pl.BlockSpec((1, 3 * count, wide), lambda i, o: (i, 0, 0)),
            ],
        ),
        out_shape=[
            jax.ShapeDtypeStruct((NZ // 2, slots, wide), BF16),
            jax.ShapeDtypeStruct((NZ // 2, 3 * count, wide), BF16),
        ],
        compiler_params=params(WEIGH_VMEM),
        cost_estimate=cost(3e9 * WEIGHT, 2 * images.size),
        name="weigh",
    )(order, groups, *[images] * NY, *[table] * NY, *[noise] * NY)


def score_kernel(jobs, first, last, panels, passes, table, *refs):
    refs = list(refs)
    chunks = [[refs.pop(0) for _ in range(n)] for _, n in jobs]
    wa, wb, sa, sb, groups = refs[:5]
    refs = refs[5:]
    if not first:
        before = refs[:2]
        refs = refs[2:]
    refs = refs[passes:]
    state = refs[-2:] if last else refs[:2]
    step = pl.program_id(0)

    @pl.when(step == 0)
    def _():
        for k, ref in enumerate(state):
            ref[...] = jnp.zeros_like(ref) if first else before[k][...]

    for number, (place, _) in enumerate(jobs):

        @pl.when(step == number)
        def _(place=place, chunk=chunks[number]):
            panel = jnp.concatenate([c[j] for c in chunk for j in range(c.shape[0])], axis=1)
            right = (wa if place < NZ // 2 else wb)[0]
            square = (sa if place < NZ // 2 else sb)[0]
            state[0][...] += dot(panel, right, NT)
            wide = panel.astype(F32)
            wide = wide * wide
            hi = wide.astype(BF16)
            low = (wide - hi.astype(F32)).astype(BF16)
            state[1][...] += dot(hi, square, NT) + dot(low, square, NT)

    if last:
        mass, peak, evidence = refs[:3]

        @pl.when(step == len(jobs) - 1)
        def _():
            member = onehot3(groups[...], state[1].shape[1] // 3)
            each = state[1][...]
            hi = each.astype(BF16)
            rest = each - hi.astype(F32)
            mid = rest.astype(BF16)
            low = (rest - mid.astype(F32)).astype(BF16)
            offset = dot(hi, member) + dot(mid, member) + dot(low, member)
            value = state[0][...] - 0.5 * offset
            row = lax.broadcasted_iota(I32, value.shape, 0)
            value = jnp.where(row < panels, value, -jnp.inf)
            top = jnp.max(value, axis=0, keepdims=True)
            value = jnp.exp(value - top)
            mass[...] = value
            peak[...] = top
            evidence[...] = top + jnp.log(jnp.sum(value, axis=0, keepdims=True))


def score(jobs, weighted, square, groups, carry, last, panels, passed=None):
    rows = jobs[0][1][0].shape[1]
    slots = groups.shape[1]
    count3 = square[0].shape[1]
    wide = NY * LANES
    table = [[], []]
    for place, _ in jobs:
        for k in range(2):
            table[k].append(place % (NZ // 2) if k == place // (NZ // 2) else None)
    for row in table:
        known = [v for v in row if v is not None] or [0]
        previous = known[0]
        for i, v in enumerate(row):
            previous = row[i] = previous if v is None else v

    if all(place < NZ // 2 for place, _ in jobs):
        weighted, square = weighted[:1] * 2, square[:1] * 2

    def whole(shape):
        return pl.BlockSpec(shape, lambda i, t: (0,) * len(shape))

    specs = [whole(a.shape) for job in jobs for a in job[1]]
    for depth in (slots, count3):
        specs += [pl.BlockSpec((1, depth, wide), lambda i, t, k=k: (t[k, i], 0, 0)) for k in (0, 1)]
    specs.append(whole((1, slots)))
    state = [jax.ShapeDtypeStruct((rows, slots), F32), jax.ShapeDtypeStruct((rows, count3), F32)]
    if carry is not None:
        specs += [whole(s.shape) for s in state]
    if last:
        outs = [state[0]] + [jax.ShapeDtypeStruct((1, slots), F32)] * 2
        scratch = [pltpu.VMEM(s.shape, s.dtype) for s in state]
    else:
        outs, scratch = list(state), []
    out_specs = [whole(o.shape) for o in outs]
    args = [jnp.array(table, I32), *[a for job in jobs for a in job[1]], *weighted, *square, groups]
    args += [] if carry is None else list(carry)
    aliases = {}
    if passed is not None:
        aliases = {len(args): len(outs)}
        args.append(passed)
        specs.append(pl.BlockSpec(memory_space=pl.ANY))
        out_specs.append(pl.BlockSpec(memory_space=pl.ANY))
        outs.append(jax.ShapeDtypeStruct(passed.shape, passed.dtype))
    work = 2.5 * rows * slots * wide * len(jobs)
    found = pl.pallas_call(
        functools.partial(
            score_kernel,
            [(j[0], len(j[1])) for j in jobs],
            carry is None,
            last,
            panels,
            int(passed is not None),
        ),
        grid_spec=pltpu.PrefetchScalarGridSpec(
            num_scalar_prefetch=1,
            grid=(len(jobs),),
            in_specs=specs,
            out_specs=out_specs,
            scratch_shapes=scratch,
        ),
        out_shape=outs,
        input_output_aliases=aliases,
        compiler_params=params(SCORE_VMEM),
        cost_estimate=cost(work * WEIGHT, 4e6 * len(jobs)),
        name="score",
    )(*args)
    return found if passed is None else (found[:-1], found[-1])


def posterior_kernel(mass, peak, evidence, place, groups, post, weights, relay):
    live = place[...] >= 0
    scale = jnp.where(live, jnp.exp(peak[...] - evidence[...]), 0.0)
    value = (mass[...] * scale).astype(BF16)
    post[...] = value
    count = weights.shape[1]
    slots = groups.shape[1]
    member = (lax.broadcasted_iota(I32, (count, slots), 0) == groups[...]).astype(F32).astype(BF16)
    for j in range(NY):
        begin = min(j * LANES, value.shape[0] - LANES)
        weights[j] = dot(member, value[begin : begin + LANES], NT)
    spot = place[...]
    line = lax.shift_right_arithmetic(spot, 7)
    high = (lax.broadcasted_iota(I32, (relay.shape[0], slots), 0) == line).astype(F32).astype(BF16)
    lane = lax.broadcasted_iota(I32, (LANES, slots), 0) == (spot & 127)
    found = split3(jnp.where(live, evidence[...], 0.0))
    out = jnp.zeros(relay.shape, F32)
    for k in (2, 1, 0):
        out += dot(high, jnp.where(lane, found[k : k + 1].astype(F32), 0.0).astype(BF16), NT)
    relay[...] = out


def posterior(mass, peak, evidence, place, groups, count):
    rows, slots = mass.shape
    return pl.pallas_call(
        posterior_kernel,
        out_shape=[
            jax.ShapeDtypeStruct((rows, slots), BF16),
            jax.ShapeDtypeStruct((NY, count, LANES), F32),
            jax.ShapeDtypeStruct((NZ * NY * 8, LANES), F32),
        ],
        compiler_params=params(POST_VMEM),
        cost_estimate=cost(1e9, 5e6),
        name="posterior",
    )(mass, peak, evidence, place, groups)


def exponent(x):
    top = jnp.max(jnp.abs(x), axis=0, keepdims=True)
    return jnp.maximum(jnp.ceil(jnp.log2(jnp.maximum(top, 2.0**LOW_EXPONENT))), LOW_EXPONENT)


def to_int(x):
    return jnp.round(x).astype(I32)


def put(out, j, sums, relay, weights):
    rows = sums.shape[0]
    e = exponent(sums)
    out[j, :rows, :] = to_int(sums * jnp.exp2(14.0 - e)).astype(I16)
    row = lax.broadcasted_iota(I32, (8, LANES), 0)
    high = jnp.where(row == 0, e, 0.0).astype(I32)
    low = jnp.zeros_like(high)
    if relay is not None:
        f, g = exponent(relay), exponent(weights)
        up, down = jnp.exp2(14.0 - f), jnp.exp2(f - 14.0)
        part = jnp.round(relay * up)
        rest = to_int((relay - part * down) * up * 2.0**14)
        high = jnp.where(row < 2, jnp.where(row == 0, e, f), part).astype(I32)
        low = jnp.where(row < 2, jnp.where(row == 0, g, 0.0).astype(I32), rest)
        out[j, rows + TILE :, :] = to_int(weights * jnp.exp2(14.0 - g)).astype(I16)
    out[j, rows : rows + TILE, :] = jnp.concatenate([high, low], axis=0).astype(I16)


def number(x):
    return x.astype(I32).astype(F32)


def decode(block, rows):
    tail = number(block[rows : rows + TILE, :])
    high, low = tail[:8], tail[8:]
    sums = number(block[:rows, :]) * jnp.exp2(high[0:1] - 14.0)
    if block.shape[0] == rows + TILE:
        return sums, None, None
    down = jnp.exp2(high[1:2] - 14.0)
    row = lax.broadcasted_iota(I32, high.shape, 0)
    relay = jnp.where(row < 2, 0.0, (high + low * 2.0**-14) * down)
    return sums, relay, number(block[rows + TILE :, :]) * jnp.exp2(low[0:1] - 14.0)


def plus(a, b, keep=None):
    if keep is not None:
        b = [None if x is None else jnp.where(keep, x, 0.0) for x in b]
    return [None if x is None else x + w for x, w in zip(a, b)]


def terms(product, j, relay, weights):
    return [
        product[:, j * LANES : (j + 1) * LANES],
        None if relay is None else relay[0, j],
        None if weights is None else weights[j],
    ]


def ring_kernel(extra, ways, post, *refs):
    refs = list(refs)
    weighted = [refs.pop(0) for _ in range(ways)]
    relay = [refs.pop(0) for _ in range(ways)] if extra else [None] * ways
    weights = refs.pop(0) if extra else None
    outs = [refs.pop() for _ in range(ways)][::-1]
    came = refs + [None] * (ways - len(refs))
    rows = post.shape[0]
    for way in range(ways):
        product = dot(post[...], weighted[way][0])
        for j in range(2):
            mine = terms(product, j, relay[way], weights)
            if came[way] is not None:
                mine = plus(mine, decode(came[way][j], rows))
            put(outs[way], j, *mine)


def ring_step(places, stream, post, weighted, relay, weights, came):
    rows, slots = post.shape[0] // 2, post.shape[1]
    extra = stream == 0
    pair = 2
    tall = rows + TILE + (weights.shape[1] if extra else 0)
    specs, args = [pl.BlockSpec((rows, slots), lambda i: (stream, 0))], [post]
    for p in places:
        far, near = p // (NZ // 2), p % (NZ // 2)
        specs.append(pl.BlockSpec((1, slots, pair * LANES), lambda i, p=near: (p, 0, i)))
        args.append(weighted[far])
    if extra:
        specs += [pl.BlockSpec((1, pair, 8, LANES), lambda i, p=p: (p, i, 0, 0)) for p in places]
        specs.append(pl.BlockSpec((pair, weights.shape[1], LANES), lambda i: (i, 0, 0)))
        args += [relay] * len(places) + [weights]
    block = pl.BlockSpec((pair, tall, LANES), lambda i: (i, 0, 0))
    return pl.pallas_call(
        functools.partial(ring_kernel, extra, len(places)),
        grid=(NY // pair,),
        in_specs=specs + [block] * len(came),
        out_specs=[block] * len(places),
        out_shape=[jax.ShapeDtypeStruct((NY, tall, LANES), I16)] * len(places),
        compiler_params=params(RING_VMEM),
        cost_estimate=cost(2 * rows * slots * NY * LANES * len(places), 4e6),
        name="ring",
    )(*args, *came)


def last_kernel(post, weighted, relay, weights, *refs):
    came, out = [refs[:2], refs[2:4]], refs[4]
    rows = post.shape[0] // 2
    step = pl.program_id(0)
    mass = []
    for j in range(NY):
        value = weights[j]
        for c in came[0]:
            value += decode(c[j], rows)[2]
        mass.append(value)
    mass = jnp.concatenate(mass, axis=0)
    product = dot(post[...], weighted[0])
    for j in range(2):
        both = []
        for stream in range(2):
            part = product[stream * rows : stream * rows + rows]
            mine = terms(part, j, relay if stream == 0 else None, None)
            for c in came[stream]:
                got = decode(c[2 * step + j], rows)
                mine = plus(mine, [got[0], got[1], None])
            both.append(mine)
        put(out, j, jnp.concatenate([both[0][0], both[1][0]], axis=0), both[0][1], mass)


def ring_last(post, weighted, relay, weights, came):
    rows, slots = post.shape
    pair = 2
    tall = rows + TILE + NY * weights.shape[1]

    def whole(a):
        return pl.BlockSpec(a.shape, lambda i: (0,) * len(a.shape))

    came = came[0] + came[1]
    return pl.pallas_call(
        last_kernel,
        grid=(NY // pair,),
        in_specs=[
            whole(post),
            pl.BlockSpec((1, slots, pair * LANES), lambda i: (0, 0, i)),
            pl.BlockSpec((1, pair, 8, LANES), lambda i: (0, i, 0, 0)),
            whole(weights),
        ]
        + [whole(c) for c in came],
        out_specs=pl.BlockSpec((pair, tall, LANES), lambda i: (i, 0, 0)),
        out_shape=jax.ShapeDtypeStruct((NY, tall, LANES), I16),
        compiler_params=params(RING_VMEM),
        cost_estimate=cost(2 * rows * slots * NY * LANES, 4e6),
        name="last",
    )(post, weighted[0], relay, weights, *came)


def finish_kernel(panels, rows, own, a, b, c, sums, evidence, weights):
    total = decode(own[0], rows)
    for other in (a, b, c):
        total = plus(total, decode(other[...], rows))
    sums[...] = total[0].T[:, :panels]
    evidence[...] = total[1]
    weights[...] = total[2]


def finish(panels, rows, own, others):
    tall = own.shape[1]
    whole = pl.BlockSpec((tall, LANES), lambda i: (0, 0))
    shapes = [(LANES, panels), (8, LANES), (tall - rows - TILE, LANES)]
    return pl.pallas_call(
        functools.partial(finish_kernel, panels, rows),
        grid=(1,),
        in_specs=[pl.BlockSpec((1, tall, LANES), lambda i: (0, 0, 0))] + [whole] * 3,
        out_specs=[pl.BlockSpec(s, lambda i: (0, 0)) for s in shapes],
        out_shape=[jax.ShapeDtypeStruct(s, F32) for s in shapes],
        compiler_params=params(RING_VMEM),
        name="finish",
    )(own, *others)


def along_z(x, shift):
    pairs = [(y * NZ + z, y * NZ + (z + shift) % NZ) for y in range(NY) for z in range(NZ)]
    return lax.ppermute(x, "ptcl", pairs)


def along_y(x, shift):
    pairs = [(y * NZ + z, (y + shift) % NY * NZ + z) for y in range(NY) for z in range(NZ)]
    return lax.ppermute(x, "ptcl", pairs)


def across(x, mask, size):
    return lax.ppermute(x, "cls", [(i, i ^ mask) for i in range(size)])


def shards(images, target, ctf_group, ctf_table, noise_weight, references):
    panels = references.shape[0]
    count = ctf_table.shape[0]
    me = lax.axis_index("ptcl")
    y, z = me // NZ, me % NZ
    slots = images.shape[0]
    groups = ctf_group.reshape(1, slots)
    noise = noise_weight.reshape(1, -1)
    rel = jnp.arange(NZ * NY, dtype=I32)
    order = (y + rel % NY) % NY * NZ + (z + rel // NY) % NZ
    middle = NZ * NY // 2
    weighted, square = zip(
        *[weigh(o, groups, images, ctf_table, noise) for o in (order[:middle], order[middle:])]
    )

    rows = -(-panels // 32) * 32
    mine = jnp.pad(references, ((0, rows - panels), (0, 0)))
    column = jnp.stack([mine] + [along_y(mine, NY - j) for j in range(1, NY)])
    common = (weighted, square, groups)
    up, down = along_z(column, 1), along_z(column, -1)
    jobs, carry = [(0, [column])], None
    for step in range(1, NZ // 2):
        jobs += [(NZ - step, [up]), (step, [down])]
        half = NY // 2
        whole = step <= half
        ahead = [along_z(up if whole else up[:half], 1), along_z(down if whole else down[half:], -1)]
        carry, jobs = score(jobs, *common, carry, False, panels), []
        up, down = ahead
    mass, peak, evidence = score([(NZ // 2, [up, down])], *common, carry, True, panels)

    size = lax.axis_size("cls")
    mask = 1
    while mask < size:
        other = across(evidence, mask, size)
        top = jnp.maximum(evidence, other)
        evidence = top + jnp.log(jnp.exp(evidence - top) + jnp.exp(other - top))
        mask *= 2

    share = 24 * NZ * NY
    shard = target // share
    shard_y, shard_z = shard // NZ, shard % NZ
    block = (shard_z - z + NZ) % NZ * NY + (shard_y - y + NY) % NY
    place = jnp.where(target >= 0, (block * 8 + 2) * LANES + target % share, -1)
    post, weights, relay = posterior(mass, peak, evidence, place.reshape(1, slots), groups, count)
    relay = relay.reshape(NZ, NY, 8, LANES)

    fixed = (post, weighted, relay, weights)
    far = NZ // 2
    came = [[along_z(ring_step([far], n, *fixed, [])[0], 1 - 2 * n)] for n in range(2)]
    for step in range(far - 1, 0, -1):
        for n in range(2):
            places = [step, NZ - step][:: 1 - 2 * n]
            blocks = ring_step(places, n, *fixed, came[n])
            came[n] = [along_z(x, d) for x, d in zip(blocks, (1 - 2 * n, 2 * n - 1))]
    own = ring_last(*fixed, came)
    others = [along_y(own[j], j) for j in range(1, NY)]
    class_sums, found, quarters = finish(panels, rows, own, others)
    log_evidence = found[2:].reshape(-1)
    quarters = quarters.reshape(NY, count, LANES)
    skip = NY * LANES - rows
    class_weights = jnp.concatenate(
        [quarters[j] for j in range(NY - 1)] + [quarters[NY - 1][:, skip:]], axis=1
    )[:, :panels]
    return class_sums, class_weights, log_evidence


def solution(mesh):
    placed = (P("ptcl", None), P("ptcl"), P("ptcl"), P(), P(), P("cls", "ptcl"))
    return jax.shard_map(
        shards,
        mesh=mesh,
        in_specs=placed,
        out_specs=(P("ptcl", "cls"), P(None, "cls"), P("ptcl")),
        check_vma=False,
    )
```

```python
import functools

import jax
import jax.numpy as jnp
from jax import lax
from jax.experimental import pallas as pl
from jax.experimental.pallas import tpu as pltpu
from jax.sharding import PartitionSpec as P

NY, NZ = 4, 8
LANES = 128
TILE = 16
F32, BF16, I16, I32 = jnp.float32, jnp.bfloat16, jnp.int16, jnp.int32
NT = (((1,), (1,)), ((), ()))
TN = (((0,), (0,)), ((), ()))
WEIGH_VMEM, SCORE_VMEM, POST_VMEM, RING_VMEM = 44, 34, 24, 16
WEIGHT = 100
LOW_EXPONENT = -100.0


def dot(a, b, dims=(((1,), (0,)), ((), ()))):
    return lax.dot_general(a, b, dims, preferred_element_type=F32)


def split3(x):
    hi = x.astype(BF16)
    rest = x - hi.astype(F32)
    mid = rest.astype(BF16)
    low = (rest - mid.astype(F32)).astype(BF16)
    return jnp.concatenate([hi.astype(F32), mid.astype(F32), low.astype(F32)], axis=0).astype(BF16)


def onehot3(groups, count):
    row = lax.broadcasted_iota(I32, (3 * count, groups.shape[1]), 0)
    row = jnp.where(row >= 2 * count, row - 2 * count, jnp.where(row >= count, row - count, row))
    return (row == groups).astype(F32).astype(BF16)


def params(size):
    return pltpu.CompilerParams(vmem_limit_bytes=size * 1024 * 1024)


def cost(flops, byte_count):
    return pl.CostEstimate(flops=int(flops), bytes_accessed=int(byte_count), transcendentals=0)


def weight_kernel(order, groups, *refs):
    images, tables, noises = refs[:NY], refs[NY : 2 * NY], refs[2 * NY : 3 * NY]
    weighted, square = refs[3 * NY :]
    count = tables[0].shape[0]
    slots = images[0].shape[0]
    table = jnp.concatenate([t[...] for t in tables], axis=1)
    noise = jnp.concatenate([n[...] for n in noises], axis=1)
    square[0] = split3(table * table * noise)
    pieces = split3(table)
    member = onehot3(groups[...], count)
    step = 256
    for begin in range(0, slots, step):
        rows = dot(member[:, begin : begin + step], pieces, TN)
        picture = jnp.concatenate([i[begin : begin + step, :] for i in images], axis=1)
        weighted[0, begin : begin + step, :] = (picture.astype(F32) * rows * noise).astype(BF16)


def weigh(order, groups, images, table, noise):
    slots, count = images.shape[0], table.shape[0]
    wide = NY * LANES

    def block(j):
        return lambda i, o: (0, o[i * NY + j])

    specs = [pl.BlockSpec((1, slots), lambda i, o: (0, 0))]
    for rows in (slots, count, 1):
        specs += [pl.BlockSpec((rows, LANES), block(j)) for j in range(NY)]
    return pl.pallas_call(
        weight_kernel,
        grid_spec=pltpu.PrefetchScalarGridSpec(
            num_scalar_prefetch=1,
            grid=(NZ // 2,),
            in_specs=specs,
            out_specs=[
                pl.BlockSpec((1, slots, wide), lambda i, o: (i, 0, 0)),
                pl.BlockSpec((1, 3 * count, wide), lambda i, o: (i, 0, 0)),
            ],
        ),
        out_shape=[
            jax.ShapeDtypeStruct((NZ // 2, slots, wide), BF16),
            jax.ShapeDtypeStruct((NZ // 2, 3 * count, wide), BF16),
        ],
        compiler_params=params(WEIGH_VMEM),
        cost_estimate=cost(3e9 * WEIGHT, 2 * images.size),
        name="weigh",
    )(order, groups, *[images] * NY, *[table] * NY, *[noise] * NY)


def stack_kernel(*refs):
    blocks, (top, bottom) = refs[:NY], refs[NY:]
    half = top.shape[1]
    rest = blocks[0].shape[0] - half
    for j, block in enumerate(blocks):
        top[j] = block[:half, :]
        bottom[j, half - TILE :, :] = jnp.zeros((TILE, LANES), BF16)
        bottom[j, :rest, :] = block[half:, :]


def stack(blocks, half):
    return pl.pallas_call(
        stack_kernel,
        out_shape=[jax.ShapeDtypeStruct((NY, half, LANES), BF16)] * 2,
        compiler_params=params(RING_VMEM),
        name="stack",
    )(*blocks)


def score_kernel(jobs, first, last, panels, table, *refs):
    refs = list(refs)
    chunks = [[refs.pop(0) for _ in range(n)] for _, n in jobs]
    wa, wb, sa, sb, groups = refs[:5]
    refs = refs[5:]
    if not first:
        before = refs[:2]
        refs = refs[2:]
    state = refs[-2:] if last else refs[:2]
    step = pl.program_id(0)

    @pl.when(step == 0)
    def _():
        for k, ref in enumerate(state):
            ref[...] = jnp.zeros_like(ref) if first else before[k][...]

    for number, (place, _) in enumerate(jobs):

        @pl.when(step == number)
        def _(place=place, chunk=chunks[number]):
            parts = [jnp.concatenate([c[j] for j in range(NY)], axis=1) for c in chunk]
            panel = jnp.concatenate(parts, axis=0)
            right = (wa if place < NZ // 2 else wb)[0]
            square = (sa if place < NZ // 2 else sb)[0]
            state[0][...] += dot(panel, right, NT)
            wide = panel.astype(F32)
            wide = wide * wide
            hi = wide.astype(BF16)
            low = (wide - hi.astype(F32)).astype(BF16)
            state[1][...] += dot(hi, square, NT) + dot(low, square, NT)

    if last:
        mass, peak, evidence = refs[:3]

        @pl.when(step == len(jobs) - 1)
        def _():
            member = onehot3(groups[...], state[1].shape[1] // 3)
            each = state[1][...]
            hi = each.astype(BF16)
            rest = each - hi.astype(F32)
            mid = rest.astype(BF16)
            low = (rest - mid.astype(F32)).astype(BF16)
            offset = dot(hi, member) + dot(mid, member) + dot(low, member)
            value = state[0][...] - 0.5 * offset
            row = lax.broadcasted_iota(I32, value.shape, 0)
            value = jnp.where(row < panels, value, -jnp.inf)
            top = jnp.max(value, axis=0, keepdims=True)
            value = jnp.exp(value - top)
            mass[...] = value
            peak[...] = top
            evidence[...] = top + jnp.log(jnp.sum(value, axis=0, keepdims=True))


def score(jobs, weighted, square, groups, carry, last, panels):
    rows = sum(a.shape[1] for a in jobs[0][1])
    slots = groups.shape[1]
    count3 = square[0].shape[1]
    wide = NY * LANES
    table = [[], []]
    for place, _ in jobs:
        for k in range(2):
            table[k].append(place % (NZ // 2) if k == place // (NZ // 2) else None)
    for row in table:
        known = [v for v in row if v is not None] or [0]
        previous = known[0]
        for i, v in enumerate(row):
            previous = row[i] = previous if v is None else v

    if all(place < NZ // 2 for place, _ in jobs):
        weighted, square = weighted[:1] * 2, square[:1] * 2

    def whole(shape):
        return pl.BlockSpec(shape, lambda i, t: (0,) * len(shape))

    specs = [whole(a.shape) for job in jobs for a in job[1]]
    for depth in (slots, count3):
        specs += [pl.BlockSpec((1, depth, wide), lambda i, t, k=k: (t[k, i], 0, 0)) for k in (0, 1)]
    specs.append(whole((1, slots)))
    state = [jax.ShapeDtypeStruct((rows, slots), F32), jax.ShapeDtypeStruct((rows, count3), F32)]
    if carry is not None:
        specs += [whole(s.shape) for s in state]
    if last:
        outs = [state[0]] + [jax.ShapeDtypeStruct((1, slots), F32)] * 2
        scratch = [pltpu.VMEM(s.shape, s.dtype) for s in state]
    else:
        outs, scratch = list(state), []
    out_specs = [whole(o.shape) for o in outs]
    args = [jnp.array(table, I32), *[a for job in jobs for a in job[1]], *weighted, *square, groups]
    args += [] if carry is None else list(carry)
    work = 2.5 * rows * slots * wide * len(jobs)
    return pl.pallas_call(
        functools.partial(
            score_kernel,
            [(j[0], len(j[1])) for j in jobs],
            carry is None,
            last,
            panels,
        ),
        grid_spec=pltpu.PrefetchScalarGridSpec(
            num_scalar_prefetch=1,
            grid=(len(jobs),),
            in_specs=specs,
            out_specs=out_specs,
            scratch_shapes=scratch,
        ),
        out_shape=outs,
        compiler_params=params(SCORE_VMEM),
        cost_estimate=cost(work * WEIGHT, 4e6 * len(jobs)),
        name="score",
    )(*args)


def posterior_kernel(mass, peak, evidence, place, groups, post, weights, relay):
    live = place[...] >= 0
    scale = jnp.where(live, jnp.exp(peak[...] - evidence[...]), 0.0)
    value = (mass[...] * scale).astype(BF16)
    post[...] = value
    count = weights.shape[1]
    slots = groups.shape[1]
    member = (lax.broadcasted_iota(I32, (count, slots), 0) == groups[...]).astype(F32).astype(BF16)
    for j in range(NY):
        begin = min(j * LANES, value.shape[0] - LANES)
        weights[j] = dot(member, value[begin : begin + LANES], NT)
    spot = place[...]
    line = lax.shift_right_arithmetic(spot, 7)
    high = (lax.broadcasted_iota(I32, (relay.shape[0], slots), 0) == line).astype(F32).astype(BF16)
    lane = lax.broadcasted_iota(I32, (LANES, slots), 0) == (spot & 127)
    found = split3(jnp.where(live, evidence[...], 0.0))
    out = jnp.zeros(relay.shape, F32)
    for k in (2, 1, 0):
        out += dot(high, jnp.where(lane, found[k : k + 1].astype(F32), 0.0).astype(BF16), NT)
    relay[...] = out


def posterior(mass, peak, evidence, place, groups, count):
    rows, slots = mass.shape
    return pl.pallas_call(
        posterior_kernel,
        out_shape=[
            jax.ShapeDtypeStruct((rows, slots), BF16),
            jax.ShapeDtypeStruct((NY, count, LANES), F32),
            jax.ShapeDtypeStruct((NZ * NY * 8, LANES), F32),
        ],
        compiler_params=params(POST_VMEM),
        cost_estimate=cost(1e9, 5e6),
        name="posterior",
    )(mass, peak, evidence, place, groups)


def exponent(x):
    top = jnp.max(jnp.abs(x), axis=0, keepdims=True)
    return jnp.maximum(jnp.ceil(jnp.log2(jnp.maximum(top, 2.0**LOW_EXPONENT))), LOW_EXPONENT)


def to_int(x):
    return jnp.round(x).astype(I32)


def put(out, j, sums, relay, weights):
    rows = sums.shape[0]
    e = exponent(sums)
    out[j, :rows, :] = to_int(sums * jnp.exp2(14.0 - e)).astype(I16)
    row = lax.broadcasted_iota(I32, (8, LANES), 0)
    high = jnp.where(row == 0, e, 0.0).astype(I32)
    low = jnp.zeros_like(high)
    if relay is not None:
        f, g = exponent(relay), exponent(weights)
        up, down = jnp.exp2(14.0 - f), jnp.exp2(f - 14.0)
        part = jnp.round(relay * up)
        rest = to_int((relay - part * down) * up * 2.0**14)
        high = jnp.where(row < 2, jnp.where(row == 0, e, f), part).astype(I32)
        low = jnp.where(row < 2, jnp.where(row == 0, g, 0.0).astype(I32), rest)
        out[j, rows + TILE :, :] = to_int(weights * jnp.exp2(14.0 - g)).astype(I16)
    out[j, rows : rows + TILE, :] = jnp.concatenate([high, low], axis=0).astype(I16)


def number(x):
    return x.astype(I32).astype(F32)


def decode(block, rows):
    tail = number(block[rows : rows + TILE, :])
    high, low = tail[:8], tail[8:]
    sums = number(block[:rows, :]) * jnp.exp2(high[0:1] - 14.0)
    if block.shape[0] == rows + TILE:
        return sums, None, None
    down = jnp.exp2(high[1:2] - 14.0)
    row = lax.broadcasted_iota(I32, high.shape, 0)
    relay = jnp.where(row < 2, 0.0, (high + low * 2.0**-14) * down)
    return sums, relay, number(block[rows + TILE :, :]) * jnp.exp2(low[0:1] - 14.0)


def plus(a, b, keep=None):
    if keep is not None:
        b = [None if x is None else jnp.where(keep, x, 0.0) for x in b]
    return [None if x is None else x + w for x, w in zip(a, b)]


def terms(product, j, relay, weights):
    return [
        product[:, j * LANES : (j + 1) * LANES],
        None if relay is None else relay[0, j],
        None if weights is None else weights[j],
    ]


def ring_kernel(extra, ways, post, *refs):
    refs = list(refs)
    weighted = [refs.pop(0) for _ in range(ways)]
    relay = [refs.pop(0) for _ in range(ways)] if extra else [None] * ways
    weights = refs.pop(0) if extra else None
    outs = [refs.pop() for _ in range(ways)][::-1]
    came = refs + [None] * (ways - len(refs))
    rows = post.shape[0]
    for way in range(ways):
        product = dot(post[...], weighted[way][0])
        for j in range(2):
            mine = terms(product, j, relay[way], weights)
            if came[way] is not None:
                mine = plus(mine, decode(came[way][j], rows))
            put(outs[way], j, *mine)


def ring_step(places, stream, post, weighted, relay, weights, came):
    rows, slots = post.shape[0] // 2, post.shape[1]
    extra = stream == 0
    pair = 2
    tall = rows + TILE + (weights.shape[1] if extra else 0)
    specs, args = [pl.BlockSpec((rows, slots), lambda i: (stream, 0))], [post]
    for p in places:
        far, near = p // (NZ // 2), p % (NZ // 2)
        specs.append(pl.BlockSpec((1, slots, pair * LANES), lambda i, p=near: (p, 0, i)))
        args.append(weighted[far])
    if extra:
        specs += [pl.BlockSpec((1, pair, 8, LANES), lambda i, p=p: (p, i, 0, 0)) for p in places]
        specs.append(pl.BlockSpec((pair, weights.shape[1], LANES), lambda i: (i, 0, 0)))
        args += [relay] * len(places) + [weights]
    block = pl.BlockSpec((pair, tall, LANES), lambda i: (i, 0, 0))
    return pl.pallas_call(
        functools.partial(ring_kernel, extra, len(places)),
        grid=(NY // pair,),
        in_specs=specs + [block] * len(came),
        out_specs=[block] * len(places),
        out_shape=[jax.ShapeDtypeStruct((NY, tall, LANES), I16)] * len(places),
        compiler_params=params(RING_VMEM),
        cost_estimate=cost(2 * rows * slots * NY * LANES * len(places), 4e6),
        name="ring",
    )(*args, *came)


def last_kernel(post, weighted, relay, weights, *refs):
    came, out = [refs[:2], refs[2:4]], refs[4]
    rows = post.shape[0] // 2
    step = pl.program_id(0)
    mass = []
    for j in range(NY):
        value = weights[j]
        for c in came[0]:
            value += decode(c[j], rows)[2]
        mass.append(value)
    mass = jnp.concatenate(mass, axis=0)
    product = dot(post[...], weighted[0])
    for j in range(2):
        both = []
        for stream in range(2):
            part = product[stream * rows : stream * rows + rows]
            mine = terms(part, j, relay if stream == 0 else None, None)
            for c in came[stream]:
                got = decode(c[2 * step + j], rows)
                mine = plus(mine, [got[0], got[1], None])
            both.append(mine)
        put(out, j, jnp.concatenate([both[0][0], both[1][0]], axis=0), both[0][1], mass)


def ring_last(post, weighted, relay, weights, came):
    rows, slots = post.shape
    pair = 2
    tall = rows + TILE + NY * weights.shape[1]

    def whole(a):
        return pl.BlockSpec(a.shape, lambda i: (0,) * len(a.shape))

    came = came[0] + came[1]
    return pl.pallas_call(
        last_kernel,
        grid=(NY // pair,),
        in_specs=[
            whole(post),
            pl.BlockSpec((1, slots, pair * LANES), lambda i: (0, 0, i)),
            pl.BlockSpec((1, pair, 8, LANES), lambda i: (0, i, 0, 0)),
            whole(weights),
        ]
        + [whole(c) for c in came],
        out_specs=pl.BlockSpec((pair, tall, LANES), lambda i: (i, 0, 0)),
        out_shape=jax.ShapeDtypeStruct((NY, tall, LANES), I16),
        compiler_params=params(RING_VMEM),
        cost_estimate=cost(2 * rows * slots * NY * LANES, 4e6),
        name="last",
    )(post, weighted[0], relay, weights, *came)


def finish_kernel(panels, rows, own, a, b, c, sums, evidence, weights):
    total = decode(own[0], rows)
    for other in (a, b, c):
        total = plus(total, decode(other[...], rows))
    sums[...] = total[0].T[:, :panels]
    evidence[...] = total[1]
    weights[...] = total[2]


def finish(panels, rows, own, others):
    tall = own.shape[1]
    whole = pl.BlockSpec((tall, LANES), lambda i: (0, 0))
    shapes = [(LANES, panels), (8, LANES), (tall - rows - TILE, LANES)]
    return pl.pallas_call(
        functools.partial(finish_kernel, panels, rows),
        grid=(1,),
        in_specs=[pl.BlockSpec((1, tall, LANES), lambda i: (0, 0, 0))] + [whole] * 3,
        out_specs=[pl.BlockSpec(s, lambda i: (0, 0)) for s in shapes],
        out_shape=[jax.ShapeDtypeStruct(s, F32) for s in shapes],
        compiler_params=params(RING_VMEM),
        name="finish",
    )(own, *others)


def along_z(x, shift):
    pairs = [(y * NZ + z, y * NZ + (z + shift) % NZ) for y in range(NY) for z in range(NZ)]
    return lax.ppermute(x, "ptcl", pairs)


def along_y(x, shift):
    pairs = [(y * NZ + z, (y + shift) % NY * NZ + z) for y in range(NY) for z in range(NZ)]
    return lax.ppermute(x, "ptcl", pairs)


def across(x, mask, size):
    return lax.ppermute(x, "cls", [(i, i ^ mask) for i in range(size)])


def shards(images, target, ctf_group, ctf_table, noise_weight, references):
    panels = references.shape[0]
    count = ctf_table.shape[0]
    me = lax.axis_index("ptcl")
    y, z = me // NZ, me % NZ
    slots = images.shape[0]
    groups = ctf_group.reshape(1, slots)
    noise = noise_weight.reshape(1, -1)
    rel = jnp.arange(NZ * NY, dtype=I32)
    order = (y + rel % NY) % NY * NZ + (z + rel // NY) % NZ
    middle = NZ * NY // 2
    weighted, square = zip(
        *[weigh(o, groups, images, ctf_table, noise) for o in (order[:middle], order[middle:])]
    )

    rows = -(-panels // 32) * 32
    half = rows // 2
    near = [references] + [along_y(references, NY - j) for j in range(1, NY)]
    column = stack(near, half)
    common = (weighted, square, groups)
    jobs, carry = [(0, column)], None
    up = [along_z(c, 1) for c in column]
    down = [along_z(c, -1) for c in column]
    for step in range(1, NZ // 2):
        jobs += [(NZ - step, up), (step, down)]
        if step < NZ // 2 - 1:
            up, down = [along_z(c, 1) for c in up], [along_z(c, -1) for c in down]
        else:
            far = [along_z(up[0], 1), along_z(down[1], -1)]
        carry, jobs = score(jobs, *common, carry, False, panels), []
    mass, peak, evidence = score([(NZ // 2, far)], *common, carry, True, panels)

    size = lax.axis_size("cls")
    mask = 1
    while mask < size:
        other = across(evidence, mask, size)
        top = jnp.maximum(evidence, other)
        evidence = top + jnp.log(jnp.exp(evidence - top) + jnp.exp(other - top))
        mask *= 2

    share = 24 * NZ * NY
    shard = target // share
    shard_y, shard_z = shard // NZ, shard % NZ
    block = (shard_z - z + NZ) % NZ * NY + (shard_y - y + NY) % NY
    place = jnp.where(target >= 0, (block * 8 + 2) * LANES + target % share, -1)
    post, weights, relay = posterior(mass, peak, evidence, place.reshape(1, slots), groups, count)
    relay = relay.reshape(NZ, NY, 8, LANES)

    fixed = (post, weighted, relay, weights)
    far = NZ // 2
    came = [[along_z(ring_step([far], n, *fixed, [])[0], 1 - 2 * n)] for n in range(2)]
    for step in range(far - 1, 0, -1):
        for n in range(2):
            places = [step, NZ - step][:: 1 - 2 * n]
            blocks = ring_step(places, n, *fixed, came[n])
            came[n] = [along_z(x, d) for x, d in zip(blocks, (1 - 2 * n, 2 * n - 1))]
    own = ring_last(*fixed, came)
    others = [along_y(own[j], j) for j in range(1, NY)]
    class_sums, found, quarters = finish(panels, rows, own, others)
    log_evidence = found[2:].reshape(-1)
    quarters = quarters.reshape(NY, count, LANES)
    skip = NY * LANES - rows
    class_weights = jnp.concatenate(
        [quarters[j] for j in range(NY - 1)] + [quarters[NY - 1][:, skip:]], axis=1
    )[:, :panels]
    return class_sums, class_weights, log_evidence


def solution(mesh):
    placed = (P("ptcl", None), P("ptcl"), P("ptcl"), P(), P(), P("cls", "ptcl"))
    return jax.shard_map(
        shards,
        mesh=mesh,
        in_specs=placed,
        out_specs=(P("ptcl", "cls"), P(None, "cls"), P("ptcl")),
        check_vma=False,
    )
```

```python
import functools

import jax
import jax.numpy as jnp
from jax import lax
from jax.experimental import pallas as pl
from jax.experimental.pallas import tpu as pltpu
from jax.sharding import PartitionSpec as P

NY, NZ = 4, 8
LANES = 128
TILE = 16
F32, BF16, I16, I32 = jnp.float32, jnp.bfloat16, jnp.int16, jnp.int32
NT = (((1,), (1,)), ((), ()))
TN = (((0,), (0,)), ((), ()))
WEIGH_VMEM, SCORE_VMEM, POST_VMEM, RING_VMEM = 44, 12, 16, 8
WEIGHT = 100
LOW_EXPONENT = -100.0


def dot(a, b, dims=(((1,), (0,)), ((), ()))):
    return lax.dot_general(a, b, dims, preferred_element_type=F32)


def split3(x):
    hi = x.astype(BF16)
    rest = x - hi.astype(F32)
    mid = rest.astype(BF16)
    low = (rest - mid.astype(F32)).astype(BF16)
    return jnp.concatenate([hi.astype(F32), mid.astype(F32), low.astype(F32)], axis=0).astype(BF16)


def onehot3(groups, count):
    row = lax.broadcasted_iota(I32, (3 * count, groups.shape[1]), 0)
    row = jnp.where(row >= 2 * count, row - 2 * count, jnp.where(row >= count, row - count, row))
    return (row == groups).astype(F32).astype(BF16)


def params(size):
    return pltpu.CompilerParams(vmem_limit_bytes=size * 1024 * 1024)


def cost(flops, byte_count):
    return pl.CostEstimate(flops=int(flops), bytes_accessed=int(byte_count), transcendentals=0)


def weight_kernel(order, groups, *refs):
    images, tables, noises = refs[:NY], refs[NY : 2 * NY], refs[2 * NY : 3 * NY]
    weighted, square = refs[3 * NY :]
    count = tables[0].shape[0]
    slots = images[0].shape[0]
    table = jnp.concatenate([t[...] for t in tables], axis=1)
    noise = jnp.concatenate([n[...] for n in noises], axis=1)
    square[0] = split3(table * table * noise)
    pieces = split3(table)
    member = onehot3(groups[...], count)
    step = 256
    for begin in range(0, slots, step):
        rows = dot(member[:, begin : begin + step], pieces, TN)
        picture = jnp.concatenate([i[begin : begin + step, :] for i in images], axis=1)
        weighted[0, begin : begin + step, :] = (picture.astype(F32) * rows * noise).astype(BF16)


def weigh(order, groups, images, table, noise):
    slots, count = images.shape[0], table.shape[0]
    wide = NY * LANES

    def block(j):
        return lambda i, o: (0, o[i * NY + j])

    specs = [pl.BlockSpec((1, slots), lambda i, o: (0, 0))]
    for rows in (slots, count, 1):
        specs += [pl.BlockSpec((rows, LANES), block(j)) for j in range(NY)]
    return pl.pallas_call(
        weight_kernel,
        grid_spec=pltpu.PrefetchScalarGridSpec(
            num_scalar_prefetch=1,
            grid=(NZ // 2,),
            in_specs=specs,
            out_specs=[
                pl.BlockSpec((1, slots, wide), lambda i, o: (i, 0, 0)),
                pl.BlockSpec((1, 3 * count, wide), lambda i, o: (i, 0, 0)),
            ],
        ),
        out_shape=[
            jax.ShapeDtypeStruct((NZ // 2, slots, wide), BF16),
            jax.ShapeDtypeStruct((NZ // 2, 3 * count, wide), BF16),
        ],
        compiler_params=params(WEIGH_VMEM),
        cost_estimate=cost(3e9 * WEIGHT, 2 * images.size),
        name="weigh",
    )(order, groups, *[images] * NY, *[table] * NY, *[noise] * NY)


def stack_kernel(*refs):
    blocks, (top, bottom) = refs[:NY], refs[NY:]
    half = top.shape[1]
    rest = blocks[0].shape[0] - half
    for j, block in enumerate(blocks):
        top[j] = block[:half, :]
        bottom[j, half - TILE :, :] = jnp.zeros((TILE, LANES), BF16)
        bottom[j, :rest, :] = block[half:, :]


def stack(blocks, half):
    return pl.pallas_call(
        stack_kernel,
        out_shape=[jax.ShapeDtypeStruct((NY, half, LANES), BF16)] * 2,
        compiler_params=params(RING_VMEM),
        name="stack",
    )(*blocks)


def in_vmem(count):
    return [pl.BlockSpec(memory_space=pltpu.VMEM)] * count


def score_kernel(jobs, first, last, panels, *refs):
    refs = list(refs)
    chunks = [[refs.pop(0) for _ in range(n)] for _, n in jobs]
    wa, wb, sa, sb, groups = [refs.pop(0) for _ in range(5)]
    total_in, energy_in = (None, None) if first else [refs.pop(0) for _ in range(2)]
    panel, right, square = [], [], []
    for (place, _), chunk in zip(jobs, chunks):
        parts = [jnp.concatenate([c[j] for j in range(NY)], axis=1) for c in chunk]
        panel.append(jnp.concatenate(parts, axis=0))
        far, near = place // (NZ // 2), place % (NZ // 2)
        right.append(((wa, wb)[far], near))
        square.append((sa, sb)[far][near])
    panel = jnp.concatenate(panel, axis=1)
    square = jnp.concatenate(square, axis=1)
    wide = panel.astype(F32)
    wide = wide * wide
    hi = wide.astype(BF16)
    low = (wide - hi.astype(F32)).astype(BF16)
    energy = dot(hi, square, NT) + dot(low, square, NT)
    if not first:
        energy += energy_in[...]
    if last:
        mass, peak, evidence = refs
        hi = energy.astype(BF16)
        rest = energy - hi.astype(F32)
        mid = rest.astype(BF16)
        low = (rest - mid.astype(F32)).astype(BF16)
    else:
        total, refs[1][...] = refs[0], energy
    slots = groups.shape[1]
    step = 256
    for begin in range(0, slots, step):
        here = slice(begin, begin + step)
        value = dot(panel, jnp.concatenate([w[k, here, :] for w, k in right], axis=1), NT)
        if not first:
            value += total_in[:, here]
        if not last:
            total[:, here] = value
            continue
        member = onehot3(groups[:, here], energy.shape[1] // 3)
        value -= 0.5 * (dot(hi, member) + dot(mid, member) + dot(low, member))
        row = lax.broadcasted_iota(I32, value.shape, 0)
        value = jnp.where(row < panels, value, -jnp.inf)
        top = jnp.max(value, axis=0, keepdims=True)
        value = jnp.exp(value - top)
        mass[:, here] = value
        peak[:, here] = top
        evidence[:, here] = top + jnp.log(jnp.sum(value, axis=0, keepdims=True))


def score(jobs, weighted, square, groups, carry, last, panels):
    rows = sum(a.shape[1] for a in jobs[0][1])
    slots = groups.shape[1]
    count3 = square[0].shape[1]
    if all(place < NZ // 2 for place, _ in jobs):
        weighted, square = weighted[:1] * 2, square[:1] * 2
    outs = [jax.ShapeDtypeStruct((rows, slots), F32)]
    if last:
        outs += [jax.ShapeDtypeStruct((1, slots), F32)] * 2
    else:
        outs += [jax.ShapeDtypeStruct((rows, count3), F32)]
    args = [a for job in jobs for a in job[1]] + [*weighted, *square, groups]
    args += [] if carry is None else list(carry)
    work = 2.5 * rows * slots * NY * LANES * len(jobs)
    return pl.pallas_call(
        functools.partial(
            score_kernel, [(j[0], len(j[1])) for j in jobs], carry is None, last, panels
        ),
        in_specs=in_vmem(len(args)),
        out_specs=in_vmem(len(outs)),
        out_shape=outs,
        compiler_params=params(SCORE_VMEM),
        cost_estimate=cost(work * WEIGHT, 4e6 * len(jobs)),
        name="score",
    )(*args)


def posterior_kernel(mass, peak, evidence, place, groups, post, weights, relay):
    live = place[...] >= 0
    scale = jnp.where(live, jnp.exp(peak[...] - evidence[...]), 0.0)
    value = (mass[...] * scale).astype(BF16)
    post[...] = value
    count = weights.shape[1]
    slots = groups.shape[1]
    member = (lax.broadcasted_iota(I32, (count, slots), 0) == groups[...]).astype(F32).astype(BF16)
    for j in range(NY):
        begin = min(j * LANES, value.shape[0] - LANES)
        weights[j] = dot(member, value[begin : begin + LANES], NT)
    spot = place[...]
    line = lax.shift_right_arithmetic(spot, 7)
    high = (lax.broadcasted_iota(I32, (relay.shape[0], slots), 0) == line).astype(F32).astype(BF16)
    lane = lax.broadcasted_iota(I32, (LANES, slots), 0) == (spot & 127)
    found = split3(jnp.where(live, evidence[...], 0.0))
    out = jnp.zeros(relay.shape, F32)
    for k in (2, 1, 0):
        out += dot(high, jnp.where(lane, found[k : k + 1].astype(F32), 0.0).astype(BF16), NT)
    relay[...] = out


def posterior(mass, peak, evidence, place, groups, count):
    rows, slots = mass.shape
    return pl.pallas_call(
        posterior_kernel,
        out_shape=[
            jax.ShapeDtypeStruct((rows, slots), BF16),
            jax.ShapeDtypeStruct((NY, count, LANES), F32),
            jax.ShapeDtypeStruct((NZ * NY * 8, LANES), F32),
        ],
        compiler_params=params(POST_VMEM),
        cost_estimate=cost(1e9, 5e6),
        name="posterior",
    )(mass, peak, evidence, place, groups)


def exponent(x):
    top = jnp.max(jnp.abs(x), axis=0, keepdims=True)
    return jnp.maximum(jnp.ceil(jnp.log2(jnp.maximum(top, 2.0**LOW_EXPONENT))), LOW_EXPONENT)


def to_int(x):
    return jnp.round(x).astype(I32)


def put(out, j, sums, relay, weights):
    rows = sums.shape[0]
    e = exponent(sums)
    main = to_int(sums * jnp.exp2(14.0 - e))
    if relay is None:
        last = lax.broadcasted_iota(I32, sums.shape, 0) == rows - 1
        out[j] = jnp.where(last, e.astype(I32), main).astype(I16)
        return
    out[j, :rows, :] = main.astype(I16)
    row = lax.broadcasted_iota(I32, (8, LANES), 0)
    f, g = exponent(relay), exponent(weights)
    up, down = jnp.exp2(14.0 - f), jnp.exp2(f - 14.0)
    part = jnp.round(relay * up)
    rest = to_int((relay - part * down) * up * 2.0**14)
    high = jnp.where(row < 2, jnp.where(row == 0, e, f), part).astype(I32)
    low = jnp.where(row < 2, jnp.where(row == 0, g, 0.0).astype(I32), rest)
    out[j, rows + TILE :, :] = to_int(weights * jnp.exp2(14.0 - g)).astype(I16)
    out[j, rows : rows + TILE, :] = jnp.concatenate([high, low], axis=0).astype(I16)


def number(x):
    return x.astype(I32).astype(F32)


def decode(block, rows):
    if block.shape[0] == rows:
        last = lax.broadcasted_iota(I32, block.shape, 0) == rows - 1
        e = number(block[rows - TILE :, :])[TILE - 1 : TILE]
        return jnp.where(last, 0.0, number(block) * jnp.exp2(e - 14.0)), None, None
    tail = number(block[rows : rows + TILE, :])
    high, low = tail[:8], tail[8:]
    sums = number(block[:rows, :]) * jnp.exp2(high[0:1] - 14.0)
    down = jnp.exp2(high[1:2] - 14.0)
    row = lax.broadcasted_iota(I32, high.shape, 0)
    relay = jnp.where(row < 2, 0.0, (high + low * 2.0**-14) * down)
    return sums, relay, number(block[rows + TILE :, :]) * jnp.exp2(low[0:1] - 14.0)


def plus(a, b):
    return [None if x is None else x + w for x, w in zip(a, b)]


def products(post, weighted, place):
    for begin in range(0, NY, 2):
        right = weighted[place % (NZ // 2), :, begin * LANES : (begin + 2) * LANES]
        product = dot(post, right)
        yield begin, product[:, :LANES]
        yield begin + 1, product[:, LANES:]


def ring_kernel(stream, places, post, *refs):
    refs = list(refs)
    ways = len(places)
    weighted = [refs.pop(0) for _ in range(ways)]
    relay, weights = [refs.pop(0) for _ in range(2)] if stream == 0 else (None, None)
    outs = [refs.pop() for _ in range(ways)][::-1]
    came = refs + [None] * (ways - len(refs))
    rows = post.shape[0] // 2
    left = post[stream * rows : (stream + 1) * rows, :]
    for way, place in enumerate(places):
        for j, sums in products(left, weighted[way], place):
            mine = [sums, None, None]
            if stream == 0:
                mine = [sums, relay[place, j], weights[j]]
            if came[way] is not None:
                mine = plus(mine, decode(came[way][j], rows))
            put(outs[way], j, *mine)


def ring_step(places, stream, post, weighted, relay, weights, came):
    rows, slots = post.shape[0] // 2, post.shape[1]
    tall = rows if stream else rows + TILE + weights.shape[1]
    args = [post] + [weighted[p // (NZ // 2)] for p in places]
    args += [] if stream else [relay, weights]
    args += came
    return pl.pallas_call(
        functools.partial(ring_kernel, stream, places),
        in_specs=in_vmem(len(args)),
        out_specs=in_vmem(len(places)),
        out_shape=[jax.ShapeDtypeStruct((NY, tall, LANES), I16)] * len(places),
        compiler_params=params(RING_VMEM),
        cost_estimate=cost(2 * rows * slots * NY * LANES * len(places), 4e6),
        name="ring",
    )(*args)


def last_kernel(post, weighted, relay, weights, *refs):
    came, out = [refs[:2], refs[2:4]], refs[4]
    rows = post.shape[0] // 2
    got = [[[decode(c[j], rows) for c in pair] for j in range(NY)] for pair in came]
    mass = [weights[j] + got[0][j][0][2] + got[0][j][1][2] for j in range(NY)]
    mass = jnp.concatenate(mass, axis=0)
    for j, sums in products(post[...], weighted, 0):
        both = [
            sums[n * rows : (n + 1) * rows] + got[n][j][0][0] + got[n][j][1][0] for n in range(2)
        ]
        extra = relay[0, j] + got[0][j][0][1] + got[0][j][1][1]
        put(out, j, jnp.concatenate(both, axis=0), extra, mass)


def ring_last(post, weighted, relay, weights, came):
    rows, slots = post.shape
    tall = rows + TILE + NY * weights.shape[1]
    args = [post, weighted[0], relay, weights, *came[0], *came[1]]
    return pl.pallas_call(
        last_kernel,
        in_specs=in_vmem(len(args)),
        out_specs=pl.BlockSpec(memory_space=pltpu.VMEM),
        out_shape=jax.ShapeDtypeStruct((NY, tall, LANES), I16),
        compiler_params=params(RING_VMEM),
        cost_estimate=cost(2 * rows * slots * NY * LANES, 4e6),
        name="last",
    )(*args)


def finish_kernel(panels, rows, own, a, b, c, sums, evidence, weights):
    total = decode(own[0], rows)
    for other in (a, b, c):
        total = plus(total, decode(other[...], rows))
    sums[...] = total[0].T[:, :panels]
    evidence[...] = total[1]
    weights[...] = total[2]


def finish(panels, rows, own, others):
    tall = own.shape[1]
    whole = pl.BlockSpec((tall, LANES), lambda i: (0, 0))
    shapes = [(LANES, panels), (8, LANES), (tall - rows - TILE, LANES)]
    return pl.pallas_call(
        functools.partial(finish_kernel, panels, rows),
        grid=(1,),
        in_specs=[pl.BlockSpec((1, tall, LANES), lambda i: (0, 0, 0))] + [whole] * 3,
        out_specs=[pl.BlockSpec(s, lambda i: (0, 0)) for s in shapes],
        out_shape=[jax.ShapeDtypeStruct(s, F32) for s in shapes],
        compiler_params=params(RING_VMEM),
        name="finish",
    )(own, *others)


def along_z(x, shift):
    pairs = [(y * NZ + z, y * NZ + (z + shift) % NZ) for y in range(NY) for z in range(NZ)]
    return lax.ppermute(x, "ptcl", pairs)


def along_y(x, shift):
    pairs = [(y * NZ + z, (y + shift) % NY * NZ + z) for y in range(NY) for z in range(NZ)]
    return lax.ppermute(x, "ptcl", pairs)


def across(x, mask, size):
    return lax.ppermute(x, "cls", [(i, i ^ mask) for i in range(size)])


def shards(images, target, ctf_group, ctf_table, noise_weight, references):
    panels = references.shape[0]
    count = ctf_table.shape[0]
    me = lax.axis_index("ptcl")
    y, z = me // NZ, me % NZ
    slots = images.shape[0]
    groups = ctf_group.reshape(1, slots)
    noise = noise_weight.reshape(1, -1)
    rel = jnp.arange(NZ * NY, dtype=I32)
    order = (y + rel % NY) % NY * NZ + (z + rel // NY) % NZ
    middle = NZ * NY // 2
    weighted, square = zip(
        *[weigh(o, groups, images, ctf_table, noise) for o in (order[:middle], order[middle:])]
    )

    rows = -(-panels // 32) * 32
    half = rows // 2
    near = [references] + [along_y(references, NY - j) for j in range(1, NY)]
    column = stack(near, half)
    common = (weighted, square, groups)
    jobs, carry = [(0, column)], None
    up = [along_z(c, 1) for c in column]
    down = [along_z(c, -1) for c in column]
    for step in range(1, NZ // 2):
        jobs += [(NZ - step, up), (step, down)]
        if step < NZ // 2 - 1:
            up, down = [along_z(c, 1) for c in up], [along_z(c, -1) for c in down]
        else:
            far = [along_z(up[0], 1), along_z(down[1], -1)]
        carry, jobs = score(jobs, *common, carry, False, panels), []
    mass, peak, evidence = score([(NZ // 2, far)], *common, carry, True, panels)

    size = lax.axis_size("cls")
    mask = 1
    while mask < size:
        other = across(evidence, mask, size)
        top = jnp.maximum(evidence, other)
        evidence = top + jnp.log(jnp.exp(evidence - top) + jnp.exp(other - top))
        mask *= 2

    share = 24 * NZ * NY
    shard = target // share
    shard_y, shard_z = shard // NZ, shard % NZ
    block = (shard_z - z + NZ) % NZ * NY + (shard_y - y + NY) % NY
    place = jnp.where(target >= 0, (block * 8 + 2) * LANES + target % share, -1)
    post, weights, relay = posterior(mass, peak, evidence, place.reshape(1, slots), groups, count)
    relay = relay.reshape(NZ, NY, 8, LANES)

    fixed = (post, weighted, relay, weights)
    far = NZ // 2
    came = [[along_z(ring_step([far], n, *fixed, [])[0], 1 - 2 * n)] for n in range(2)]
    for step in range(far - 1, 0, -1):
        for n in range(2):
            places = [step, NZ - step][:: 1 - 2 * n]
            blocks = ring_step(places, n, *fixed, came[n])
            came[n] = [along_z(x, d) for x, d in zip(blocks, (1 - 2 * n, 2 * n - 1))]
    own = ring_last(*fixed, came)
    others = [along_y(own[j], j) for j in range(1, NY)]
    class_sums, found, quarters = finish(panels, rows, own, others)
    log_evidence = found[2:].reshape(-1)
    quarters = quarters.reshape(NY, count, LANES)
    skip = NY * LANES - rows
    class_weights = jnp.concatenate(
        [quarters[j] for j in range(NY - 1)] + [quarters[NY - 1][:, skip:]], axis=1
    )[:, :panels]
    return class_sums, class_weights, log_evidence


def solution(mesh):
    placed = (P("ptcl", None), P("ptcl"), P("ptcl"), P(), P(), P("cls", "ptcl"))
    return jax.shard_map(
        shards,
        mesh=mesh,
        in_specs=placed,
        out_specs=(P("ptcl", "cls"), P(None, "cls"), P("ptcl")),
        check_vma=False,
    )
```

```python
import functools

import jax
import jax.numpy as jnp
from jax import lax
from jax.experimental import pallas as pl
from jax.experimental.pallas import tpu as pltpu
from jax.sharding import PartitionSpec as P

NY, NZ = 4, 8
LANES = 128
TILE = 16
F32, BF16, I16, I32 = jnp.float32, jnp.bfloat16, jnp.int16, jnp.int32
NT = (((1,), (1,)), ((), ()))
TN = (((0,), (0,)), ((), ()))
WEIGH_VMEM, SCORE_VMEM, POST_VMEM, RING_VMEM = 44, 12, 16, 8
WEIGHT = 100
LOW_EXPONENT = -100.0


def dot(a, b, dims=(((1,), (0,)), ((), ()))):
    return lax.dot_general(a, b, dims, preferred_element_type=F32)


def split3(x):
    hi = x.astype(BF16)
    rest = x - hi.astype(F32)
    mid = rest.astype(BF16)
    low = (rest - mid.astype(F32)).astype(BF16)
    return jnp.concatenate([hi.astype(F32), mid.astype(F32), low.astype(F32)], axis=0).astype(BF16)


def onehot3(groups, count):
    row = lax.broadcasted_iota(I32, (3 * count, groups.shape[1]), 0)
    row = jnp.where(row >= 2 * count, row - 2 * count, jnp.where(row >= count, row - count, row))
    return (row == groups).astype(F32).astype(BF16)


def params(size):
    return pltpu.CompilerParams(vmem_limit_bytes=size * 1024 * 1024)


def cost(flops, byte_count):
    return pl.CostEstimate(flops=int(flops), bytes_accessed=int(byte_count), transcendentals=0)


def weight_kernel(order, groups, *refs):
    images, tables, noises = refs[:NY], refs[NY : 2 * NY], refs[2 * NY : 3 * NY]
    weighted, square = refs[3 * NY :]
    count = tables[0].shape[0]
    slots = images[0].shape[0]
    table = jnp.concatenate([t[...] for t in tables], axis=1)
    noise = jnp.concatenate([n[...] for n in noises], axis=1)
    square[0] = split3(table * table * noise)
    pieces = split3(table * noise)
    member = onehot3(groups[...], count)
    step = 256
    for begin in range(0, slots, step):
        rows = dot(member[:, begin : begin + step], pieces, TN)
        picture = jnp.concatenate([i[begin : begin + step, :] for i in images], axis=1)
        weighted[0, begin : begin + step, :] = (picture.astype(F32) * rows).astype(BF16)


def weigh(order, groups, images, table, noise):
    slots, count = images.shape[0], table.shape[0]
    wide = NY * LANES

    def block(j):
        return lambda i, o: (0, o[i * NY + j])

    specs = [pl.BlockSpec((1, slots), lambda i, o: (0, 0))]
    for rows in (slots, count, 1):
        specs += [pl.BlockSpec((rows, LANES), block(j)) for j in range(NY)]
    return pl.pallas_call(
        weight_kernel,
        grid_spec=pltpu.PrefetchScalarGridSpec(
            num_scalar_prefetch=1,
            grid=(NZ // 2,),
            in_specs=specs,
            out_specs=[
                pl.BlockSpec((1, slots, wide), lambda i, o: (i, 0, 0)),
                pl.BlockSpec((1, 3 * count, wide), lambda i, o: (i, 0, 0)),
            ],
        ),
        out_shape=[
            jax.ShapeDtypeStruct((NZ // 2, slots, wide), BF16),
            jax.ShapeDtypeStruct((NZ // 2, 3 * count, wide), BF16),
        ],
        compiler_params=params(WEIGH_VMEM),
        cost_estimate=cost(3e9 * WEIGHT, 2 * images.size),
        name="weigh",
    )(order, groups, *[images] * NY, *[table] * NY, *[noise] * NY)


def stack_kernel(*refs):
    blocks, (top, bottom) = refs[:NY], refs[NY:]
    half = top.shape[1]
    rest = blocks[0].shape[0] - half
    for j, block in enumerate(blocks):
        top[j] = block[:half, :]
        bottom[j, half - TILE :, :] = jnp.zeros((TILE, LANES), BF16)
        bottom[j, :rest, :] = block[half:, :]


def stack(blocks, half):
    return pl.pallas_call(
        stack_kernel,
        out_shape=[jax.ShapeDtypeStruct((NY, half, LANES), BF16)] * 2,
        compiler_params=params(RING_VMEM),
        name="stack",
    )(*blocks)


def in_vmem(count):
    return [pl.BlockSpec(memory_space=pltpu.VMEM)] * count


def score_kernel(jobs, first, last, panels, *refs):
    refs = list(refs)
    chunks = [[refs.pop(0) for _ in range(n)] for _, n in jobs]
    wa, wb, sa, sb, groups = [refs.pop(0) for _ in range(5)]
    total_in, energy_in = (None, None) if first else [refs.pop(0) for _ in range(2)]
    panel, right, square = [], [], []
    for (place, _), chunk in zip(jobs, chunks):
        parts = [jnp.concatenate([c[j] for j in range(NY)], axis=1) for c in chunk]
        panel.append(jnp.concatenate(parts, axis=0))
        far, near = place // (NZ // 2), place % (NZ // 2)
        right.append(((wa, wb)[far], near))
        square.append((sa, sb)[far][near])
    panel = jnp.concatenate(panel, axis=1)
    square = jnp.concatenate(square, axis=1)
    wide = panel.astype(F32)
    wide = wide * wide
    hi = wide.astype(BF16)
    low = (wide - hi.astype(F32)).astype(BF16)
    energy = dot(hi, square, NT) + dot(low, square, NT)
    if not first:
        energy += energy_in[...]
    if last:
        mass, peak, evidence = refs
        hi = energy.astype(BF16)
        rest = energy - hi.astype(F32)
        mid = rest.astype(BF16)
        low = (rest - mid.astype(F32)).astype(BF16)
    else:
        total, refs[1][...] = refs[0], energy
    slots = groups.shape[1]
    step = 256
    for begin in range(0, slots, step):
        here = slice(begin, begin + step)
        value = dot(panel, jnp.concatenate([w[k, here, :] for w, k in right], axis=1), NT)
        if not first:
            value += total_in[:, here]
        if not last:
            total[:, here] = value
            continue
        member = onehot3(groups[:, here], energy.shape[1] // 3)
        value -= 0.5 * (dot(hi, member) + dot(mid, member) + dot(low, member))
        row = lax.broadcasted_iota(I32, value.shape, 0)
        value = jnp.where(row < panels, value, -jnp.inf)
        top = jnp.max(value, axis=0, keepdims=True)
        value = jnp.exp(value - top)
        mass[:, here] = value
        peak[:, here] = top
        found = top + jnp.log(jnp.sum(value, axis=0, keepdims=True))
        for k in range(evidence.shape[0]):
            evidence[k, :, here] = found


def score(jobs, weighted, square, groups, carry, last, panels):
    rows = sum(a.shape[1] for a in jobs[0][1])
    slots = groups.shape[1]
    count3 = square[0].shape[1]
    if all(place < NZ // 2 for place, _ in jobs):
        weighted, square = weighted[:1] * 2, square[:1] * 2
    outs = [jax.ShapeDtypeStruct((rows, slots), F32)]
    if last:
        outs.append(jax.ShapeDtypeStruct((1, slots), F32))
        outs.append(jax.ShapeDtypeStruct((last, 1, slots), F32))
    else:
        outs += [jax.ShapeDtypeStruct((rows, count3), F32)]
    args = [a for job in jobs for a in job[1]] + [*weighted, *square, groups]
    args += [] if carry is None else list(carry)
    work = 2.5 * rows * slots * NY * LANES * len(jobs)
    return pl.pallas_call(
        functools.partial(
            score_kernel, [(j[0], len(j[1])) for j in jobs], carry is None, last, panels
        ),
        in_specs=in_vmem(len(args)),
        out_specs=in_vmem(len(outs)),
        out_shape=outs,
        compiler_params=params(SCORE_VMEM),
        cost_estimate=cost(work * WEIGHT, 4e6 * len(jobs)),
        name="score",
    )(*args)


def posterior_kernel(mass, peak, evidence, place, groups, post, weights, relay):
    live = place[...] >= 0
    each = [evidence[k] for k in range(evidence.shape[0])]
    top = functools.reduce(jnp.maximum, each)
    norm = top + jnp.log(sum(jnp.exp(e - top) for e in each))
    scale = jnp.where(live, jnp.exp(peak[...] - norm), 0.0)
    value = (mass[...] * scale).astype(BF16)
    post[...] = value
    count = weights.shape[1]
    slots = groups.shape[1]
    member = (lax.broadcasted_iota(I32, (count, slots), 0) == groups[...]).astype(F32).astype(BF16)
    filled = [value, jnp.zeros((NY * LANES - value.shape[0], slots), BF16)]
    filled = jnp.concatenate(filled, axis=0)
    for j in range(NY):
        weights[j] = dot(member, filled[j * LANES : (j + 1) * LANES], NT)
    spot = place[...]
    line = lax.shift_right_arithmetic(spot, 7)
    high = (lax.broadcasted_iota(I32, (relay.shape[0], slots), 0) == line).astype(F32).astype(BF16)
    lane = lax.broadcasted_iota(I32, (LANES, slots), 0) == (spot & 127)
    found = split3(jnp.where(live, norm, 0.0))
    out = jnp.zeros(relay.shape, F32)
    for k in (2, 1, 0):
        out += dot(high, jnp.where(lane, found[k : k + 1].astype(F32), 0.0).astype(BF16), NT)
    relay[...] = out


def posterior(mass, peak, evidence, place, groups, count):
    rows, slots = mass.shape
    return pl.pallas_call(
        posterior_kernel,
        out_shape=[
            jax.ShapeDtypeStruct((rows, slots), BF16),
            jax.ShapeDtypeStruct((NY, count, LANES), F32),
            jax.ShapeDtypeStruct((NZ * NY * 8, LANES), F32),
        ],
        compiler_params=params(POST_VMEM),
        cost_estimate=cost(1e9, 5e6),
        name="posterior",
    )(mass, peak, evidence, place, groups)


def exponent(x):
    top = jnp.max(jnp.abs(x), axis=0, keepdims=True)
    return jnp.maximum(jnp.ceil(jnp.log2(jnp.maximum(top, 2.0**LOW_EXPONENT))), LOW_EXPONENT)


def to_int(x):
    return jnp.round(x).astype(I32)


def put(out, j, sums, relay, weights):
    rows = sums.shape[0]
    e = exponent(sums)
    main = to_int(sums * jnp.exp2(14.0 - e))
    if relay is None:
        last = lax.broadcasted_iota(I32, sums.shape, 0) == rows - 1
        out[j] = jnp.where(last, e.astype(I32), main).astype(I16)
        return
    out[j, :rows, :] = main.astype(I16)
    row = lax.broadcasted_iota(I32, (8, LANES), 0)
    f, g = exponent(relay), exponent(weights)
    up, down = jnp.exp2(14.0 - f), jnp.exp2(f - 14.0)
    part = jnp.round(relay * up)
    rest = to_int((relay - part * down) * up * 2.0**14)
    high = jnp.where(row < 2, jnp.where(row == 0, e, f), part).astype(I32)
    low = jnp.where(row < 2, jnp.where(row == 0, g, 0.0).astype(I32), rest)
    out[j, rows + TILE :, :] = to_int(weights * jnp.exp2(14.0 - g)).astype(I16)
    out[j, rows : rows + TILE, :] = jnp.concatenate([high, low], axis=0).astype(I16)


def number(x):
    return x.astype(I32).astype(F32)


def decode(block, rows):
    if block.shape[0] == rows:
        last = lax.broadcasted_iota(I32, block.shape, 0) == rows - 1
        e = number(block[rows - TILE :, :])[TILE - 1 : TILE]
        return jnp.where(last, 0.0, number(block) * jnp.exp2(e - 14.0)), None, None
    tail = number(block[rows : rows + TILE, :])
    high, low = tail[:8], tail[8:]
    sums = number(block[:rows, :]) * jnp.exp2(high[0:1] - 14.0)
    down = jnp.exp2(high[1:2] - 14.0)
    row = lax.broadcasted_iota(I32, high.shape, 0)
    relay = jnp.where(row < 2, 0.0, (high + low * 2.0**-14) * down)
    return sums, relay, number(block[rows + TILE :, :]) * jnp.exp2(low[0:1] - 14.0)


def plus(a, b):
    return [None if x is None else x + w for x, w in zip(a, b)]


def products(post, weighted, place):
    for begin in range(0, NY, 2):
        right = weighted[place % (NZ // 2), :, begin * LANES : (begin + 2) * LANES]
        product = dot(post, right)
        yield begin, product[:, :LANES]
        yield begin + 1, product[:, LANES:]


def ring_kernel(stream, places, post, *refs):
    refs = list(refs)
    ways = len(places)
    weighted = [refs.pop(0) for _ in range(ways)]
    relay, weights = [refs.pop(0) for _ in range(2)] if stream == 0 else (None, None)
    outs = [refs.pop() for _ in range(ways)][::-1]
    came = refs + [None] * (ways - len(refs))
    rows = post.shape[0] // 2
    left = post[stream * rows : (stream + 1) * rows, :]
    for way, place in enumerate(places):
        for j, sums in products(left, weighted[way], place):
            mine = [sums, None, None]
            if stream == 0:
                mine = [sums, relay[place, j], weights[j]]
            if came[way] is not None:
                mine = plus(mine, decode(came[way][j], rows))
            put(outs[way], j, *mine)


def ring_step(places, stream, post, weighted, relay, weights, came):
    rows, slots = post.shape[0] // 2, post.shape[1]
    tall = rows if stream else rows + TILE + weights.shape[1]
    args = [post] + [weighted[p // (NZ // 2)] for p in places]
    args += [] if stream else [relay, weights]
    args += came
    return pl.pallas_call(
        functools.partial(ring_kernel, stream, places),
        in_specs=in_vmem(len(args)),
        out_specs=in_vmem(len(places)),
        out_shape=[jax.ShapeDtypeStruct((NY, tall, LANES), I16)] * len(places),
        compiler_params=params(RING_VMEM),
        cost_estimate=cost(2 * rows * slots * NY * LANES * len(places), 4e6),
        name="ring",
    )(*args)


def last_kernel(post, weighted, relay, weights, *refs):
    came, out = [refs[:2], refs[2:4]], refs[4]
    rows = post.shape[0] // 2
    got = [[[decode(c[j], rows) for c in pair] for j in range(NY)] for pair in came]
    mass = [weights[j] + got[0][j][0][2] + got[0][j][1][2] for j in range(NY)]
    mass = jnp.concatenate(mass, axis=0)
    for j, sums in products(post[...], weighted, 0):
        both = [
            sums[n * rows : (n + 1) * rows] + got[n][j][0][0] + got[n][j][1][0] for n in range(2)
        ]
        extra = relay[0, j] + got[0][j][0][1] + got[0][j][1][1]
        put(out, j, jnp.concatenate(both, axis=0), extra, mass)


def ring_last(post, weighted, relay, weights, came):
    rows, slots = post.shape
    tall = rows + TILE + NY * weights.shape[1]
    args = [post, weighted[0], relay, weights, *came[0], *came[1]]
    return pl.pallas_call(
        last_kernel,
        in_specs=in_vmem(len(args)),
        out_specs=pl.BlockSpec(memory_space=pltpu.VMEM),
        out_shape=jax.ShapeDtypeStruct((NY, tall, LANES), I16),
        compiler_params=params(RING_VMEM),
        cost_estimate=cost(2 * rows * slots * NY * LANES, 4e6),
        name="last",
    )(*args)


def finish_kernel(panels, rows, own, a, b, c, sums, evidence, weights):
    total = decode(own[0], rows)
    for other in (a, b, c):
        total = plus(total, decode(other[...], rows))
    sums[...] = total[0].T[:, :panels]
    evidence[...] = total[1]
    count = weights.shape[0]
    for j in range(NY):
        begin, end = j * LANES, min((j + 1) * LANES, panels)
        weights[:, begin:end] = total[2][j * count : (j + 1) * count, : end - begin]


def finish(panels, rows, own, others):
    tall = own.shape[1]
    whole = pl.BlockSpec((tall, LANES), lambda i: (0, 0))
    shapes = [(LANES, panels), (8, LANES), ((tall - rows - TILE) // NY, panels)]
    return pl.pallas_call(
        functools.partial(finish_kernel, panels, rows),
        grid=(1,),
        in_specs=[pl.BlockSpec((1, tall, LANES), lambda i: (0, 0, 0))] + [whole] * 3,
        out_specs=[pl.BlockSpec(s, lambda i: (0, 0)) for s in shapes],
        out_shape=[jax.ShapeDtypeStruct(s, F32) for s in shapes],
        compiler_params=params(RING_VMEM),
        name="finish",
    )(own, *others)


def along_z(x, shift):
    pairs = [(y * NZ + z, y * NZ + (z + shift) % NZ) for y in range(NY) for z in range(NZ)]
    return lax.ppermute(x, "ptcl", pairs)


def along_y(x, shift):
    pairs = [(y * NZ + z, (y + shift) % NY * NZ + z) for y in range(NY) for z in range(NZ)]
    return lax.ppermute(x, "ptcl", pairs)


def shards(images, target, ctf_group, ctf_table, noise_weight, references):
    panels = references.shape[0]
    count = ctf_table.shape[0]
    me = lax.axis_index("ptcl")
    y, z = me // NZ, me % NZ
    slots = images.shape[0]
    groups = ctf_group.reshape(1, slots)
    noise = noise_weight.reshape(1, -1)
    rel = jnp.arange(NZ * NY, dtype=I32)
    order = (y + rel % NY) % NY * NZ + (z + rel // NY) % NZ
    middle = NZ * NY // 2
    weighted, square = zip(
        *[weigh(o, groups, images, ctf_table, noise) for o in (order[:middle], order[middle:])]
    )

    rows = -(-panels // 32) * 32
    half = rows // 2
    near = [references] + [along_y(references, NY - j) for j in range(1, NY)]
    column = stack(near, half)
    common = (weighted, square, groups)
    jobs, carry = [(0, column)], None
    up = [along_z(c, 1) for c in column]
    down = [along_z(c, -1) for c in column]
    for step in range(1, NZ // 2):
        jobs += [(NZ - step, up), (step, down)]
        if step < NZ // 2 - 1:
            up, down = [along_z(c, 1) for c in up], [along_z(c, -1) for c in down]
        else:
            far = [along_z(up[0], 1), along_z(down[1], -1)]
        carry, jobs = score(jobs, *common, carry, 0, panels), []
    classes = lax.axis_size("cls")
    mass, peak, evidence = score([(NZ // 2, far)], *common, carry, classes, panels)

    evidence = lax.all_to_all(evidence, "cls", 0, 0)

    share = 24 * NZ * NY
    shard = target // share
    shard_y, shard_z = shard // NZ, shard % NZ
    block = (shard_z - z + NZ) % NZ * NY + (shard_y - y + NY) % NY
    place = jnp.where(target >= 0, (block * 8 + 2) * LANES + target % share, -1)
    post, weights, relay = posterior(mass, peak, evidence, place.reshape(1, slots), groups, count)
    relay = relay.reshape(NZ, NY, 8, LANES)

    fixed = (post, weighted, relay, weights)
    far = NZ // 2
    came = [[along_z(ring_step([far], n, *fixed, [])[0], 1 - 2 * n)] for n in range(2)]
    for step in range(far - 1, 0, -1):
        for n in range(2):
            places = [step, NZ - step][:: 1 - 2 * n]
            blocks = ring_step(places, n, *fixed, came[n])
            came[n] = [along_z(x, d) for x, d in zip(blocks, (1 - 2 * n, 2 * n - 1))]
    own = ring_last(*fixed, came)
    others = [along_y(own[j], j) for j in range(1, NY)]
    class_sums, found, class_weights = finish(panels, rows, own, others)
    return class_sums, class_weights, found[2:].reshape(-1)


def solution(mesh):
    placed = (P("ptcl", None), P("ptcl"), P("ptcl"), P(), P(), P("cls", "ptcl"))
    return jax.shard_map(
        shards,
        mesh=mesh,
        in_specs=placed,
        out_specs=(P("ptcl", "cls"), P(None, "cls"), P("ptcl")),
        check_vma=False,
    )
```

```python
import functools

import jax
import jax.numpy as jnp
from jax import lax
from jax.experimental import pallas as pl
from jax.experimental.pallas import tpu as pltpu
from jax.sharding import PartitionSpec as P

NY, NZ = 4, 8
LANES = 128
TILE = 16
F32, BF16, I16, I32 = jnp.float32, jnp.bfloat16, jnp.int16, jnp.int32
NT = (((1,), (1,)), ((), ()))
TN = (((0,), (0,)), ((), ()))
WEIGH_VMEM, SCORE_VMEM, POST_VMEM, RING_VMEM = 36, 12, 16, 8
WEIGHT = 100
LOW_EXPONENT = -100.0


def dot(a, b, dims=(((1,), (0,)), ((), ()))):
    return lax.dot_general(a, b, dims, preferred_element_type=F32)


def split3(x):
    hi = x.astype(BF16)
    rest = x - hi.astype(F32)
    mid = rest.astype(BF16)
    low = (rest - mid.astype(F32)).astype(BF16)
    return jnp.concatenate([hi.astype(F32), mid.astype(F32), low.astype(F32)], axis=0).astype(BF16)


def onehot3(groups, count):
    row = lax.broadcasted_iota(I32, (3 * count, groups.shape[1]), 0)
    row = jnp.where(row >= 2 * count, row - 2 * count, jnp.where(row >= count, row - count, row))
    return (row == groups).astype(F32).astype(BF16)


def params(size):
    return pltpu.CompilerParams(vmem_limit_bytes=size * 1024 * 1024)


def cost(flops, byte_count):
    return pl.CostEstimate(flops=int(flops), bytes_accessed=int(byte_count), transcendentals=0)


def weight_kernel(order, groups, images, table, noise, *outs):
    weighted, square = outs[:2], outs[2:]
    count, step = table.shape[0], images.shape[0]
    begin = pl.multiple_of(pl.program_id(0) * step, step)
    member = onehot3(groups[:, pl.ds(begin, step)], count)
    for i in range(NZ):
        place = [
            pl.ds(pl.multiple_of(order[i * NY + j] * LANES, LANES), LANES) for j in range(NY)
        ]
        values = jnp.concatenate([table[:, p] for p in place], axis=1)
        scale = jnp.concatenate([noise[:, p] for p in place], axis=1)
        far, near = i // (NZ // 2), i % (NZ // 2)

        @pl.when(pl.program_id(0) == 0)
        def _(values=values, scale=scale, far=far, near=near):
            square[far][near] = split3(values * values * scale)

        rows = dot(member, split3(values), TN)
        picture = jnp.concatenate([images[:, p] for p in place], axis=1)
        weighted[far][near] = (picture.astype(F32) * rows * scale).astype(BF16)


def weigh(order, groups, images, table, noise):
    slots, count = images.shape[0], table.shape[0]
    wide = NY * LANES
    step = 256

    def whole(a):
        return pl.BlockSpec(a.shape, lambda i, o: (0, 0))

    return pl.pallas_call(
        weight_kernel,
        grid_spec=pltpu.PrefetchScalarGridSpec(
            num_scalar_prefetch=1,
            grid=(slots // step,),
            in_specs=[
                whole(groups),
                pl.BlockSpec((step, images.shape[1]), lambda i, o: (i, 0)),
                whole(table),
                whole(noise),
            ],
            out_specs=[pl.BlockSpec((NZ // 2, step, wide), lambda i, o: (0, i, 0))] * 2
            + [pl.BlockSpec((NZ // 2, 3 * count, wide), lambda i, o: (0, 0, 0))] * 2,
        ),
        out_shape=[jax.ShapeDtypeStruct((NZ // 2, slots, wide), BF16)] * 2
        + [jax.ShapeDtypeStruct((NZ // 2, 3 * count, wide), BF16)] * 2,
        compiler_params=params(WEIGH_VMEM),
        cost_estimate=cost(6e9 * WEIGHT, 4 * images.size),
        name="weigh",
    )(order, groups, images, table, noise)


def stack_kernel(*refs):
    blocks, (top, bottom) = refs[:NY], refs[-2:]
    half = top.shape[1]
    rest = blocks[0].shape[0] - half
    for j, block in enumerate(blocks):
        top[j] = block[:half, :]
        bottom[j, half - TILE :, :] = jnp.zeros((TILE, LANES), BF16)
        bottom[j, :rest, :] = block[half:, :]


def stack(blocks, half, after):
    return pl.pallas_call(
        stack_kernel,
        in_specs=in_vmem(NY) + [pl.BlockSpec(memory_space=pl.ANY)],
        out_specs=in_vmem(2),
        out_shape=[jax.ShapeDtypeStruct((NY, half, LANES), BF16)] * 2,
        compiler_params=params(RING_VMEM),
        name="stack",
    )(*blocks, after)


def in_vmem(count):
    return [pl.BlockSpec(memory_space=pltpu.VMEM)] * count


def score_kernel(jobs, first, last, panels, *refs):
    refs = list(refs)
    chunks = [[refs.pop(0) for _ in range(n)] for _, n in jobs]
    wa, wb, sa, sb, groups = [refs.pop(0) for _ in range(5)]
    total_in, energy_in = (None, None) if first else [refs.pop(0) for _ in range(2)]
    panel, right, square = [], [], []
    for (place, _), chunk in zip(jobs, chunks):
        parts = [jnp.concatenate([c[j] for j in range(NY)], axis=1) for c in chunk]
        panel.append(jnp.concatenate(parts, axis=0))
        far, near = place // (NZ // 2), place % (NZ // 2)
        right.append(((wa, wb)[far], near))
        square.append((sa, sb)[far][near])
    panel = jnp.concatenate(panel, axis=1)
    square = jnp.concatenate(square, axis=1)
    wide = panel.astype(F32)
    wide = wide * wide
    hi = wide.astype(BF16)
    low = (wide - hi.astype(F32)).astype(BF16)
    energy = dot(hi, square, NT) + dot(low, square, NT)
    if not first:
        energy += energy_in[...]
    if last:
        mass, peak, evidence = refs
        hi = energy.astype(BF16)
        rest = energy - hi.astype(F32)
        mid = rest.astype(BF16)
        low = (rest - mid.astype(F32)).astype(BF16)
    else:
        total, refs[1][...] = refs[0], energy
    slots = groups.shape[1]
    step = 256
    for begin in range(0, slots, step):
        here = slice(begin, begin + step)
        value = dot(panel, jnp.concatenate([w[k, here, :] for w, k in right], axis=1), NT)
        if not first:
            value += total_in[:, here]
        if not last:
            total[:, here] = value
            continue
        member = onehot3(groups[:, here], energy.shape[1] // 3)
        value -= 0.5 * (dot(hi, member) + dot(mid, member) + dot(low, member))
        row = lax.broadcasted_iota(I32, value.shape, 0)
        value = jnp.where(row < panels, value, -jnp.inf)
        top = jnp.max(value, axis=0, keepdims=True)
        value = jnp.exp(value - top)
        mass[:, here] = value
        peak[:, here] = top
        evidence[:, here] = top + jnp.log(jnp.sum(value, axis=0, keepdims=True))


def score(jobs, weighted, square, groups, carry, last, panels):
    rows = sum(a.shape[1] for a in jobs[0][1])
    slots = groups.shape[1]
    count3 = square[0].shape[1]
    if all(place < NZ // 2 for place, _ in jobs):
        weighted, square = weighted[:1] * 2, square[:1] * 2
    outs = [jax.ShapeDtypeStruct((rows, slots), F32)]
    if last:
        outs += [jax.ShapeDtypeStruct((1, slots), F32)] * 2
    else:
        outs += [jax.ShapeDtypeStruct((rows, count3), F32)]
    args = [a for job in jobs for a in job[1]] + [*weighted, *square, groups]
    args += [] if carry is None else list(carry)
    work = 2.5 * rows * slots * NY * LANES * len(jobs)
    return pl.pallas_call(
        functools.partial(
            score_kernel, [(j[0], len(j[1])) for j in jobs], carry is None, last, panels
        ),
        in_specs=in_vmem(len(args)),
        out_specs=in_vmem(len(outs)),
        out_shape=outs,
        compiler_params=params(SCORE_VMEM),
        cost_estimate=cost(work * WEIGHT, 4e6 * len(jobs)),
        name="score",
    )(*args)


def posterior_kernel(mass, peak, evidence, place, groups, post, weights, relay):
    live = place[...] >= 0
    scale = jnp.where(live, jnp.exp(peak[...] - evidence[...]), 0.0)
    value = (mass[...] * scale).astype(BF16)
    post[...] = value
    count = weights.shape[1]
    slots = groups.shape[1]
    member = (lax.broadcasted_iota(I32, (count, slots), 0) == groups[...]).astype(F32).astype(BF16)
    filled = [value, jnp.zeros((NY * LANES - value.shape[0], slots), BF16)]
    filled = jnp.concatenate(filled, axis=0)
    for j in range(NY):
        weights[j] = dot(member, filled[j * LANES : (j + 1) * LANES], NT)
    spot = place[...]
    line = lax.shift_right_arithmetic(spot, 7)
    high = (lax.broadcasted_iota(I32, (relay.shape[0], slots), 0) == line).astype(F32).astype(BF16)
    lane = lax.broadcasted_iota(I32, (LANES, slots), 0) == (spot & 127)
    found = split3(jnp.where(live, evidence[...], 0.0))
    out = jnp.zeros(relay.shape, F32)
    for k in (2, 1, 0):
        out += dot(high, jnp.where(lane, found[k : k + 1].astype(F32), 0.0).astype(BF16), NT)
    relay[...] = out


def posterior(mass, peak, evidence, place, groups, count):
    rows, slots = mass.shape
    return pl.pallas_call(
        posterior_kernel,
        out_shape=[
            jax.ShapeDtypeStruct((rows, slots), BF16),
            jax.ShapeDtypeStruct((NY, count, LANES), F32),
            jax.ShapeDtypeStruct((NZ * NY * 8, LANES), F32),
        ],
        compiler_params=params(POST_VMEM),
        cost_estimate=cost(1e9, 5e6),
        name="posterior",
    )(mass, peak, evidence, place, groups)


def exponent(x):
    top = jnp.max(jnp.abs(x), axis=0, keepdims=True)
    return jnp.maximum(jnp.ceil(jnp.log2(jnp.maximum(top, 2.0**LOW_EXPONENT))), LOW_EXPONENT)


def to_int(x):
    return jnp.round(x).astype(I32)


def put(out, j, sums, relay, weights):
    rows = sums.shape[0]
    e = exponent(sums)
    main = to_int(sums * jnp.exp2(14.0 - e))
    if relay is None:
        last = lax.broadcasted_iota(I32, sums.shape, 0) == rows - 1
        out[j] = jnp.where(last, e.astype(I32), main).astype(I16)
        return
    out[j, :rows, :] = main.astype(I16)
    row = lax.broadcasted_iota(I32, (8, LANES), 0)
    f, g = exponent(relay), exponent(weights)
    up, down = jnp.exp2(14.0 - f), jnp.exp2(f - 14.0)
    part = jnp.round(relay * up)
    rest = to_int((relay - part * down) * up * 2.0**14)
    high = jnp.where(row < 2, jnp.where(row == 0, e, f), part).astype(I32)
    low = jnp.where(row < 2, jnp.where(row == 0, g, 0.0).astype(I32), rest)
    out[j, rows + TILE :, :] = to_int(weights * jnp.exp2(14.0 - g)).astype(I16)
    out[j, rows : rows + TILE, :] = jnp.concatenate([high, low], axis=0).astype(I16)


def number(x):
    return x.astype(I32).astype(F32)


def decode(block, rows):
    if block.shape[0] == rows:
        last = lax.broadcasted_iota(I32, block.shape, 0) == rows - 1
        e = number(block[rows - TILE :, :])[TILE - 1 : TILE]
        return jnp.where(last, 0.0, number(block) * jnp.exp2(e - 14.0)), None, None
    tail = number(block[rows : rows + TILE, :])
    high, low = tail[:8], tail[8:]
    sums = number(block[:rows, :]) * jnp.exp2(high[0:1] - 14.0)
    down = jnp.exp2(high[1:2] - 14.0)
    row = lax.broadcasted_iota(I32, high.shape, 0)
    relay = jnp.where(row < 2, 0.0, (high + low * 2.0**-14) * down)
    return sums, relay, number(block[rows + TILE :, :]) * jnp.exp2(low[0:1] - 14.0)


def plus(a, b):
    return [None if x is None else x + w for x, w in zip(a, b)]


def products(post, weighted, place):
    for begin in range(0, NY, 2):
        right = weighted[place % (NZ // 2), :, begin * LANES : (begin + 2) * LANES]
        product = dot(post, right)
        yield begin, product[:, :LANES]
        yield begin + 1, product[:, LANES:]


def ring_kernel(stream, places, post, *refs):
    refs = list(refs)
    ways = len(places)
    weighted = [refs.pop(0) for _ in range(ways)]
    relay, weights = [refs.pop(0) for _ in range(2)] if stream == 0 else (None, None)
    outs = [refs.pop() for _ in range(ways)][::-1]
    came = refs + [None] * (ways - len(refs))
    rows = post.shape[0] // 2
    left = post[stream * rows : (stream + 1) * rows, :]
    for way, place in enumerate(places):
        for j, sums in products(left, weighted[way], place):
            mine = [sums, None, None]
            if stream == 0:
                mine = [sums, relay[place, j], weights[j]]
            if came[way] is not None:
                mine = plus(mine, decode(came[way][j], rows))
            put(outs[way], j, *mine)


def ring_step(places, stream, post, weighted, relay, weights, came):
    rows, slots = post.shape[0] // 2, post.shape[1]
    tall = rows if stream else rows + TILE + weights.shape[1]
    args = [post] + [weighted[p // (NZ // 2)] for p in places]
    args += [] if stream else [relay, weights]
    args += came
    return pl.pallas_call(
        functools.partial(ring_kernel, stream, places),
        in_specs=in_vmem(len(args)),
        out_specs=in_vmem(len(places)),
        out_shape=[jax.ShapeDtypeStruct((NY, tall, LANES), I16)] * len(places),
        compiler_params=params(RING_VMEM),
        cost_estimate=cost(2 * rows * slots * NY * LANES * len(places), 4e6),
        name="ring",
    )(*args)


def last_kernel(post, weighted, relay, weights, *refs):
    came, out = [refs[:2], refs[2:4]], refs[4]
    rows = post.shape[0] // 2
    got = [[[decode(c[j], rows) for c in pair] for j in range(NY)] for pair in came]
    mass = [weights[j] + got[0][j][0][2] + got[0][j][1][2] for j in range(NY)]
    mass = jnp.concatenate(mass, axis=0)
    for j, sums in products(post[...], weighted, 0):
        both = [
            sums[n * rows : (n + 1) * rows] + got[n][j][0][0] + got[n][j][1][0] for n in range(2)
        ]
        extra = relay[0, j] + got[0][j][0][1] + got[0][j][1][1]
        put(out, j, jnp.concatenate(both, axis=0), extra, mass)


def ring_last(post, weighted, relay, weights, came):
    rows, slots = post.shape
    tall = rows + TILE + NY * weights.shape[1]
    args = [post, weighted[0], relay, weights, *came[0], *came[1]]
    return pl.pallas_call(
        last_kernel,
        in_specs=in_vmem(len(args)),
        out_specs=pl.BlockSpec(memory_space=pltpu.VMEM),
        out_shape=jax.ShapeDtypeStruct((NY, tall, LANES), I16),
        compiler_params=params(RING_VMEM),
        cost_estimate=cost(2 * rows * slots * NY * LANES, 4e6),
        name="last",
    )(*args)


def finish_kernel(panels, rows, own, a, b, c, sums, evidence, weights):
    total = decode(own[0], rows)
    for other in (a, b, c):
        total = plus(total, decode(other[...], rows))
    sums[...] = total[0].T[:, :panels]
    evidence[...] = total[1]
    count = weights.shape[0]
    for j in range(NY):
        begin, end = j * LANES, min((j + 1) * LANES, panels)
        weights[:, begin:end] = total[2][j * count : (j + 1) * count, : end - begin]


def finish(panels, rows, own, others):
    tall = own.shape[1]
    whole = pl.BlockSpec((tall, LANES), lambda i: (0, 0))
    shapes = [(LANES, panels), (8, LANES), ((tall - rows - TILE) // NY, panels)]
    return pl.pallas_call(
        functools.partial(finish_kernel, panels, rows),
        grid=(1,),
        in_specs=[pl.BlockSpec((1, tall, LANES), lambda i: (0, 0, 0))] + [whole] * 3,
        out_specs=[pl.BlockSpec(s, lambda i: (0, 0)) for s in shapes],
        out_shape=[jax.ShapeDtypeStruct(s, F32) for s in shapes],
        compiler_params=params(RING_VMEM),
        name="finish",
    )(own, *others)


def along_z(x, shift):
    pairs = [(y * NZ + z, y * NZ + (z + shift) % NZ) for y in range(NY) for z in range(NZ)]
    return lax.ppermute(x, "ptcl", pairs)


def along_y(x, shift):
    pairs = [(y * NZ + z, (y + shift) % NY * NZ + z) for y in range(NY) for z in range(NZ)]
    return lax.ppermute(x, "ptcl", pairs)


def across(x, mask, size):
    return lax.ppermute(x, "cls", [(i, i ^ mask) for i in range(size)])


def shards(images, target, ctf_group, ctf_table, noise_weight, references):
    panels = references.shape[0]
    count = ctf_table.shape[0]
    me = lax.axis_index("ptcl")
    y, z = me // NZ, me % NZ
    slots = images.shape[0]
    groups = ctf_group.reshape(1, slots)
    noise = noise_weight.reshape(1, -1)
    rel = jnp.arange(NZ * NY, dtype=I32)
    order = (y + rel % NY) % NY * NZ + (z + rel // NY) % NZ
    found = weigh(order, groups, images, ctf_table, noise)
    weighted, square = found[:2], found[2:]

    rows = -(-panels // 32) * 32
    half = rows // 2
    near = [references] + [along_y(references, NY - j) for j in range(1, NY)]
    column = stack(near, half, square[0])
    common = (weighted, square, groups)
    jobs, carry = [(0, column)], None
    up = [along_z(c, 1) for c in column]
    down = [along_z(c, -1) for c in column]
    for step in range(1, NZ // 2):
        jobs += [(NZ - step, up), (step, down)]
        if step < NZ // 2 - 1:
            up, down = [along_z(c, 1) for c in up], [along_z(c, -1) for c in down]
        else:
            far = [along_z(up[0], 1), along_z(down[1], -1)]
        carry, jobs = score(jobs, *common, carry, False, panels), []
    mass, peak, evidence = score([(NZ // 2, far)], *common, carry, True, panels)

    size = lax.axis_size("cls")
    mask = 1
    while mask < size:
        other = across(evidence, mask, size)
        top = jnp.maximum(evidence, other)
        evidence = top + jnp.log(jnp.exp(evidence - top) + jnp.exp(other - top))
        mask *= 2

    share = 24 * NZ * NY
    shard = target // share
    shard_y, shard_z = shard // NZ, shard % NZ
    block = (shard_z - z + NZ) % NZ * NY + (shard_y - y + NY) % NY
    place = jnp.where(target >= 0, (block * 8 + 2) * LANES + target % share, -1)
    post, weights, relay = posterior(mass, peak, evidence, place.reshape(1, slots), groups, count)
    relay = relay.reshape(NZ, NY, 8, LANES)

    fixed = (post, weighted, relay, weights)
    far = NZ // 2
    came = [[along_z(ring_step([far], n, *fixed, [])[0], 1 - 2 * n)] for n in range(2)]
    for step in range(far - 1, 0, -1):
        for n in range(2):
            places = [step, NZ - step][:: 1 - 2 * n]
            blocks = ring_step(places, n, *fixed, came[n])
            came[n] = [along_z(x, d) for x, d in zip(blocks, (1 - 2 * n, 2 * n - 1))]
    own = ring_last(*fixed, came)
    others = [along_y(own[j], j) for j in range(1, NY)]
    class_sums, found, class_weights = finish(panels, rows, own, others)
    return class_sums, class_weights, found[2:].reshape(-1)


def solution(mesh):
    placed = (P("ptcl", None), P("ptcl"), P("ptcl"), P(), P(), P("cls", "ptcl"))
    return jax.shard_map(
        shards,
        mesh=mesh,
        in_specs=placed,
        out_specs=(P("ptcl", "cls"), P(None, "cls"), P("ptcl")),
        check_vma=False,
    )
```

```python
import functools

import jax
import jax.numpy as jnp
from jax import lax
from jax.experimental import pallas as pl
from jax.experimental.pallas import tpu as pltpu
from jax.sharding import PartitionSpec as P

NY, NZ = 4, 8
LANES = 128
TILE = 16
F32, BF16, I16, I32 = jnp.float32, jnp.bfloat16, jnp.int16, jnp.int32
NT = (((1,), (1,)), ((), ()))
TN = (((0,), (0,)), ((), ()))
WEIGH_VMEM, SCORE_VMEM, POST_VMEM, RING_VMEM = 36, 12, 16, 8
WEIGHT = 100
LOW_EXPONENT = -100.0


def dot(a, b, dims=(((1,), (0,)), ((), ()))):
    return lax.dot_general(a, b, dims, preferred_element_type=F32)


def split3(x):
    hi = x.astype(BF16)
    rest = x - hi.astype(F32)
    mid = rest.astype(BF16)
    low = (rest - mid.astype(F32)).astype(BF16)
    return jnp.concatenate([hi.astype(F32), mid.astype(F32), low.astype(F32)], axis=0).astype(BF16)


def onehot3(groups, count):
    row = lax.broadcasted_iota(I32, (3 * count, groups.shape[1]), 0)
    row = jnp.where(row >= 2 * count, row - 2 * count, jnp.where(row >= count, row - count, row))
    return (row == groups).astype(F32).astype(BF16)


def params(size):
    return pltpu.CompilerParams(vmem_limit_bytes=size * 1024 * 1024)


def cost(flops, byte_count):
    return pl.CostEstimate(flops=int(flops), bytes_accessed=int(byte_count), transcendentals=0)


def weight_kernel(order, groups, images, table, noise, *outs):
    weighted, square = outs[:2], outs[2:]
    count, step = table.shape[0], images.shape[0]
    begin = pl.multiple_of(pl.program_id(0) * step, step)
    member = onehot3(groups[:, pl.ds(begin, step)], count)
    for i in range(NZ):
        place = [
            pl.ds(pl.multiple_of(order[i * NY + j] * LANES, LANES), LANES) for j in range(NY)
        ]
        values = jnp.concatenate([table[:, p] for p in place], axis=1)
        scale = jnp.concatenate([noise[:, p] for p in place], axis=1)
        far, near = i // (NZ // 2), i % (NZ // 2)

        @pl.when(pl.program_id(0) == 0)
        def _(values=values, scale=scale, far=far, near=near):
            square[far][near] = split3(values * values * scale)

        rows = dot(member, split3(values), TN)
        picture = jnp.concatenate([images[:, p] for p in place], axis=1)
        weighted[far][near] = (picture.astype(F32) * rows * scale).astype(BF16)


def weigh(order, groups, images, table, noise):
    slots, count = images.shape[0], table.shape[0]
    wide = NY * LANES
    step = slots // 3

    def whole(a):
        return pl.BlockSpec(a.shape, lambda i, o: (0, 0))

    return pl.pallas_call(
        weight_kernel,
        grid_spec=pltpu.PrefetchScalarGridSpec(
            num_scalar_prefetch=1,
            grid=(slots // step,),
            in_specs=[
                whole(groups),
                pl.BlockSpec((step, images.shape[1]), lambda i, o: (i, 0)),
                whole(table),
                whole(noise),
            ],
            out_specs=[pl.BlockSpec((NZ // 2, step, wide), lambda i, o: (0, i, 0))] * 2
            + [pl.BlockSpec((NZ // 2, 3 * count, wide), lambda i, o: (0, 0, 0))] * 2,
        ),
        out_shape=[jax.ShapeDtypeStruct((NZ // 2, slots, wide), BF16)] * 2
        + [jax.ShapeDtypeStruct((NZ // 2, 3 * count, wide), BF16)] * 2,
        compiler_params=params(WEIGH_VMEM),
        cost_estimate=cost(6e9 * WEIGHT, 4 * images.size),
        name="weigh",
    )(order, groups, images, table, noise)


def stack_kernel(*refs):
    blocks, (top, bottom) = refs[:NY], refs[-2:]
    half = top.shape[1]
    rest = blocks[0].shape[0] - half
    for j, block in enumerate(blocks):
        top[j] = block[:half, :]
        bottom[j, half - TILE :, :] = jnp.zeros((TILE, LANES), BF16)
        bottom[j, :rest, :] = block[half:, :]


def stack(blocks, half, after):
    return pl.pallas_call(
        stack_kernel,
        in_specs=in_vmem(NY) + [pl.BlockSpec(memory_space=pl.ANY)],
        out_specs=in_vmem(2),
        out_shape=[jax.ShapeDtypeStruct((NY, half, LANES), BF16)] * 2,
        compiler_params=params(RING_VMEM),
        name="stack",
    )(*blocks, after)


def in_vmem(count):
    return [pl.BlockSpec(memory_space=pltpu.VMEM)] * count


def score_kernel(jobs, first, last, panels, *refs):
    refs = list(refs)
    chunks = [[refs.pop(0) for _ in range(n)] for _, n in jobs]
    wa, wb, sa, sb, groups = [refs.pop(0) for _ in range(5)]
    total_in, energy_in = (None, None) if first else [refs.pop(0) for _ in range(2)]
    panel, right, square = [], [], []
    for (place, _), chunk in zip(jobs, chunks):
        parts = [jnp.concatenate([c[j] for j in range(NY)], axis=1) for c in chunk]
        panel.append(jnp.concatenate(parts, axis=0))
        far, near = place // (NZ // 2), place % (NZ // 2)
        right.append(((wa, wb)[far], near))
        square.append((sa, sb)[far][near])
    panel = jnp.concatenate(panel, axis=1)
    square = jnp.concatenate(square, axis=1)
    wide = panel.astype(F32)
    wide = wide * wide
    hi = wide.astype(BF16)
    low = (wide - hi.astype(F32)).astype(BF16)
    energy = dot(hi, square, NT) + dot(low, square, NT)
    if not first:
        energy += energy_in[...]
    if last:
        mass, peak, evidence = refs
        hi = energy.astype(BF16)
        rest = energy - hi.astype(F32)
        mid = rest.astype(BF16)
        low = (rest - mid.astype(F32)).astype(BF16)
    else:
        total, refs[1][...] = refs[0], energy
    slots = groups.shape[1]
    step = 256
    for begin in range(0, slots, step):
        here = slice(begin, begin + step)
        value = dot(panel, jnp.concatenate([w[k, here, :] for w, k in right], axis=1), NT)
        if not first:
            value += total_in[:, here]
        if not last:
            total[:, here] = value
            continue
        member = onehot3(groups[:, here], energy.shape[1] // 3)
        value -= 0.5 * (dot(hi, member) + dot(mid, member) + dot(low, member))
        row = lax.broadcasted_iota(I32, value.shape, 0)
        value = jnp.where(row < panels, value, -jnp.inf)
        top = jnp.max(value, axis=0, keepdims=True)
        value = jnp.exp(value - top)
        mass[:, here] = value
        peak[:, here] = top
        evidence[:, here] = top + jnp.log(jnp.sum(value, axis=0, keepdims=True))


def score(jobs, weighted, square, groups, carry, last, panels):
    rows = sum(a.shape[1] for a in jobs[0][1])
    slots = groups.shape[1]
    count3 = square[0].shape[1]
    if all(place < NZ // 2 for place, _ in jobs):
        weighted, square = weighted[:1] * 2, square[:1] * 2
    outs = [jax.ShapeDtypeStruct((rows, slots), F32)]
    if last:
        outs += [jax.ShapeDtypeStruct((1, slots), F32)] * 2
    else:
        outs += [jax.ShapeDtypeStruct((rows, count3), F32)]
    args = [a for job in jobs for a in job[1]] + [*weighted, *square, groups]
    args += [] if carry is None else list(carry)
    work = 2.5 * rows * slots * NY * LANES * len(jobs)
    return pl.pallas_call(
        functools.partial(
            score_kernel, [(j[0], len(j[1])) for j in jobs], carry is None, last, panels
        ),
        in_specs=in_vmem(len(args)),
        out_specs=in_vmem(len(outs)),
        out_shape=outs,
        compiler_params=params(SCORE_VMEM),
        cost_estimate=cost(work * WEIGHT, 4e6 * len(jobs)),
        name="score",
    )(*args)


def posterior_kernel(mass, peak, evidence, place, groups, post, weights, relay):
    live = place[...] >= 0
    scale = jnp.where(live, jnp.exp(peak[...] - evidence[...]), 0.0)
    value = (mass[...] * scale).astype(BF16)
    post[...] = value
    count = weights.shape[1]
    slots = groups.shape[1]
    member = (lax.broadcasted_iota(I32, (count, slots), 0) == groups[...]).astype(F32).astype(BF16)
    filled = [value, jnp.zeros((NY * LANES - value.shape[0], slots), BF16)]
    filled = jnp.concatenate(filled, axis=0)
    for j in range(NY):
        weights[j] = dot(member, filled[j * LANES : (j + 1) * LANES], NT)
    spot = place[...]
    line = lax.shift_right_arithmetic(spot, 7)
    high = (lax.broadcasted_iota(I32, (relay.shape[0], slots), 0) == line).astype(F32).astype(BF16)
    lane = lax.broadcasted_iota(I32, (LANES, slots), 0) == (spot & 127)
    found = split3(jnp.where(live, evidence[...], 0.0))
    out = jnp.zeros(relay.shape, F32)
    for k in (2, 1, 0):
        out += dot(high, jnp.where(lane, found[k : k + 1].astype(F32), 0.0).astype(BF16), NT)
    relay[...] = out


def posterior(mass, peak, evidence, place, groups, count):
    rows, slots = mass.shape
    return pl.pallas_call(
        posterior_kernel,
        out_shape=[
            jax.ShapeDtypeStruct((rows, slots), BF16),
            jax.ShapeDtypeStruct((NY, count, LANES), F32),
            jax.ShapeDtypeStruct((NZ * NY * 8, LANES), F32),
        ],
        compiler_params=params(POST_VMEM),
        cost_estimate=cost(1e9, 5e6),
        name="posterior",
    )(mass, peak, evidence, place, groups)


def exponent(x):
    top = jnp.max(jnp.abs(x), axis=0, keepdims=True)
    return jnp.maximum(jnp.ceil(jnp.log2(jnp.maximum(top, 2.0**LOW_EXPONENT))), LOW_EXPONENT)


def to_int(x):
    return jnp.round(x).astype(I32)


def put(out, j, sums, relay, weights):
    rows = sums.shape[0]
    e = exponent(sums)
    main = to_int(sums * jnp.exp2(14.0 - e))
    if relay is None:
        last = lax.broadcasted_iota(I32, sums.shape, 0) == rows - 1
        out[j] = jnp.where(last, e.astype(I32), main).astype(I16)
        return
    out[j, :rows, :] = main.astype(I16)
    row = lax.broadcasted_iota(I32, (8, LANES), 0)
    f, g = exponent(relay), exponent(weights)
    up, down = jnp.exp2(14.0 - f), jnp.exp2(f - 14.0)
    part = jnp.round(relay * up)
    rest = to_int((relay - part * down) * up * 2.0**14)
    high = jnp.where(row < 2, jnp.where(row == 0, e, f), part).astype(I32)
    low = jnp.where(row < 2, jnp.where(row == 0, g, 0.0).astype(I32), rest)
    out[j, rows + TILE :, :] = to_int(weights * jnp.exp2(14.0 - g)).astype(I16)
    out[j, rows : rows + TILE, :] = jnp.concatenate([high, low], axis=0).astype(I16)


def number(x):
    return x.astype(I32).astype(F32)


def decode(block, rows):
    if block.shape[0] == rows:
        last = lax.broadcasted_iota(I32, block.shape, 0) == rows - 1
        e = number(block[rows - TILE :, :])[TILE - 1 : TILE]
        return jnp.where(last, 0.0, number(block) * jnp.exp2(e - 14.0)), None, None
    tail = number(block[rows : rows + TILE, :])
    high, low = tail[:8], tail[8:]
    sums = number(block[:rows, :]) * jnp.exp2(high[0:1] - 14.0)
    down = jnp.exp2(high[1:2] - 14.0)
    row = lax.broadcasted_iota(I32, high.shape, 0)
    relay = jnp.where(row < 2, 0.0, (high + low * 2.0**-14) * down)
    return sums, relay, number(block[rows + TILE :, :]) * jnp.exp2(low[0:1] - 14.0)


def plus(a, b):
    return [None if x is None else x + w for x, w in zip(a, b)]


def products(post, weighted, place):
    for begin in range(0, NY, 2):
        right = weighted[place % (NZ // 2), :, begin * LANES : (begin + 2) * LANES]
        product = dot(post, right)
        yield begin, product[:, :LANES]
        yield begin + 1, product[:, LANES:]


def ring_kernel(stream, places, post, *refs):
    refs = list(refs)
    ways = len(places)
    weighted = [refs.pop(0) for _ in range(ways)]
    relay, weights = [refs.pop(0) for _ in range(2)] if stream == 0 else (None, None)
    outs = [refs.pop() for _ in range(ways)][::-1]
    came = refs + [None] * (ways - len(refs))
    rows = post.shape[0] // 2
    left = post[stream * rows : (stream + 1) * rows, :]
    for way, place in enumerate(places):
        for j, sums in products(left, weighted[way], place):
            mine = [sums, None, None]
            if stream == 0:
                mine = [sums, relay[place, j], weights[j]]
            if came[way] is not None:
                mine = plus(mine, decode(came[way][j], rows))
            put(outs[way], j, *mine)


def ring_step(places, stream, post, weighted, relay, weights, came):
    rows, slots = post.shape[0] // 2, post.shape[1]
    tall = rows if stream else rows + TILE + weights.shape[1]
    args = [post] + [weighted[p // (NZ // 2)] for p in places]
    args += [] if stream else [relay, weights]
    args += came
    return pl.pallas_call(
        functools.partial(ring_kernel, stream, places),
        in_specs=in_vmem(len(args)),
        out_specs=in_vmem(len(places)),
        out_shape=[jax.ShapeDtypeStruct((NY, tall, LANES), I16)] * len(places),
        compiler_params=params(RING_VMEM),
        cost_estimate=cost(2 * rows * slots * NY * LANES * len(places), 4e6),
        name="ring",
    )(*args)


def last_kernel(post, weighted, relay, weights, *refs):
    came, out = [refs[:2], refs[2:4]], refs[4]
    rows = post.shape[0] // 2
    got = [[[decode(c[j], rows) for c in pair] for j in range(NY)] for pair in came]
    mass = [weights[j] + got[0][j][0][2] + got[0][j][1][2] for j in range(NY)]
    mass = jnp.concatenate(mass, axis=0)
    for j, sums in products(post[...], weighted, 0):
        both = [
            sums[n * rows : (n + 1) * rows] + got[n][j][0][0] + got[n][j][1][0] for n in range(2)
        ]
        extra = relay[0, j] + got[0][j][0][1] + got[0][j][1][1]
        put(out, j, jnp.concatenate(both, axis=0), extra, mass)


def ring_last(post, weighted, relay, weights, came):
    rows, slots = post.shape
    tall = rows + TILE + NY * weights.shape[1]
    args = [post, weighted[0], relay, weights, *came[0], *came[1]]
    return pl.pallas_call(
        last_kernel,
        in_specs=in_vmem(len(args)),
        out_specs=pl.BlockSpec(memory_space=pltpu.VMEM),
        out_shape=jax.ShapeDtypeStruct((NY, tall, LANES), I16),
        compiler_params=params(RING_VMEM),
        cost_estimate=cost(2 * rows * slots * NY * LANES, 4e6),
        name="last",
    )(*args)


def finish_kernel(panels, rows, own, a, b, c, sums, evidence, weights):
    total = decode(own[0], rows)
    for other in (a, b, c):
        total = plus(total, decode(other[...], rows))
    sums[...] = total[0].T[:, :panels]
    evidence[...] = total[1]
    count = weights.shape[0]
    for j in range(NY):
        begin, end = j * LANES, min((j + 1) * LANES, panels)
        weights[:, begin:end] = total[2][j * count : (j + 1) * count, : end - begin]


def finish(panels, rows, own, others):
    tall = own.shape[1]
    whole = pl.BlockSpec((tall, LANES), lambda i: (0, 0))
    shapes = [(LANES, panels), (8, LANES), ((tall - rows - TILE) // NY, panels)]
    return pl.pallas_call(
        functools.partial(finish_kernel, panels, rows),
        grid=(1,),
        in_specs=[pl.BlockSpec((1, tall, LANES), lambda i: (0, 0, 0))] + [whole] * 3,
        out_specs=[pl.BlockSpec(s, lambda i: (0, 0)) for s in shapes],
        out_shape=[jax.ShapeDtypeStruct(s, F32) for s in shapes],
        compiler_params=params(RING_VMEM),
        name="finish",
    )(own, *others)


def along_z(x, shift):
    pairs = [(y * NZ + z, y * NZ + (z + shift) % NZ) for y in range(NY) for z in range(NZ)]
    return lax.ppermute(x, "ptcl", pairs)


def along_y(x, shift):
    pairs = [(y * NZ + z, (y + shift) % NY * NZ + z) for y in range(NY) for z in range(NZ)]
    return lax.ppermute(x, "ptcl", pairs)


def across(x, mask, size):
    return lax.ppermute(x, "cls", [(i, i ^ mask) for i in range(size)])


def shards(images, target, ctf_group, ctf_table, noise_weight, references):
    panels = references.shape[0]
    count = ctf_table.shape[0]
    me = lax.axis_index("ptcl")
    y, z = me // NZ, me % NZ
    slots = images.shape[0]
    groups = ctf_group.reshape(1, slots)
    noise = noise_weight.reshape(1, -1)
    rel = jnp.arange(NZ * NY, dtype=I32)
    order = (y + rel % NY) % NY * NZ + (z + rel // NY) % NZ
    found = weigh(order, groups, images, ctf_table, noise)
    weighted, square = found[:2], found[2:]

    rows = -(-panels // 32) * 32
    half = rows // 2
    near = [references] + [along_y(references, NY - j) for j in range(1, NY)]
    column = stack(near, half, square[0])
    common = (weighted, square, groups)
    jobs, carry = [(0, column)], None
    up = [along_z(c, 1) for c in column]
    down = [along_z(c, -1) for c in column]
    for step in range(1, NZ // 2):
        jobs += [(NZ - step, up), (step, down)]
        if step < NZ // 2 - 1:
            up, down = [along_z(c, 1) for c in up], [along_z(c, -1) for c in down]
        else:
            far = [along_z(up[0], 1), along_z(down[1], -1)]
        carry, jobs = score(jobs, *common, carry, False, panels), []
    mass, peak, evidence = score([(NZ // 2, far)], *common, carry, True, panels)

    size = lax.axis_size("cls")
    mask = 1
    while mask < size:
        other = across(evidence, mask, size)
        top = jnp.maximum(evidence, other)
        evidence = top + jnp.log(jnp.exp(evidence - top) + jnp.exp(other - top))
        mask *= 2

    share = 24 * NZ * NY
    shard = target // share
    shard_y, shard_z = shard // NZ, shard % NZ
    block = (shard_z - z + NZ) % NZ * NY + (shard_y - y + NY) % NY
    place = jnp.where(target >= 0, (block * 8 + 2) * LANES + target % share, -1)
    post, weights, relay = posterior(mass, peak, evidence, place.reshape(1, slots), groups, count)
    relay = relay.reshape(NZ, NY, 8, LANES)

    fixed = (post, weighted, relay, weights)
    far = NZ // 2
    came = [[along_z(ring_step([far], n, *fixed, [])[0], 1 - 2 * n)] for n in range(2)]
    for step in range(far - 1, 0, -1):
        for n in range(2):
            places = [step, NZ - step][:: 1 - 2 * n]
            blocks = ring_step(places, n, *fixed, came[n])
            came[n] = [along_z(x, d) for x, d in zip(blocks, (1 - 2 * n, 2 * n - 1))]
    own = ring_last(*fixed, came)
    others = [along_y(own[j], j) for j in range(1, NY)]
    class_sums, found, class_weights = finish(panels, rows, own, others)
    return class_sums, class_weights, found[2:].reshape(-1)


def solution(mesh):
    placed = (P("ptcl", None), P("ptcl"), P("ptcl"), P(), P(), P("cls", "ptcl"))
    return jax.shard_map(
        shards,
        mesh=mesh,
        in_specs=placed,
        out_specs=(P("ptcl", "cls"), P(None, "cls"), P("ptcl")),
        check_vma=False,
    )
```

```python
import functools

import jax
import jax.numpy as jnp
from jax import lax
from jax.experimental import pallas as pl
from jax.experimental.pallas import tpu as pltpu
from jax.sharding import PartitionSpec as P

NY, NZ = 4, 8
LANES = 128
TILE = 16
F32, BF16, I16, I32 = jnp.float32, jnp.bfloat16, jnp.int16, jnp.int32
NT = (((1,), (1,)), ((), ()))
TN = (((0,), (0,)), ((), ()))
WEIGH_VMEM, SCORE_VMEM, POST_VMEM, RING_VMEM = 36, 12, 16, 8
WEIGHT = 100
LOW_EXPONENT = -100.0


def dot(a, b, dims=(((1,), (0,)), ((), ()))):
    return lax.dot_general(a, b, dims, preferred_element_type=F32)


def split3(x):
    hi = x.astype(BF16)
    rest = x - hi.astype(F32)
    mid = rest.astype(BF16)
    low = (rest - mid.astype(F32)).astype(BF16)
    return jnp.concatenate([hi.astype(F32), mid.astype(F32), low.astype(F32)], axis=0).astype(BF16)


def onehot3(groups, count):
    row = lax.broadcasted_iota(I32, (3 * count, groups.shape[1]), 0)
    row = jnp.where(row >= 2 * count, row - 2 * count, jnp.where(row >= count, row - count, row))
    return (row == groups).astype(F32).astype(BF16)


def params(size):
    return pltpu.CompilerParams(vmem_limit_bytes=size * 1024 * 1024)


def cost(flops, byte_count):
    return pl.CostEstimate(flops=int(flops), bytes_accessed=int(byte_count), transcendentals=0)


def weight_kernel(order, groups, images, table, noise, *outs):
    weighted, square = outs[:2], outs[2:]
    count, step = table.shape[0], images.shape[0]
    begin = pl.multiple_of(pl.program_id(0) * step, step)
    member = onehot3(groups[:, pl.ds(begin, step)], count)
    for i in range(NZ):
        place = [
            pl.ds(pl.multiple_of(order[i * NY + j] * LANES, LANES), LANES) for j in range(NY)
        ]
        values = jnp.concatenate([table[:, p] for p in place], axis=1)
        scale = jnp.concatenate([noise[:, p] for p in place], axis=1)
        far, near = i // (NZ // 2), i % (NZ // 2)

        @pl.when(pl.program_id(0) == 0)
        def _(values=values, scale=scale, far=far, near=near):
            square[far][near] = split3(values * values * scale)

        rows = dot(member, split3(values), TN)
        picture = jnp.concatenate([images[:, p] for p in place], axis=1)
        weighted[far][near] = (picture.astype(F32) * rows * scale).astype(BF16)


def weigh(order, groups, images, table, noise):
    slots, count = images.shape[0], table.shape[0]
    wide = NY * LANES
    step = slots // 3

    def whole(a):
        return pl.BlockSpec(a.shape, lambda i, o: (0, 0))

    return pl.pallas_call(
        weight_kernel,
        grid_spec=pltpu.PrefetchScalarGridSpec(
            num_scalar_prefetch=1,
            grid=(slots // step,),
            in_specs=[
                whole(groups),
                pl.BlockSpec((step, images.shape[1]), lambda i, o: (i, 0)),
                whole(table),
                whole(noise),
            ],
            out_specs=[pl.BlockSpec((NZ // 2, step, wide), lambda i, o: (0, i, 0))] * 2
            + [pl.BlockSpec((NZ // 2, 3 * count, wide), lambda i, o: (0, 0, 0))] * 2,
        ),
        out_shape=[jax.ShapeDtypeStruct((NZ // 2, slots, wide), BF16)] * 2
        + [jax.ShapeDtypeStruct((NZ // 2, 3 * count, wide), BF16)] * 2,
        compiler_params=params(WEIGH_VMEM),
        cost_estimate=cost(6e9 * WEIGHT, 4 * images.size),
        name="weigh",
    )(order, groups, images, table, noise)


def stack_kernel(*refs):
    blocks, (top, bottom) = refs[:NY], refs[-2:]
    half = top.shape[1]
    rest = blocks[0].shape[0] - half
    for j, block in enumerate(blocks):
        top[j] = block[:half, :]
        bottom[j, half - TILE :, :] = jnp.zeros((TILE, LANES), BF16)
        bottom[j, :rest, :] = block[half:, :]


def stack(blocks, half, after):
    return pl.pallas_call(
        stack_kernel,
        in_specs=in_vmem(NY) + [pl.BlockSpec(memory_space=pl.ANY)],
        out_specs=in_vmem(2),
        out_shape=[jax.ShapeDtypeStruct((NY, half, LANES), BF16)] * 2,
        compiler_params=params(RING_VMEM),
        name="stack",
    )(*blocks, after)


def in_vmem(count):
    return [pl.BlockSpec(memory_space=pltpu.VMEM)] * count


def score_kernel(jobs, first, last, panels, *refs):
    refs = list(refs)
    chunks = [[refs.pop(0) for _ in range(n)] for _, n in jobs]
    wa, wb, sa, sb, groups = [refs.pop(0) for _ in range(5)]
    total_in, energy_in = (None, None) if first else [refs.pop(0) for _ in range(2)]
    panel, right, square = [], [], []
    for (place, _), chunk in zip(jobs, chunks):
        parts = [jnp.concatenate([c[j] for j in range(NY)], axis=1) for c in chunk]
        panel.append(jnp.concatenate(parts, axis=0))
        far, near = place // (NZ // 2), place % (NZ // 2)
        right.append(((wa, wb)[far], near))
        square.append((sa, sb)[far][near])
    panel = jnp.concatenate(panel, axis=1)
    square = jnp.concatenate(square, axis=1)
    wide = panel.astype(F32)
    wide = wide * wide
    hi = wide.astype(BF16)
    low = (wide - hi.astype(F32)).astype(BF16)
    energy = dot(hi, square, NT) + dot(low, square, NT)
    if not first:
        energy += energy_in[...]
    if last:
        mass, peak, evidence = refs
        hi = energy.astype(BF16)
        rest = energy - hi.astype(F32)
        mid = rest.astype(BF16)
        low = (rest - mid.astype(F32)).astype(BF16)
    else:
        total, refs[1][...] = refs[0], energy
    slots = groups.shape[1]
    step = 256
    for begin in range(0, slots, step):
        here = slice(begin, begin + step)
        value = dot(panel, jnp.concatenate([w[k, here, :] for w, k in right], axis=1), NT)
        if not first:
            value += total_in[:, here]
        if not last:
            total[:, here] = value
            continue
        member = onehot3(groups[:, here], energy.shape[1] // 3)
        value -= 0.5 * (dot(hi, member) + dot(mid, member) + dot(low, member))
        row = lax.broadcasted_iota(I32, value.shape, 0)
        value = jnp.where(row < panels, value, -jnp.inf)
        top = jnp.max(value, axis=0, keepdims=True)
        value = jnp.exp(value - top)
        mass[:, here] = value
        peak[:, here] = top
        evidence[:, here] = top + jnp.log(jnp.sum(value, axis=0, keepdims=True))


def score(jobs, weighted, square, groups, carry, last, panels):
    rows = sum(a.shape[1] for a in jobs[0][1])
    slots = groups.shape[1]
    count3 = square[0].shape[1]
    if all(place < NZ // 2 for place, _ in jobs):
        weighted, square = weighted[:1] * 2, square[:1] * 2
    outs = [jax.ShapeDtypeStruct((rows, slots), F32)]
    if last:
        outs += [jax.ShapeDtypeStruct((1, slots), F32)] * 2
    else:
        outs += [jax.ShapeDtypeStruct((rows, count3), F32)]
    args = [a for job in jobs for a in job[1]] + [*weighted, *square, groups]
    args += [] if carry is None else list(carry)
    work = 2.5 * rows * slots * NY * LANES * len(jobs)
    return pl.pallas_call(
        functools.partial(
            score_kernel, [(j[0], len(j[1])) for j in jobs], carry is None, last, panels
        ),
        in_specs=in_vmem(len(args)),
        out_specs=in_vmem(len(outs)),
        out_shape=outs,
        compiler_params=params(SCORE_VMEM),
        cost_estimate=cost(work * WEIGHT, 4e6 * len(jobs)),
        name="score",
    )(*args)


def posterior_kernel(mass, peak, evidence, place, groups, post, weights, relay):
    live = place[...] >= 0
    scale = jnp.where(live, jnp.exp(peak[...] - evidence[...]), 0.0)
    value = (mass[...] * scale).astype(BF16)
    post[...] = value
    count = weights.shape[1]
    slots = groups.shape[1]
    member = (lax.broadcasted_iota(I32, (count, slots), 0) == groups[...]).astype(F32).astype(BF16)
    filled = [value, jnp.zeros((NY * LANES - value.shape[0], slots), BF16)]
    filled = jnp.concatenate(filled, axis=0)
    for j in range(NY):
        weights[j] = dot(member, filled[j * LANES : (j + 1) * LANES], NT)
    spot = place[...]
    line = lax.shift_right_arithmetic(spot, 7)
    high = (lax.broadcasted_iota(I32, (relay.shape[0], slots), 0) == line).astype(F32).astype(BF16)
    lane = lax.broadcasted_iota(I32, (LANES, slots), 0) == (spot & 127)
    found = split3(jnp.where(live, evidence[...], 0.0))
    out = jnp.zeros(relay.shape, F32)
    for k in (2, 1, 0):
        out += dot(high, jnp.where(lane, found[k : k + 1].astype(F32), 0.0).astype(BF16), NT)
    relay[...] = out


def posterior(mass, peak, evidence, place, groups, count):
    rows, slots = mass.shape
    return pl.pallas_call(
        posterior_kernel,
        out_shape=[
            jax.ShapeDtypeStruct((rows, slots), BF16),
            jax.ShapeDtypeStruct((NY, count, LANES), F32),
            jax.ShapeDtypeStruct((NZ * NY * 8, LANES), F32),
        ],
        compiler_params=params(POST_VMEM),
        cost_estimate=cost(1e9, 5e6),
        name="posterior",
    )(mass, peak, evidence, place, groups)


def exponent(x):
    top = jnp.max(jnp.abs(x), axis=0, keepdims=True)
    return jnp.maximum(jnp.ceil(jnp.log2(jnp.maximum(top, 2.0**LOW_EXPONENT))), LOW_EXPONENT)


def to_int(x):
    return jnp.round(x).astype(I32)


def put(out, j, sums, relay, weights):
    rows = sums.shape[0]
    e = exponent(sums)
    main = to_int(sums * jnp.exp2(14.0 - e))
    if relay is None:
        last = lax.broadcasted_iota(I32, sums.shape, 0) == rows - 1
        out[j] = jnp.where(last, e.astype(I32), main).astype(I16)
        return
    out[j, :rows, :] = main.astype(I16)
    row = lax.broadcasted_iota(I32, (8, LANES), 0)
    f, g = exponent(relay), exponent(weights)
    up, down = jnp.exp2(14.0 - f), jnp.exp2(f - 14.0)
    part = jnp.round(relay * up)
    rest = to_int((relay - part * down) * up * 2.0**14)
    high = jnp.where(row < 2, jnp.where(row == 0, e, f), part).astype(I32)
    low = jnp.where(row < 2, jnp.where(row == 0, g, 0.0).astype(I32), rest)
    out[j, rows + TILE :, :] = to_int(weights * jnp.exp2(14.0 - g)).astype(I16)
    out[j, rows : rows + TILE, :] = jnp.concatenate([high, low], axis=0).astype(I16)


def number(x):
    return x.astype(I32).astype(F32)


def decode(block, rows):
    if block.shape[0] == rows:
        last = lax.broadcasted_iota(I32, block.shape, 0) == rows - 1
        e = number(block[rows - TILE :, :])[TILE - 1 : TILE]
        return jnp.where(last, 0.0, number(block) * jnp.exp2(e - 14.0)), None, None
    tail = number(block[rows : rows + TILE, :])
    high, low = tail[:8], tail[8:]
    sums = number(block[:rows, :]) * jnp.exp2(high[0:1] - 14.0)
    down = jnp.exp2(high[1:2] - 14.0)
    row = lax.broadcasted_iota(I32, high.shape, 0)
    relay = jnp.where(row < 2, 0.0, (high + low * 2.0**-14) * down)
    return sums, relay, number(block[rows + TILE :, :]) * jnp.exp2(low[0:1] - 14.0)


def plus(a, b):
    return [None if x is None else x + w for x, w in zip(a, b)]


def products(post, weighted, place):
    for begin in range(0, NY, 2):
        right = weighted[place % (NZ // 2), :, begin * LANES : (begin + 2) * LANES]
        product = dot(post, right)
        yield begin, product[:, :LANES]
        yield begin + 1, product[:, LANES:]


def ring_kernel(stream, places, post, *refs):
    refs = list(refs)
    ways = len(places)
    weighted = [refs.pop(0) for _ in range(ways)]
    relay, weights = [refs.pop(0) for _ in range(2)] if stream == 0 else (None, None)
    outs = [refs.pop() for _ in range(ways)][::-1]
    came = refs + [None] * (ways - len(refs))
    rows = post.shape[0] // 2
    left = post[stream * rows : (stream + 1) * rows, :]
    for way, place in enumerate(places):
        for j, sums in products(left, weighted[way], place):
            mine = [sums, None, None]
            if stream == 0:
                mine = [sums, relay[place, j], weights[j]]
            if came[way] is not None:
                mine = plus(mine, decode(came[way][j], rows))
            put(outs[way], j, *mine)


def ring_step(places, stream, post, weighted, relay, weights, came):
    rows, slots = post.shape[0] // 2, post.shape[1]
    tall = rows if stream else rows + TILE + weights.shape[1]
    args = [post] + [weighted[p // (NZ // 2)] for p in places]
    args += [] if stream else [relay, weights]
    args += came
    return pl.pallas_call(
        functools.partial(ring_kernel, stream, places),
        in_specs=in_vmem(len(args)),
        out_specs=in_vmem(len(places)),
        out_shape=[jax.ShapeDtypeStruct((NY, tall, LANES), I16)] * len(places),
        compiler_params=params(RING_VMEM),
        cost_estimate=cost(2 * rows * slots * NY * LANES * len(places), 4e6),
        name="ring",
    )(*args)


def last_kernel(post, weighted, relay, weights, *refs):
    came, out = [refs[:2], refs[2:4]], refs[4]
    rows = post.shape[0] // 2
    got = [[[decode(c[j], rows) for c in pair] for j in range(NY)] for pair in came]
    mass = [weights[j] + got[0][j][0][2] + got[0][j][1][2] for j in range(NY)]
    mass = jnp.concatenate(mass, axis=0)
    for j, sums in products(post[...], weighted, 0):
        both = [
            sums[n * rows : (n + 1) * rows] + got[n][j][0][0] + got[n][j][1][0] for n in range(2)
        ]
        extra = relay[0, j] + got[0][j][0][1] + got[0][j][1][1]
        put(out, j, jnp.concatenate(both, axis=0), extra, mass)


def ring_last(post, weighted, relay, weights, came):
    rows, slots = post.shape
    tall = rows + TILE + NY * weights.shape[1]
    args = [post, weighted[0], relay, weights, *came[0], *came[1]]
    return pl.pallas_call(
        last_kernel,
        in_specs=in_vmem(len(args)),
        out_specs=pl.BlockSpec(memory_space=pltpu.VMEM),
        out_shape=jax.ShapeDtypeStruct((NY, tall, LANES), I16),
        compiler_params=params(RING_VMEM),
        cost_estimate=cost(2 * rows * slots * NY * LANES, 4e6),
        name="last",
    )(*args)


def finish_kernel(panels, rows, own, a, b, c, sums, evidence, weights):
    total = decode(own[0], rows)
    for other in (a, b, c):
        total = plus(total, decode(other[...], rows))
    sums[...] = total[0].T[:, :panels]
    evidence[...] = total[1]
    count = weights.shape[0]
    for j in range(NY):
        begin, end = j * LANES, min((j + 1) * LANES, panels)
        weights[:, begin:end] = total[2][j * count : (j + 1) * count, : end - begin]


def finish(panels, rows, own, others):
    tall = own.shape[1]
    whole = pl.BlockSpec((tall, LANES), lambda i: (0, 0))
    shapes = [(LANES, panels), (8, LANES), ((tall - rows - TILE) // NY, panels)]
    return pl.pallas_call(
        functools.partial(finish_kernel, panels, rows),
        grid=(1,),
        in_specs=[pl.BlockSpec((1, tall, LANES), lambda i: (0, 0, 0))] + [whole] * 3,
        out_specs=[pl.BlockSpec(s, lambda i: (0, 0)) for s in shapes],
        out_shape=[jax.ShapeDtypeStruct(s, F32) for s in shapes],
        compiler_params=params(RING_VMEM),
        name="finish",
    )(own, *others)


def along_z(x, shift):
    pairs = [(y * NZ + z, y * NZ + (z + shift) % NZ) for y in range(NY) for z in range(NZ)]
    return lax.ppermute(x, "ptcl", pairs)


def along_y(x, shift):
    pairs = [(y * NZ + z, (y + shift) % NY * NZ + z) for y in range(NY) for z in range(NZ)]
    return lax.ppermute(x, "ptcl", pairs)


def across(x, mask, size):
    return lax.ppermute(x, "cls", [(i, i ^ mask) for i in range(size)])


def log_sum(parts):
    top = functools.reduce(jnp.maximum, parts)
    parts = [jnp.exp(p - top) for p in parts]
    while len(parts) > 1:
        parts = [p + q for p, q in zip(parts[::2], parts[1::2])]
    return top + jnp.log(parts[0])


def shards(images, target, ctf_group, ctf_table, noise_weight, references):
    panels = references.shape[0]
    count = ctf_table.shape[0]
    me = lax.axis_index("ptcl")
    y, z = me // NZ, me % NZ
    slots = images.shape[0]
    groups = ctf_group.reshape(1, slots)
    noise = noise_weight.reshape(1, -1)
    rel = jnp.arange(NZ * NY, dtype=I32)
    order = (y + rel % NY) % NY * NZ + (z + rel // NY) % NZ
    found = weigh(order, groups, images, ctf_table, noise)
    weighted, square = found[:2], found[2:]

    rows = -(-panels // 32) * 32
    half = rows // 2
    near = [references] + [along_y(references, NY - j) for j in range(1, NY)]
    column = stack(near, half, square[0])
    common = (weighted, square, groups)
    jobs, carry = [(0, column)], None
    up = [along_z(c, 1) for c in column]
    down = [along_z(c, -1) for c in column]
    for step in range(1, NZ // 2):
        jobs += [(NZ - step, up), (step, down)]
        if step < NZ // 2 - 1:
            up, down = [along_z(c, 1) for c in up], [along_z(c, -1) for c in down]
        else:
            far = [along_z(up[0], 1), along_z(down[1], -1)]
        carry, jobs = score(jobs, *common, carry, False, panels), []
    mass, peak, evidence = score([(NZ // 2, far)], *common, carry, True, panels)

    size = lax.axis_size("cls")
    evidence = log_sum([evidence, across(evidence, 1, size)])
    evidence = log_sum([evidence] + [across(evidence, mask, size) for mask in range(2, size, 2)])

    share = 24 * NZ * NY
    shard = target // share
    shard_y, shard_z = shard // NZ, shard % NZ
    block = (shard_z - z + NZ) % NZ * NY + (shard_y - y + NY) % NY
    place = jnp.where(target >= 0, (block * 8 + 2) * LANES + target % share, -1)
    post, weights, relay = posterior(mass, peak, evidence, place.reshape(1, slots), groups, count)
    relay = relay.reshape(NZ, NY, 8, LANES)

    fixed = (post, weighted, relay, weights)
    far = NZ // 2
    came = [[along_z(ring_step([far], n, *fixed, [])[0], 1 - 2 * n)] for n in range(2)]
    for step in range(far - 1, 0, -1):
        for n in range(2):
            places = [step, NZ - step][:: 1 - 2 * n]
            blocks = ring_step(places, n, *fixed, came[n])
            came[n] = [along_z(x, d) for x, d in zip(blocks, (1 - 2 * n, 2 * n - 1))]
    own = ring_last(*fixed, came)
    others = [along_y(own[j], j) for j in range(1, NY)]
    class_sums, found, class_weights = finish(panels, rows, own, others)
    return class_sums, class_weights, found[2:].reshape(-1)


def solution(mesh):
    placed = (P("ptcl", None), P("ptcl"), P("ptcl"), P(), P(), P("cls", "ptcl"))
    return jax.shard_map(
        shards,
        mesh=mesh,
        in_specs=placed,
        out_specs=(P("ptcl", "cls"), P(None, "cls"), P("ptcl")),
        check_vma=False,
    )
```

```python
import functools

import jax
import jax.numpy as jnp
from jax import lax
from jax.experimental import pallas as pl
from jax.experimental.pallas import tpu as pltpu
from jax.sharding import PartitionSpec as P

NY, NZ = 4, 8
LANES = 128
TILE = 16
F32, BF16, I16, I32 = jnp.float32, jnp.bfloat16, jnp.int16, jnp.int32
NT = (((1,), (1,)), ((), ()))
TN = (((0,), (0,)), ((), ()))
WEIGH_VMEM, SCORE_VMEM, POST_VMEM, RING_VMEM = 36, 12, 16, 8
WEIGHT = 100
LOW_EXPONENT = -100.0


def dot(a, b, dims=(((1,), (0,)), ((), ()))):
    return lax.dot_general(a, b, dims, preferred_element_type=F32)


def split3(x):
    hi = x.astype(BF16)
    rest = x - hi.astype(F32)
    mid = rest.astype(BF16)
    low = (rest - mid.astype(F32)).astype(BF16)
    return jnp.concatenate([hi.astype(F32), mid.astype(F32), low.astype(F32)], axis=0).astype(BF16)


def onehot3(groups, count):
    row = lax.broadcasted_iota(I32, (3 * count, groups.shape[1]), 0)
    row = jnp.where(row >= 2 * count, row - 2 * count, jnp.where(row >= count, row - count, row))
    return (row == groups).astype(F32).astype(BF16)


def params(size):
    return pltpu.CompilerParams(vmem_limit_bytes=size * 1024 * 1024)


def cost(flops, byte_count):
    return pl.CostEstimate(flops=int(flops), bytes_accessed=int(byte_count), transcendentals=0)


def weight_kernel(order, groups, images, table, noise, *outs):
    weighted, square = outs[:2], outs[2:]
    count, step = table.shape[0], images.shape[0]
    begin = pl.multiple_of(pl.program_id(0) * step, step)
    member = onehot3(groups[:, pl.ds(begin, step)], count)
    for i in range(NZ):
        place = [
            pl.ds(pl.multiple_of(order[i * NY + j] * LANES, LANES), LANES) for j in range(NY)
        ]
        values = jnp.concatenate([table[:, p] for p in place], axis=1)
        scale = jnp.concatenate([noise[:, p] for p in place], axis=1)
        far, near = i // (NZ // 2), i % (NZ // 2)

        @pl.when(pl.program_id(0) == 0)
        def _(values=values, scale=scale, far=far, near=near):
            square[far][near] = split3(values * values * scale)

        rows = dot(member, split3(values), TN)
        picture = jnp.concatenate([images[:, p] for p in place], axis=1)
        weighted[far][near] = (picture.astype(F32) * rows * scale).astype(BF16)


def weigh(order, groups, images, table, noise):
    slots, count = images.shape[0], table.shape[0]
    wide = NY * LANES
    step = slots // 2

    def whole(a):
        return pl.BlockSpec(a.shape, lambda i, o: (0, 0))

    return pl.pallas_call(
        weight_kernel,
        grid_spec=pltpu.PrefetchScalarGridSpec(
            num_scalar_prefetch=1,
            grid=(slots // step,),
            in_specs=[
                whole(groups),
                pl.BlockSpec((step, images.shape[1]), lambda i, o: (i, 0)),
                whole(table),
                whole(noise),
            ],
            out_specs=[pl.BlockSpec((NZ // 2, step, wide), lambda i, o: (0, i, 0))] * 2
            + [pl.BlockSpec((NZ // 2, 3 * count, wide), lambda i, o: (0, 0, 0))] * 2,
        ),
        out_shape=[jax.ShapeDtypeStruct((NZ // 2, slots, wide), BF16)] * 2
        + [jax.ShapeDtypeStruct((NZ // 2, 3 * count, wide), BF16)] * 2,
        compiler_params=params(WEIGH_VMEM),
        cost_estimate=cost(6e9 * WEIGHT, 4 * images.size),
        name="weigh",
    )(order, groups, images, table, noise)


def stack_kernel(*refs):
    blocks, (top, bottom) = refs[:NY], refs[-2:]
    half = top.shape[1]
    rest = blocks[0].shape[0] - half
    for j, block in enumerate(blocks):
        top[j] = block[:half, :]
        bottom[j, half - TILE :, :] = jnp.zeros((TILE, LANES), BF16)
        bottom[j, :rest, :] = block[half:, :]


def stack(blocks, half, after):
    return pl.pallas_call(
        stack_kernel,
        in_specs=in_vmem(NY) + [pl.BlockSpec(memory_space=pl.ANY)],
        out_specs=in_vmem(2),
        out_shape=[jax.ShapeDtypeStruct((NY, half, LANES), BF16)] * 2,
        compiler_params=params(RING_VMEM),
        name="stack",
    )(*blocks, after)


def in_vmem(count):
    return [pl.BlockSpec(memory_space=pltpu.VMEM)] * count


def score_kernel(jobs, first, last, panels, *refs):
    refs = list(refs)
    chunks = [[refs.pop(0) for _ in range(n)] for _, n in jobs]
    wa, wb, sa, sb, groups = [refs.pop(0) for _ in range(5)]
    total_in, energy_in = (None, None) if first else [refs.pop(0) for _ in range(2)]
    panel, right, square = [], [], []
    for (place, _), chunk in zip(jobs, chunks):
        parts = [jnp.concatenate([c[j] for j in range(NY)], axis=1) for c in chunk]
        panel.append(jnp.concatenate(parts, axis=0))
        far, near = place // (NZ // 2), place % (NZ // 2)
        right.append(((wa, wb)[far], near))
        square.append((sa, sb)[far][near])
    panel = jnp.concatenate(panel, axis=1)
    square = jnp.concatenate(square, axis=1)
    wide = panel.astype(F32)
    wide = wide * wide
    hi = wide.astype(BF16)
    low = (wide - hi.astype(F32)).astype(BF16)
    energy = dot(hi, square, NT) + dot(low, square, NT)
    if not first:
        energy += energy_in[...]
    if last:
        mass, peak, evidence = refs
        hi = energy.astype(BF16)
        rest = energy - hi.astype(F32)
        mid = rest.astype(BF16)
        low = (rest - mid.astype(F32)).astype(BF16)
    else:
        total, refs[1][...] = refs[0], energy
    slots = groups.shape[1]
    step = 256
    for begin in range(0, slots, step):
        here = slice(begin, begin + step)
        value = dot(panel, jnp.concatenate([w[k, here, :] for w, k in right], axis=1), NT)
        if not first:
            value += total_in[:, here]
        if not last:
            total[:, here] = value
            continue
        member = onehot3(groups[:, here], energy.shape[1] // 3)
        value -= 0.5 * (dot(hi, member) + dot(mid, member) + dot(low, member))
        row = lax.broadcasted_iota(I32, value.shape, 0)
        value = jnp.where(row < panels, value, -jnp.inf)
        top = jnp.max(value, axis=0, keepdims=True)
        value = jnp.exp(value - top)
        mass[:, here] = value
        peak[:, here] = top
        evidence[:, here] = top + jnp.log(jnp.sum(value, axis=0, keepdims=True))


def score(jobs, weighted, square, groups, carry, last, panels):
    rows = sum(a.shape[1] for a in jobs[0][1])
    slots = groups.shape[1]
    count3 = square[0].shape[1]
    if all(place < NZ // 2 for place, _ in jobs):
        weighted, square = weighted[:1] * 2, square[:1] * 2
    outs = [jax.ShapeDtypeStruct((rows, slots), F32)]
    if last:
        outs += [jax.ShapeDtypeStruct((1, slots), F32)] * 2
    else:
        outs += [jax.ShapeDtypeStruct((rows, count3), F32)]
    args = [a for job in jobs for a in job[1]] + [*weighted, *square, groups]
    args += [] if carry is None else list(carry)
    work = 2.5 * rows * slots * NY * LANES * len(jobs)
    return pl.pallas_call(
        functools.partial(
            score_kernel, [(j[0], len(j[1])) for j in jobs], carry is None, last, panels
        ),
        in_specs=in_vmem(len(args)),
        out_specs=in_vmem(len(outs)),
        out_shape=outs,
        compiler_params=params(SCORE_VMEM),
        cost_estimate=cost(work * WEIGHT, 4e6 * len(jobs)),
        name="score",
    )(*args)


def posterior_kernel(mass, peak, evidence, place, groups, post, weights, relay):
    live = place[...] >= 0
    scale = jnp.where(live, jnp.exp(peak[...] - evidence[...]), 0.0)
    value = (mass[...] * scale).astype(BF16)
    post[...] = value
    count = weights.shape[1]
    slots = groups.shape[1]
    member = (lax.broadcasted_iota(I32, (count, slots), 0) == groups[...]).astype(F32).astype(BF16)
    filled = [value, jnp.zeros((NY * LANES - value.shape[0], slots), BF16)]
    filled = jnp.concatenate(filled, axis=0)
    for j in range(NY):
        weights[j] = dot(member, filled[j * LANES : (j + 1) * LANES], NT)
    spot = place[...]
    line = lax.shift_right_arithmetic(spot, 7)
    high = (lax.broadcasted_iota(I32, (relay.shape[0], slots), 0) == line).astype(F32).astype(BF16)
    lane = lax.broadcasted_iota(I32, (LANES, slots), 0) == (spot & 127)
    found = split3(jnp.where(live, evidence[...], 0.0))
    out = jnp.zeros(relay.shape, F32)
    for k in (2, 1, 0):
        out += dot(high, jnp.where(lane, found[k : k + 1].astype(F32), 0.0).astype(BF16), NT)
    relay[...] = out


def posterior(mass, peak, evidence, place, groups, count):
    rows, slots = mass.shape
    return pl.pallas_call(
        posterior_kernel,
        out_shape=[
            jax.ShapeDtypeStruct((rows, slots), BF16),
            jax.ShapeDtypeStruct((NY, count, LANES), F32),
            jax.ShapeDtypeStruct((NZ * NY * 8, LANES), F32),
        ],
        compiler_params=params(POST_VMEM),
        cost_estimate=cost(1e9, 5e6),
        name="posterior",
    )(mass, peak, evidence, place, groups)


def exponent(x):
    top = jnp.max(jnp.abs(x), axis=0, keepdims=True)
    return jnp.maximum(jnp.ceil(jnp.log2(jnp.maximum(top, 2.0**LOW_EXPONENT))), LOW_EXPONENT)


def to_int(x):
    return jnp.round(x).astype(I32)


def put(out, j, sums, relay, weights):
    rows = sums.shape[0]
    e = exponent(sums)
    main = to_int(sums * jnp.exp2(14.0 - e))
    if relay is None:
        last = lax.broadcasted_iota(I32, sums.shape, 0) == rows - 1
        out[j] = jnp.where(last, e.astype(I32), main).astype(I16)
        return
    out[j, :rows, :] = main.astype(I16)
    row = lax.broadcasted_iota(I32, (8, LANES), 0)
    f, g = exponent(relay), exponent(weights)
    up, down = jnp.exp2(14.0 - f), jnp.exp2(f - 14.0)
    part = jnp.round(relay * up)
    rest = to_int((relay - part * down) * up * 2.0**14)
    high = jnp.where(row < 2, jnp.where(row == 0, e, f), part).astype(I32)
    low = jnp.where(row < 2, jnp.where(row == 0, g, 0.0).astype(I32), rest)
    out[j, rows + TILE :, :] = to_int(weights * jnp.exp2(14.0 - g)).astype(I16)
    out[j, rows : rows + TILE, :] = jnp.concatenate([high, low], axis=0).astype(I16)


def number(x):
    return x.astype(I32).astype(F32)


def decode(block, rows):
    if block.shape[0] == rows:
        last = lax.broadcasted_iota(I32, block.shape, 0) == rows - 1
        e = number(block[rows - TILE :, :])[TILE - 1 : TILE]
        return jnp.where(last, 0.0, number(block) * jnp.exp2(e - 14.0)), None, None
    tail = number(block[rows : rows + TILE, :])
    high, low = tail[:8], tail[8:]
    sums = number(block[:rows, :]) * jnp.exp2(high[0:1] - 14.0)
    down = jnp.exp2(high[1:2] - 14.0)
    row = lax.broadcasted_iota(I32, high.shape, 0)
    relay = jnp.where(row < 2, 0.0, (high + low * 2.0**-14) * down)
    return sums, relay, number(block[rows + TILE :, :]) * jnp.exp2(low[0:1] - 14.0)


def plus(a, b):
    return [None if x is None else x + w for x, w in zip(a, b)]


def products(post, weighted, place):
    for begin in range(0, NY, 2):
        right = weighted[place % (NZ // 2), :, begin * LANES : (begin + 2) * LANES]
        product = dot(post, right)
        yield begin, product[:, :LANES]
        yield begin + 1, product[:, LANES:]


def ring_kernel(stream, places, post, *refs):
    refs = list(refs)
    ways = len(places)
    weighted = [refs.pop(0) for _ in range(ways)]
    relay, weights = [refs.pop(0) for _ in range(2)] if stream == 0 else (None, None)
    outs = [refs.pop() for _ in range(ways)][::-1]
    came = refs + [None] * (ways - len(refs))
    rows = post.shape[0] // 2
    left = post[stream * rows : (stream + 1) * rows, :]
    for way, place in enumerate(places):
        for j, sums in products(left, weighted[way], place):
            mine = [sums, None, None]
            if stream == 0:
                mine = [sums, relay[place, j], weights[j]]
            if came[way] is not None:
                mine = plus(mine, decode(came[way][j], rows))
            put(outs[way], j, *mine)


def ring_step(places, stream, post, weighted, relay, weights, came):
    rows, slots = post.shape[0] // 2, post.shape[1]
    tall = rows if stream else rows + TILE + weights.shape[1]
    args = [post] + [weighted[p // (NZ // 2)] for p in places]
    args += [] if stream else [relay, weights]
    args += came
    return pl.pallas_call(
        functools.partial(ring_kernel, stream, places),
        in_specs=in_vmem(len(args)),
        out_specs=in_vmem(len(places)),
        out_shape=[jax.ShapeDtypeStruct((NY, tall, LANES), I16)] * len(places),
        compiler_params=params(RING_VMEM),
        cost_estimate=cost(2 * rows * slots * NY * LANES * len(places), 4e6),
        name="ring",
    )(*args)


def last_kernel(post, weighted, relay, weights, *refs):
    came, out = [refs[:2], refs[2:4]], refs[4]
    rows = post.shape[0] // 2
    got = [[[decode(c[j], rows) for c in pair] for j in range(NY)] for pair in came]
    mass = [weights[j] + got[0][j][0][2] + got[0][j][1][2] for j in range(NY)]
    mass = jnp.concatenate(mass, axis=0)
    for j, sums in products(post[...], weighted, 0):
        both = [
            sums[n * rows : (n + 1) * rows] + got[n][j][0][0] + got[n][j][1][0] for n in range(2)
        ]
        extra = relay[0, j] + got[0][j][0][1] + got[0][j][1][1]
        put(out, j, jnp.concatenate(both, axis=0), extra, mass)


def ring_last(post, weighted, relay, weights, came):
    rows, slots = post.shape
    tall = rows + TILE + NY * weights.shape[1]
    args = [post, weighted[0], relay, weights, *came[0], *came[1]]
    return pl.pallas_call(
        last_kernel,
        in_specs=in_vmem(len(args)),
        out_specs=pl.BlockSpec(memory_space=pltpu.VMEM),
        out_shape=jax.ShapeDtypeStruct((NY, tall, LANES), I16),
        compiler_params=params(RING_VMEM),
        cost_estimate=cost(2 * rows * slots * NY * LANES, 4e6),
        name="last",
    )(*args)


def finish_kernel(panels, rows, own, a, b, c, sums, evidence, weights):
    total = decode(own[0], rows)
    for other in (a, b, c):
        total = plus(total, decode(other[...], rows))
    sums[...] = total[0].T[:, :panels]
    evidence[...] = total[1]
    count = weights.shape[0]
    for j in range(NY):
        begin, end = j * LANES, min((j + 1) * LANES, panels)
        weights[:, begin:end] = total[2][j * count : (j + 1) * count, : end - begin]


def finish(panels, rows, own, others):
    tall = own.shape[1]
    whole = pl.BlockSpec((tall, LANES), lambda i: (0, 0))
    shapes = [(LANES, panels), (8, LANES), ((tall - rows - TILE) // NY, panels)]
    return pl.pallas_call(
        functools.partial(finish_kernel, panels, rows),
        grid=(1,),
        in_specs=[pl.BlockSpec((1, tall, LANES), lambda i: (0, 0, 0))] + [whole] * 3,
        out_specs=[pl.BlockSpec(s, lambda i: (0, 0)) for s in shapes],
        out_shape=[jax.ShapeDtypeStruct(s, F32) for s in shapes],
        compiler_params=params(RING_VMEM),
        name="finish",
    )(own, *others)


def along_z(x, shift):
    pairs = [(y * NZ + z, y * NZ + (z + shift) % NZ) for y in range(NY) for z in range(NZ)]
    return lax.ppermute(x, "ptcl", pairs)


def along_y(x, shift):
    pairs = [(y * NZ + z, (y + shift) % NY * NZ + z) for y in range(NY) for z in range(NZ)]
    return lax.ppermute(x, "ptcl", pairs)


def across(x, mask, size):
    return lax.ppermute(x, "cls", [(i, i ^ mask) for i in range(size)])


def shards(images, target, ctf_group, ctf_table, noise_weight, references):
    panels = references.shape[0]
    count = ctf_table.shape[0]
    me = lax.axis_index("ptcl")
    y, z = me // NZ, me % NZ
    slots = images.shape[0]
    groups = ctf_group.reshape(1, slots)
    noise = noise_weight.reshape(1, -1)
    rel = jnp.arange(NZ * NY, dtype=I32)
    order = (y + rel % NY) % NY * NZ + (z + rel // NY) % NZ
    found = weigh(order, groups, images, ctf_table, noise)
    weighted, square = found[:2], found[2:]

    rows = -(-panels // 32) * 32
    half = rows // 2
    near = [references] + [along_y(references, NY - j) for j in range(1, NY)]
    column = stack(near, half, square[0])
    common = (weighted, square, groups)
    carry = score([(0, column)], *common, None, False, panels)
    up = [along_z(c, 1) for c in column]
    down = [along_z(c, -1) for c in column]
    for step in range(1, NZ // 2):
        jobs = [(NZ - step, up), (step, down)]
        if step < NZ // 2 - 1:
            up, down = [along_z(c, 1) for c in up], [along_z(c, -1) for c in down]
        else:
            far = [along_z(up[0], 1), along_z(down[1], -1)]
        carry = score(jobs, *common, carry, False, panels)
    mass, peak, evidence = score([(NZ // 2, far)], *common, carry, True, panels)

    size = lax.axis_size("cls")
    mask = 1
    while mask < size:
        other = across(evidence, mask, size)
        top = jnp.maximum(evidence, other)
        evidence = top + jnp.log(jnp.exp(evidence - top) + jnp.exp(other - top))
        mask *= 2

    share = 24 * NZ * NY
    shard = target // share
    shard_y, shard_z = shard // NZ, shard % NZ
    block = (shard_z - z + NZ) % NZ * NY + (shard_y - y + NY) % NY
    place = jnp.where(target >= 0, (block * 8 + 2) * LANES + target % share, -1)
    post, weights, relay = posterior(mass, peak, evidence, place.reshape(1, slots), groups, count)
    relay = relay.reshape(NZ, NY, 8, LANES)

    fixed = (post, weighted, relay, weights)
    far = NZ // 2
    came = [[along_z(ring_step([far], n, *fixed, [])[0], 1 - 2 * n)] for n in range(2)]
    for step in range(far - 1, 0, -1):
        for n in range(2):
            places = [step, NZ - step][:: 1 - 2 * n]
            blocks = ring_step(places, n, *fixed, came[n])
            came[n] = [along_z(x, d) for x, d in zip(blocks, (1 - 2 * n, 2 * n - 1))]
    own = ring_last(*fixed, came)
    others = [along_y(own[j], j) for j in range(1, NY)]
    class_sums, found, class_weights = finish(panels, rows, own, others)
    return class_sums, class_weights, found[2:].reshape(-1)


def solution(mesh):
    placed = (P("ptcl", None), P("ptcl"), P("ptcl"), P(), P(), P("cls", "ptcl"))
    return jax.shard_map(
        shards,
        mesh=mesh,
        in_specs=placed,
        out_specs=(P("ptcl", "cls"), P(None, "cls"), P("ptcl")),
        check_vma=False,
    )
```
